32 devices in a mesh: ent: 16 (over z, y, x), rep: 2 (over core).
Axes of the slice: x: 2, y: 2, z: 4, core: 2. Of those that a mesh axis runs over, the one named last changes fastest.
Arguments:
- pieces: bfloat16 [4096, 8, 512], P(('ent', 'rep')), may hold values from -6 to 6
- lengths: int32 [4096], P(('ent', 'rep')), may hold values from 1 to 7
- scripts: int32 [4096], P(('ent', 'rep')), may hold values from 0 to 15
- script_table: float32 [16, 512], replicated, may hold values from -3 to 3
- gain_attn: float32 [512], replicated, may hold values from 0.5 to 1.5
- gain_ffn: float32 [512], replicated, may hold values from 0.5 to 1.5
- w_qkv: bfloat16 [512, 1536], replicated, may hold values from -0.25 to 0.25
- w_out: bfloat16 [512, 512], replicated, may hold values from -0.5 to 0.5
- w_up: bfloat16 [512, 2048], replicated, may hold values from -0.25 to 0.25
- w_down: bfloat16 [2048, 512], replicated, may hold values from -0.125 to 0.125
- w_proj: bfloat16 [512, 4096], P(None, 'ent'), may hold values from -0.25 to 0.25
- token_ids: int32 [8, 2048], P('rep'), may hold values from 0 to 4095
- out_grad: bfloat16 [4096, 8, 2048], P('ent', 'rep'), may hold values from -6 to 6
Outputs:
- looked_up: bfloat16 [4096, 8, 2048], P('ent', 'rep')
- grad_pieces: float32 [4096, 8, 512], P(('ent', 'rep'))
- grad_script_table: float32 [16, 512], replicated
- grad_gain_attn: float32 [512], replicated
- grad_gain_ffn: float32 [512], replicated
- grad_w_qkv: float32 [512, 1536], replicated
- grad_w_out: float32 [512, 512], replicated
- grad_w_up: float32 [512, 2048], replicated
- grad_w_down: float32 [2048, 512], replicated
- grad_w_proj: float32 [512, 4096], P(None, 'ent')
The draws below stay inside these ranges and needn't reach their ends.
All inputs are finite; a program needn't handle non-finite values.
Results may differ from the reference program's by a relative error of at most 0.0074.
Values may be sent and summed in bfloat16 or wider, within the bound.
No kernel may reach another device: no remote copies, remote signals or barrier semaphores. Data moves between devices by JAX's collectives and lax.ppermute only.
A program may use at most 128 MiB of HBM per device.

```python
import math
import jax
import jax.numpy as jnp
import numpy as np
from jax import lax

D = 512
HEADS = 8
HEAD_DIM = 64
FF = 2048
EMB = 4096
SLOTS = 8
SCRIPTS = 16
TEXT_LEN = 2048
VOCAB = 4096
ROWS = 8


def place_ends(values, own_key, least, high):
    extent = values.shape
    place = [jax.random.randint(jax.random.fold_in(own_key, axis), (), 0, extent[axis]) for axis in range(len(extent))]
    values = values.at[tuple(place)].set(least)
    longest = extent.index(max(extent))
    place[longest] = (place[longest] + 1) % extent[longest]
    return values.at[tuple(place)].set(high)


def block_levels(rng, shape, split, low, high):
    factor_of = 1.0
    for dim, blocks in split:
        steps = jax.random.uniform(jax.random.fold_in(jax.random.fold_in(rng, 6), dim), (blocks,), jnp.float32, low / len(split), high / len(split))
        factor_of = factor_of * jnp.repeat(jnp.exp(steps), shape[dim] // blocks).reshape((-1,) + (1,) * (len(shape) - 1 - dim))
    return factor_of


def rank_bounds(count, skew):
    loads = [(1 << 20) // math.isqrt(standing ** skew) + 1 for standing in range(1, count + 1)]
    deviation = 1 + sum(loads) // (1 << 30)
    return np.cumsum(np.array([max(1, weight // deviation) for weight in loads]))


def ranked_ids(stream_key, extent, amount, slope):
    grid = rank_bounds(amount, slope)
    lot = jax.random.randint(jax.random.fold_in(stream_key, 1), extent, 0, int(grid[amount - 1]))
    rank = jnp.searchsorted(jnp.asarray(grid, jnp.int32), lot, side="right")
    return jax.random.permutation(jax.random.fold_in(stream_key, 2), amount)[rank].astype(jnp.int32)


def noise(stream_key, extent, scale, most, cuts=(), held_as=jnp.bfloat16):
    drawn = scale * jax.random.normal(stream_key, extent, jnp.float32)
    if cuts:
        drawn = drawn * block_levels(stream_key, extent, cuts, -0.22, 0.18)
    return jnp.clip(drawn, -most, most).astype(held_as)


def setup_inputs(seed: int = 0) -> dict:
    key_list = jax.random.split(jax.random.key(seed), 14)
    return {
        "pieces": noise(key_list[0], (VOCAB, SLOTS, D), 1.0, 6.0, ((0, 32),)),
        "lengths": place_ends(jax.random.randint(key_list[1], (VOCAB,), 1, 8), jax.random.fold_in(key_list[1], 1), 1, 7).astype(jnp.int32),
        "scripts": place_ends(ranked_ids(key_list[2], (VOCAB,), SCRIPTS, 2), jax.random.fold_in(key_list[2], 3), 0, SCRIPTS - 1).astype(jnp.int32),
        "script_table": noise(key_list[3], (SCRIPTS, D), 0.5, 3.0, (), jnp.float32),
        "gain_attn": jnp.clip(1.0 + 0.1 * jax.random.normal(key_list[4], (D,), jnp.float32), 0.5, 1.5),
        "gain_ffn": jnp.clip(1.0 + 0.1 * jax.random.normal(key_list[5], (D,), jnp.float32), 0.5, 1.5),
        "w_qkv": noise(key_list[6], (D, 3 * D), D ** -0.5, 0.25),
        "w_out": noise(key_list[7], (D, D), (D // 4) ** -0.5, 0.5),
        "w_up": noise(key_list[8], (D, FF), D ** -0.5, 0.25),
        "w_down": noise(key_list[9], (FF, D), FF ** -0.5, 0.125),
        "w_proj": noise(key_list[10], (D, EMB), D ** -0.5, 0.25, ((1, 16),)),
        "token_ids": place_ends(ranked_ids(key_list[11], (ROWS, TEXT_LEN), VOCAB, 2), jax.random.fold_in(key_list[11], 3), 0, VOCAB - 1).astype(jnp.int32),
        "out_grad": noise(key_list[12], (EMB, ROWS, TEXT_LEN), 1.0, 6.0, ((0, 16), (1, 2))),
    }


@jax.custom_vjp
def low(v):
    return lax.optimization_barrier(v.astype(jnp.bfloat16)).astype(jnp.float32)

@jax.custom_vjp
def low_back(v):
    return v

def low_keep(v):
    return (low(v), None)

def low_pass(kept, grad):
    return (grad,)

def back_keep(v):
    return (v, None)

def back_low(kept, grad):
    return (low(grad),)
low.defvjp(low_keep, low_pass)
low_back.defvjp(back_keep, back_low)
highest = lax.Precision.HIGHEST
block_entries = 512

def normalize(values, gain):
    centered = values - lax.optimization_barrier(jnp.mean(values, axis=-1, keepdims=True))
    spread = lax.optimization_barrier(jnp.mean(centered * centered, axis=-1, keepdims=True))
    return centered * lax.rsqrt(spread + 1e-05) * gain

def entry_block(params, pieces_blk, lengths_blk, scripts_blk):
    script_table, gain_attn, gain_ffn, w_qkv, w_out, w_up, w_down, w_proj = params
    entries, slots, width = pieces_blk.shape
    start = pieces_blk + script_table[scripts_blk][:, None, :]
    normed = low(normalize(start, gain_attn)).reshape(entries * slots, width)
    mixed = low(low_back(jnp.dot(normed, w_qkv, precision=highest)))
    mixed = mixed.reshape(entries, slots, 3, HEADS, HEAD_DIM)
    queries = mixed[:, :, 0]
    key_heads = mixed[:, :, 1]
    value_heads = mixed[:, :, 2]
    raw = low_back(jnp.einsum('eshd,ethd->ehst', queries, key_heads, precision=highest))
    valid = jnp.arange(slots)[None, :] <= lengths_blk[:, None]
    scores = jnp.where(valid[:, None, None, :], raw * HEAD_DIM ** (-0.5), -1000000000.0)
    attn_probs = low(jax.nn.softmax(scores, axis=-1))
    context = low(low_back(jnp.einsum('ehst,ethd->eshd', attn_probs, value_heads, precision=highest)))
    branch = low_back(jnp.dot(context.reshape(entries * slots, width), w_out, precision=highest))
    middle = start + branch.reshape(entries, slots, width)
    normed_ffn = low(normalize(middle, gain_ffn)).reshape(entries * slots, width)
    up_proj = low_back(jnp.dot(normed_ffn, w_up, precision=highest))
    hidden = low(jax.nn.gelu(up_proj, approximate=True))
    branch_ffn = low_back(jnp.dot(hidden, w_down, precision=highest))
    final = middle + branch_ffn.reshape(entries, slots, width)
    pool_weights = valid.astype(jnp.float32) / (lengths_blk + 1).astype(jnp.float32)[:, None]
    pooled = low(lax.optimization_barrier(jnp.sum(final * pool_weights[:, :, None], axis=1)))
    return low(low_back(jnp.dot(pooled, w_proj, precision=highest)))

def reference(pieces, lengths, scripts, script_table, gain_attn, gain_ffn, w_qkv, w_out, w_up, w_down, w_proj, token_ids, out_grad):
    params = (script_table.astype(jnp.float32), gain_attn.astype(jnp.float32), gain_ffn.astype(jnp.float32), w_qkv.astype(jnp.float32), w_out.astype(jnp.float32), w_up.astype(jnp.float32), w_down.astype(jnp.float32), w_proj.astype(jnp.float32))
    pieces_wide = pieces.astype(jnp.float32)
    blocks = VOCAB // block_entries

    def whole(params, pieces_wide):

        def one_block(items):
            return jax.checkpoint(entry_block)(params, items[0], items[1], items[2])
        tables = lax.map(one_block, (pieces_wide.reshape(blocks, block_entries, SLOTS, D), lengths.reshape(blocks, block_entries), scripts.reshape(blocks, block_entries)))
        table = tables.reshape(VOCAB, EMB)
        return jnp.take(table.T, token_ids, axis=1)
    looked, pull = jax.vjp(whole, params, pieces_wide)
    grad_params, grad_pieces = pull(out_grad.astype(jnp.float32))
    return (looked.astype(jnp.bfloat16), grad_pieces, grad_params[0], grad_params[1], grad_params[2], grad_params[3], grad_params[4], grad_params[5], grad_params[6], grad_params[7])
```

```python
import functools
import math

import jax
import jax.numpy as jnp
from jax import lax
from jax.experimental import pallas as pl
from jax.experimental.pallas import tpu as pltpu
from jax.sharding import PartitionSpec as P

HEADS = 8
HEAD_DIM = 64
F32 = jnp.float32
BF16 = jnp.bfloat16
highest = lax.Precision.HIGHEST
PARAMS = pltpu.CompilerParams(vmem_limit_bytes=56 * 1024 * 1024)


def make_levels(ent_count, rep_count):
    levels = [("rep", rep_count, 0)]
    bit, total = 0, ent_count.bit_length() - 1
    while bit < total:
        width = 1 if bit < 2 else min(2, total - bit)
        levels.append(("ent", 1 << width, bit))
        bit += width
    return levels


def slot_of(number, levels):
    rep_count = levels[0][1]
    slot = number % rep_count
    ent = number // rep_count
    for _, size, shift in levels[1:]:
        slot = slot * size + (ent >> shift) % size
    return slot


def swap(value, level, k):
    name, size, shift = level
    count = lax.axis_size(name)
    return lax.ppermute(value, name, [(i, i ^ (k << shift)) for i in range(count)])


def reduce_scatter(value, levels, order):
    left = list(range(len(levels)))
    for position, level in enumerate(order):
        axis = left.index(level)
        left.remove(level)
        parts = [lax.index_in_dim(value, k, axis, keepdims=False) for k in range(levels[level][1])]
        total = parts[0].astype(F32)
        for k in range(1, len(parts)):
            total = total + swap(parts[k], levels[level], k).astype(F32)
        value = total if position == len(order) - 1 else total.astype(value.dtype)
    return value


def gather_slots(value, levels, order):
    held = []
    for level in order:
        parts = [value] + [swap(value, levels[level], k) for k in range(1, levels[level][1])]
        held = sorted(held + [level])
        value = jnp.stack(parts, axis=held.index(level))
    return value


def orders(levels):
    rest = list(range(3, len(levels)))
    return [0, 1, 2] + rest, [0, 2, 1] + rest


def selector(ids, base, rows):
    entry = lax.broadcasted_iota(jnp.int32, (rows, 1), 0).astype(jnp.int16)
    return jnp.where(entry == (ids - base).astype(jnp.int16), jnp.ones((), BF16), jnp.zeros((), BF16))


def nt(left, right):
    return lax.dot_general(left, right, (((1,), (1,)), ((), ())), preferred_element_type=F32)


def tn(left, right):
    return lax.dot_general(left, right, (((0,), (0,)), ((), ())), preferred_element_type=F32)


def mm(left, right):
    return jnp.dot(left, right, preferred_element_type=F32)


def scatter_body(ids_ref, grad_ref, proj_ref, table_ref, half_a_ref, half_b_ref):
    rows = table_ref.shape[0]
    pick = selector(ids_ref[...], pl.program_id(0) * rows, rows)
    part = nt(pick, grad_ref[...]).astype(BF16)
    table_ref[...] = part
    pooled_part = nt(part, proj_ref[...]).astype(BF16)
    half = pooled_part.shape[1] // 2
    half_a_ref[...] = pooled_part[:, :half]
    half_b_ref[...] = pooled_part[:, half:]


def scatter_rows(ids, grad, w_proj, vocab):
    features, tokens = grad.shape
    width = w_proj.shape[0]
    rows = min(512, vocab)
    return pl.pallas_call(
        scatter_body,
        grid=(vocab // rows,),
        in_specs=[
            pl.BlockSpec((1, tokens), lambda i: (0, 0)),
            pl.BlockSpec((features, tokens), lambda i: (0, 0)),
            pl.BlockSpec((width, features), lambda i: (0, 0)),
        ],
        out_specs=[
            pl.BlockSpec((rows, features), lambda i: (i, 0)),
            pl.BlockSpec((rows, width // 2), lambda i: (i, 0)),
            pl.BlockSpec((rows, width // 2), lambda i: (i, 0)),
        ],
        out_shape=[
            jax.ShapeDtypeStruct((vocab, features), BF16),
            jax.ShapeDtypeStruct((vocab, width // 2), BF16),
            jax.ShapeDtypeStruct((vocab, width // 2), BF16),
        ],
        compiler_params=PARAMS,
        name="scatter_rows",
    )(ids, grad, w_proj)


def table_body(half_a_ref, half_b_ref, proj_ref, part_ref, table_ref, grad_ref):
    half = half_a_ref.shape[1]
    proj = proj_ref[...]
    pooled_a, pooled_b = half_a_ref[...], half_b_ref[...]
    cols = lax.dot_general(proj[:half], pooled_a, (((0,), (1,)), ((), ())), preferred_element_type=F32)
    cols += lax.dot_general(proj[half:], pooled_b, (((0,), (1,)), ((), ())), preferred_element_type=F32)
    table_ref[...] = cols.astype(BF16)

    @pl.when(pl.program_id(0) == 0)
    def _():
        grad_ref[...] = jnp.zeros_like(grad_ref)

    part = part_ref[...]
    grad_ref[:half] += tn(pooled_a, part)
    grad_ref[half:] += tn(pooled_b, part)


def table_and_grad(half_a, half_b, w_proj, part):
    vocab, half = half_a.shape
    width, features = w_proj.shape
    rows = min(1024, vocab)
    return pl.pallas_call(
        table_body,
        grid=(vocab // rows,),
        in_specs=[
            pl.BlockSpec((rows, half), lambda i: (i, 0)),
            pl.BlockSpec((rows, half), lambda i: (i, 0)),
            pl.BlockSpec((width, features), lambda i: (0, 0)),
            pl.BlockSpec((rows, features), lambda i: (i, 0)),
        ],
        out_specs=[
            pl.BlockSpec((features, rows), lambda i: (0, i)),
            pl.BlockSpec((width, features), lambda i: (0, 0)),
        ],
        out_shape=[
            jax.ShapeDtypeStruct((features, vocab), BF16),
            jax.ShapeDtypeStruct((width, features), F32),
        ],
        compiler_params=PARAMS,
        name="table_and_grad",
    )(half_a, half_b, w_proj, part)


def lookup_body(chunk, ids_ref, *refs):
    table_refs, out_ref = refs[:-1], refs[-1]
    ids = ids_ref[...]
    total = None
    for index, table_ref in enumerate(table_refs):
        vocab = table_ref.shape[1]

        def step(base, inner, table_ref=table_ref):
            inner = pl.multiple_of(inner, chunk)
            return mm(table_ref[:, pl.ds(inner, chunk)], selector(ids, base + inner, chunk))

        base = index * vocab
        if vocab == chunk:
            part = step(base, 0)
        else:
            zero = jnp.zeros(out_ref.shape, F32)
            part = lax.fori_loop(0, vocab // chunk, lambda i, t: t + step(base, i * chunk), zero)
        total = part if total is None else total + part
    out_ref[...] = total.astype(BF16)


def lookup(ids, tables):
    tokens = ids.shape[1]
    features, vocab = tables[0].shape
    block = math.gcd(tokens, 1024)
    return pl.pallas_call(
        functools.partial(lookup_body, min(vocab, 4096)),
        grid=(tokens // block,),
        in_specs=[pl.BlockSpec((1, block), lambda i: (0, i))]
        + [pl.BlockSpec((features, vocab), lambda i: (0, 0))] * len(tables),
        out_specs=pl.BlockSpec((features, block), lambda i: (0, i)),
        out_shape=jax.ShapeDtypeStruct((features, tokens), BF16),
        compiler_params=PARAMS,
        name="lookup",
    )(ids, *tables)


def weight_body(slots_ref, left_ref, right_ref, out_ref):
    rows = out_ref.shape[1]
    part = tn(left_ref[...], right_ref[...]).astype(BF16)
    each = part.shape[0] // rows
    for j in range(each):
        out_ref[slots_ref[pl.program_id(0) * each + j]] = part[j * rows : (j + 1) * rows]


def weight_slots(slots, left, right):
    count = slots.shape[0]
    depth, height = left.shape
    width = right.shape[1]
    tile = max(256, height // count)
    return pl.pallas_call(
        weight_body,
        grid_spec=pltpu.PrefetchScalarGridSpec(
            num_scalar_prefetch=1,
            grid=(height // tile,),
            in_specs=[
                pl.BlockSpec((depth, tile), lambda i, s: (0, i)),
                pl.BlockSpec((depth, width), lambda i, s: (0, 0)),
            ],
            out_specs=pl.BlockSpec((count, height // count, width), lambda i, s: (0, 0, 0)),
        ),
        out_shape=jax.ShapeDtypeStruct((count, height // count, width), BF16),
        compiler_params=PARAMS,
        name="weight_slots",
    )(slots, left, right)


def unpack_body(slots_ref, in_ref, out_ref):
    rows = in_ref.shape[1]
    each = out_ref.shape[0] // rows
    for j in range(each):
        out_ref[j * rows : (j + 1) * rows] = in_ref[slots_ref[pl.program_id(0) * each + j]].astype(F32)


def unpack(slots, value):
    count, rows, width = value.shape
    each = max(1, count // 4)
    return pl.pallas_call(
        unpack_body,
        grid_spec=pltpu.PrefetchScalarGridSpec(
            num_scalar_prefetch=1,
            grid=(count // each,),
            in_specs=[pl.BlockSpec((count, rows, width), lambda i, s: (0, 0, 0))],
            out_specs=pl.BlockSpec((each * rows, width), lambda i, s: (i, 0)),
        ),
        out_shape=jax.ShapeDtypeStruct((count * rows, width), F32),
        compiler_params=PARAMS,
        name="unpack",
    )(slots, value)


GROUP = 128
PAIR = 2 * HEAD_DIM
GELU_SCALE = 0.7978845608028654
GELU_CUBE = 0.044715


def center(values):
    centered = values - jnp.mean(values, axis=-1, keepdims=True)
    spread = jnp.mean(centered * centered, axis=-1, keepdims=True)
    rate = lax.rsqrt(spread + 1e-05)
    return centered * rate, rate


def center_back(grad, gain, unit, rate):
    gain_grad = jnp.sum(grad * unit, axis=0, keepdims=True)
    grad = grad * gain
    mean_grad = jnp.mean(grad, axis=-1, keepdims=True)
    mean_unit = jnp.mean(grad * unit, axis=-1, keepdims=True)
    return rate * (grad - mean_grad - unit * mean_unit), gain_grad


def start_of(pieces_ref, scripts_ref, script_table_ref):
    entries, slots, width = pieces_ref.shape
    groups = script_table_ref.shape[0]
    pieces = pieces_ref[...].astype(F32).reshape(entries * slots, width)
    onehot = (scripts_ref[...] == lax.broadcasted_iota(jnp.int32, (1, groups), 1)).astype(F32)
    return pieces + jnp.dot(onehot, script_table_ref[...], precision=highest), onehot


def slot_weights(lengths, slots):
    rows = lengths.shape[0]
    slot = lax.broadcasted_iota(jnp.int32, (rows, 1), 0) % slots
    return jnp.where(slot <= lengths, 1.0 / (lengths + 1).astype(F32), 0.0)


def split_heads(pair):
    first = lax.broadcasted_iota(jnp.int32, pair.shape, 1) < HEAD_DIM
    zero = jnp.zeros_like(pair)
    return jnp.concatenate([jnp.where(first, pair, zero), jnp.where(first, zero, pair)], axis=0)


def join_heads(stacked):
    first = lax.broadcasted_iota(jnp.int32, (GROUP, PAIR), 1) < HEAD_DIM
    return jnp.where(first, stacked[:GROUP], stacked[GROUP:])


def forward_body(
    slots,
    pieces_ref,
    scripts_ref,
    lengths_ref,
    script_table_ref,
    gain_attn_ref,
    gain_ffn_ref,
    w_qkv_ref,
    w_out_ref,
    w_up_ref,
    w_down_ref,
    normed_ref,
    mixed_ref,
    context_ref,
    middle_ref,
    normed_ffn_ref,
    up_ref,
    hidden_ref,
    half_a_ref,
    half_b_ref,
):
    start, _ = start_of(pieces_ref, scripts_ref, script_table_ref)
    rows, width = start.shape
    lengths = lengths_ref[...]
    normed = (center(start)[0] * gain_attn_ref[...]).astype(BF16)
    normed_ref[...] = normed
    mixed = mm(normed, w_qkv_ref[...]).astype(BF16)
    mixed_ref[...] = mixed
    row = lax.broadcasted_iota(jnp.int32, (GROUP, GROUP), 0)
    col = lax.broadcasted_iota(jnp.int32, (GROUP, GROUP), 1)
    groups = []
    for base in range(0, rows, GROUP):
        part = mixed[base : base + GROUP]
        valid = (row // slots == col // slots) & (col % slots <= lengths[base : base + GROUP])
        pairs = []
        for low in range(0, width, PAIR):
            queries = part[:, low : low + PAIR]
            keys = split_heads(part[:, width + low : width + low + PAIR])
            values = split_heads(part[:, 2 * width + low : 2 * width + low + PAIR])
            raw = nt(queries, keys)
            probs = []
            for head in (raw[:, :GROUP], raw[:, GROUP:]):
                scores = jnp.where(valid, head * HEAD_DIM ** (-0.5), -1000000000.0)
                power = jnp.exp(scores - jnp.max(scores, axis=1, keepdims=True))
                power = jnp.where(valid, power, 0.0)
                probs.append((power / jnp.sum(power, axis=1, keepdims=True)).astype(BF16))
            pairs.append(mm(jnp.concatenate(probs, axis=1), values))
        groups.append(jnp.concatenate(pairs, axis=1).astype(BF16))
    context = jnp.concatenate(groups, axis=0)
    context_ref[...] = context
    middle = start + mm(context, w_out_ref[...])
    middle_ref[...] = middle
    normed_ffn = (center(middle)[0] * gain_ffn_ref[...]).astype(BF16)
    normed_ffn_ref[...] = normed_ffn
    weights = slot_weights(lengths, slots)

    def pool(value):
        return jnp.sum((value * weights).reshape(rows // slots, slots, value.shape[1]), axis=1)

    pooled = pool(middle)
    ff = w_up_ref.shape[1]
    step = ff // 4
    for low in range(0, ff, step):
        up = mm(normed_ffn, w_up_ref[:, low : low + step])
        up_ref[:, low : low + step] = up
        inner = GELU_SCALE * (up + GELU_CUBE * (up * up * up))
        hidden = (0.5 * up * (1.0 + jnp.tanh(inner))).astype(BF16)
        mean_hidden = pool(hidden.astype(F32))
        high = mean_hidden.astype(BF16)
        rest = (mean_hidden - high.astype(F32)).astype(BF16)
        hidden_ref[:, low : low + step] = high
        w_down = w_down_ref[low : low + step]
        pooled += mm(high, w_down) + mm(rest, w_down)
    pooled = pooled.astype(BF16)
    half_a_ref[...] = pooled[:, : width // 2]
    half_b_ref[...] = pooled[:, width // 2 :]


def whole_spec(value):
    return pl.BlockSpec(value.shape, lambda i: (0,) * value.ndim)


def rows_spec(rows, width):
    return pl.BlockSpec((rows, width), lambda i: (i, 0))


def block_forward(
    pieces, scripts, lengths, script_table, gain_attn, gain_ffn, w_qkv, w_out, w_up, w_down
):
    entries, slots, width = pieces.shape
    total = entries * slots
    rows = math.gcd(total, 256)
    some = rows // slots
    ff = w_up.shape[1]
    outs = [
        (total, width, BF16),
        (total, 3 * width, BF16),
        (total, width, BF16),
        (total, width, F32),
        (total, width, BF16),
        (total, ff, F32),
        (entries, ff, BF16),
        (entries, width // 2, BF16),
        (entries, width // 2, BF16),
    ]
    weights = (script_table, gain_attn, gain_ffn, w_qkv, w_out, w_up, w_down)
    return pl.pallas_call(
        functools.partial(forward_body, slots),
        grid=(total // rows,),
        in_specs=[
            pl.BlockSpec((some, slots, width), lambda i: (i, 0, 0)),
            rows_spec(rows, 1),
            rows_spec(rows, 1),
        ]
        + [whole_spec(value) for value in weights],
        out_specs=[rows_spec(rows if height == total else some, cols) for height, cols, _ in outs],
        out_shape=[jax.ShapeDtypeStruct((height, cols), dtype) for height, cols, dtype in outs],
        compiler_params=PARAMS,
        name="block_forward",
    )(pieces, scripts, lengths, *weights)


def ffn_back_body(
    slots,
    half_a_ref,
    half_b_ref,
    lengths_ref,
    up_ref,
    middle_ref,
    gain_ffn_ref,
    w_up_ref,
    w_down_ref,
    grad_up_ref,
    grad_middle_ref,
    grad_branch_ref,
    gain_grad_ref,
):
    pooled_grad = jnp.concatenate([half_a_ref[...], half_b_ref[...]], axis=1)
    rows, width = middle_ref.shape
    some = rows // slots
    weights = slot_weights(lengths_ref[...], slots)

    def spread(value):
        cols = value.shape[1]
        wide = jnp.broadcast_to(value[:, None, :], (some, slots, cols)).reshape(rows, cols)
        return wide * weights

    low_grad = pooled_grad.astype(BF16)
    ff = w_up_ref.shape[1]
    step = ff // 4
    grad_normed = jnp.zeros((rows, width), F32)
    for low in range(0, ff, step):
        up = up_ref[:, low : low + step]
        square = up * up
        tanh = jnp.tanh(GELU_SCALE * up * (1.0 + GELU_CUBE * square))
        slope = 0.5 * (1.0 + tanh) + 0.5 * up * (1.0 - tanh * tanh) * (
            GELU_SCALE + 3.0 * GELU_SCALE * GELU_CUBE * square
        )
        grad_hidden = spread(nt(low_grad, w_down_ref[low : low + step]))
        grad_up = (slope * grad_hidden).astype(BF16)
        grad_up_ref[:, low : low + step] = grad_up
        grad_normed += nt(grad_up, w_up_ref[:, low : low + step])
    unit, rate = center(middle_ref[...])
    grad, gain_grad = center_back(grad_normed, gain_ffn_ref[...], unit, rate)
    grad_middle = spread(pooled_grad) + grad
    grad_middle_ref[...] = grad_middle
    grad_branch_ref[...] = grad_middle.astype(BF16)

    @pl.when(pl.program_id(0) == 0)
    def _():
        gain_grad_ref[...] = jnp.zeros_like(gain_grad_ref)

    gain_grad_ref[...] += gain_grad


def ffn_back(half_a, half_b, lengths, up, middle, gain_ffn, w_up, w_down):
    total, width = middle.shape
    entries = half_a.shape[0]
    slots = total // entries
    rows = math.gcd(total, 256)
    some = rows // slots
    ff = w_up.shape[1]
    return pl.pallas_call(
        functools.partial(ffn_back_body, slots),
        grid=(total // rows,),
        in_specs=[
            rows_spec(some, width // 2),
            rows_spec(some, width // 2),
            rows_spec(rows, 1),
            rows_spec(rows, ff),
            rows_spec(rows, width),
            whole_spec(gain_ffn),
            whole_spec(w_up),
            whole_spec(w_down),
        ],
        out_specs=[
            rows_spec(rows, ff),
            rows_spec(rows, width),
            rows_spec(rows, width),
            pl.BlockSpec((1, width), lambda i: (0, 0)),
        ],
        out_shape=[
            jax.ShapeDtypeStruct((total, ff), BF16),
            jax.ShapeDtypeStruct((total, width), F32),
            jax.ShapeDtypeStruct((total, width), BF16),
            jax.ShapeDtypeStruct((1, width), F32),
        ],
        compiler_params=PARAMS,
        name="ffn_back",
    )(half_a, half_b, lengths, up, middle, gain_ffn, w_up, w_down)


def attn_back_body(
    pieces_ref,
    scripts_ref,
    lengths_ref,
    script_table_ref,
    gain_attn_ref,
    w_qkv_ref,
    w_out_ref,
    mixed_ref,
    grad_branch_ref,
    grad_middle_ref,
    grad_mixed_ref,
    grad_pieces_ref,
    gain_grad_ref,
    script_grad_ref,
):
    slots = pieces_ref.shape[1]
    start, onehot = start_of(pieces_ref, scripts_ref, script_table_ref)
    rows, width = start.shape
    lengths = lengths_ref[...]
    grad_ctx = nt(grad_branch_ref[...], w_out_ref[...]).astype(BF16)
    row = lax.broadcasted_iota(jnp.int32, (GROUP, GROUP), 0)
    col = lax.broadcasted_iota(jnp.int32, (GROUP, GROUP), 1)
    same = row // slots == col // slots
    for base in range(0, rows, GROUP):
        span = slice(base, base + GROUP)
        valid = same & (row % slots <= lengths[span])
        for low in range(0, width, PAIR):
            queries = mixed_ref[span, low : low + PAIR]
            keys = split_heads(mixed_ref[span, width + low : width + low + PAIR])
            values = split_heads(mixed_ref[span, 2 * width + low : 2 * width + low + PAIR])
            grad_pair = grad_ctx[span, low : low + PAIR]
            raw = nt(keys, queries)
            grad_raw = nt(values, grad_pair)
            probs, scores_grads = [], []
            for head in (slice(0, GROUP), slice(GROUP, 2 * GROUP)):
                scores = jnp.where(valid, raw[head] * HEAD_DIM ** (-0.5), -1000000000.0)
                power = jnp.exp(scores - jnp.max(scores, axis=0, keepdims=True))
                power = jnp.where(valid, power, 0.0)
                prob = power / jnp.sum(power, axis=0, keepdims=True)
                grad = grad_raw[head]
                inner = jnp.sum(grad * prob, axis=0, keepdims=True)
                probs.append(prob.astype(BF16))
                scores_grads.append((prob * (grad - inner) * HEAD_DIM ** (-0.5)).astype(BF16))
            scores_grad = jnp.concatenate(scores_grads, axis=0)
            grad_mixed_ref[span, low : low + PAIR] = tn(scores_grad, keys).astype(BF16)
            grad_keys = join_heads(mm(scores_grad, queries))
            grad_mixed_ref[span, width + low : width + low + PAIR] = grad_keys.astype(BF16)
            grad_values = join_heads(mm(jnp.concatenate(probs, axis=0), grad_pair))
            grad_mixed_ref[span, 2 * width + low : 2 * width + low + PAIR] = grad_values.astype(BF16)
    grad_normed = nt(grad_mixed_ref[...], w_qkv_ref[...])
    unit, rate = center(start)
    grad, gain_grad = center_back(grad_normed, gain_attn_ref[...], unit, rate)
    grad_pieces = grad_middle_ref[...] + grad
    grad_pieces_ref[...] = grad_pieces.reshape(grad_pieces_ref.shape)

    @pl.when(pl.program_id(0) == 0)
    def _():
        gain_grad_ref[...] = jnp.zeros_like(gain_grad_ref)
        script_grad_ref[...] = jnp.zeros_like(script_grad_ref)

    gain_grad_ref[...] += gain_grad
    script_grad_ref[...] += lax.dot_general(
        onehot, grad_pieces, (((0,), (0,)), ((), ())), precision=highest
    )


def attn_back(
    pieces, scripts, lengths, script_table, gain_attn, w_qkv, w_out, mixed, grad_branch, grad_middle
):
    entries, slots, width = pieces.shape
    total = entries * slots
    rows = math.gcd(total, 256)
    some = rows // slots
    return pl.pallas_call(
        attn_back_body,
        grid=(total // rows,),
        in_specs=[
            pl.BlockSpec((some, slots, width), lambda i: (i, 0, 0)),
            rows_spec(rows, 1),
            rows_spec(rows, 1),
            whole_spec(script_table),
            whole_spec(gain_attn),
            whole_spec(w_qkv),
            whole_spec(w_out),
            rows_spec(rows, 3 * width),
            rows_spec(rows, width),
            rows_spec(rows, width),
        ],
        out_specs=[
            rows_spec(rows, 3 * width),
            pl.BlockSpec((some, slots, width), lambda i: (i, 0, 0)),
            pl.BlockSpec((1, width), lambda i: (0, 0)),
            whole_spec(script_table),
        ],
        out_shape=[
            jax.ShapeDtypeStruct((total, 3 * width), BF16),
            jax.ShapeDtypeStruct((entries, slots, width), F32),
            jax.ShapeDtypeStruct((1, width), F32),
            jax.ShapeDtypeStruct(script_table.shape, F32),
        ],
        compiler_params=PARAMS,
        name="attn_back",
    )(pieces, scripts, lengths, script_table, gain_attn, w_qkv, w_out, mixed, grad_branch, grad_middle)


def per_device(
    pieces,
    lengths,
    scripts,
    script_table,
    gain_attn,
    gain_ffn,
    w_qkv,
    w_out,
    w_up,
    w_down,
    w_proj,
    token_ids,
    out_grad,
):
    entries, slots, width = pieces.shape
    ent_count = lax.axis_size("ent")
    rep_count = lax.axis_size("rep")
    devices = ent_count * rep_count
    features = w_proj.shape[1]
    vocab = entries * devices
    rows_dev, text_len = token_ids.shape
    tokens = rows_dev * text_len
    levels = make_levels(ent_count, rep_count)
    sizes = tuple(size for _, size, _ in levels)
    order_a, order_b = orders(levels)
    me = lax.axis_index("ent") * rep_count + lax.axis_index("rep")
    chunks = 1 if devices <= 32 else 4
    each = entries // chunks
    span = vocab // chunks
    half = width // 2
    slot = slot_of(token_ids // entries ^ me, levels)
    within = token_ids % entries
    slot_ids = (within // each * span + slot * each + within % each).reshape(1, tokens)

    def then(value, before):
        return value if chunks == 1 or before is None else lax.optimization_barrier((value, before))[0]

    flat_grad = out_grad.reshape(features, tokens)
    part_tables, grad_pooled_a, grad_pooled_b = [], [], []
    last = None
    for chunk in range(chunks):
        part, part_a, part_b = scatter_rows(
            then(slot_ids - chunk * span, last), flat_grad, w_proj, span
        )
        part_a = reduce_scatter(part_a.reshape(sizes + (each, half)), levels, order_a)
        part_b = reduce_scatter(part_b.reshape(sizes + (each, half)), levels, order_b)
        part_tables.append(part)
        grad_pooled_a.append(part_a)
        grad_pooled_b.append(part_b)
        last = (part_a, part_b)
    grad_pooled_a = jnp.concatenate(grad_pooled_a, axis=0)
    grad_pooled_b = jnp.concatenate(grad_pooled_b, axis=0)
    pieces = then(pieces, last)

    script_rows = jnp.repeat(scripts, slots)[:, None]
    length_rows = jnp.repeat(lengths, slots)[:, None]
    gain_attn, gain_ffn = gain_attn[None], gain_ffn[None]
    normed, mixed, context, middle, normed_ffn, up, hidden, half_a, half_b = block_forward(
        pieces, script_rows, length_rows, script_table, gain_attn, gain_ffn, w_qkv, w_out, w_up, w_down
    )
    tables, part_proj = [], jnp.zeros((width, features), F32)
    for chunk in range(chunks):
        mine_a, mine_b = half_a[chunk * each :][:each], half_b[chunk * each :][:each]
        mine_a = then(mine_a, tables[-1] if tables else None)
        mine_b = then(mine_b, tables[-1] if tables else None)
        pooled_a = gather_slots(mine_a, levels, order_a[::-1]).reshape(span, half)
        pooled_b = gather_slots(mine_b, levels, order_b[::-1]).reshape(span, half)
        table, part = table_and_grad(pooled_a, pooled_b, w_proj, part_tables[chunk])
        tables.append(table)
        part_proj = part_proj + part
    grad_w_proj = part_proj + swap(part_proj, levels[0], 1)
    looked_up = lookup(slot_ids, tables).reshape(features, rows_dev, text_len)

    def summed(left, right, order):
        height, cols = left.shape[1], right.shape[1]
        cut = len(levels)
        while math.prod(sizes[:cut]) * 16 > height:
            cut -= 1
        near, far = levels[:cut], levels[cut:]
        count = math.prod(sizes[:cut])
        order = [level for level in order if level < cut]
        slot_index = jnp.arange(count, dtype=jnp.int32) ^ slot_of(me, near)
        part = weight_slots(slot_index, left, right)
        mine = reduce_scatter(part.reshape(sizes[:cut] + part.shape[1:]), near, order)
        mine = summed_small(mine.astype(BF16), far)
        return unpack(slot_index, gather_slots(mine, near, order[::-1]).reshape(part.shape))

    def summed_small(value, over):
        for level in over:
            total = value.astype(F32)
            for k in range(1, level[1]):
                total = total + swap(value, level, k).astype(F32)
            value = total.astype(value.dtype)
        return value

    grad_rows = jnp.concatenate([grad_pooled_a, grad_pooled_b], axis=1).astype(BF16)
    grad_w_down = summed(hidden, grad_rows, order_a)
    grad_up, grad_middle, grad_branch, part_gain_ffn = ffn_back(
        grad_pooled_a, grad_pooled_b, length_rows, up, middle, gain_ffn, w_up, w_down
    )
    grad_w_up = summed(normed_ffn, grad_up, order_b)
    grad_w_out = summed(context, grad_branch, order_b)
    grad_mixed, grad_pieces, part_gain_attn, part_script = attn_back(
        pieces,
        script_rows,
        length_rows,
        script_table,
        gain_attn,
        w_qkv,
        w_out,
        mixed,
        grad_branch,
        grad_middle,
    )
    grad_w_qkv = summed(normed, grad_mixed, order_a)
    small = summed_small(
        jnp.concatenate([part_script, part_gain_attn, part_gain_ffn], axis=0), levels
    )
    groups = script_table.shape[0]
    return (
        looked_up,
        grad_pieces,
        small[:groups],
        small[groups],
        small[groups + 1],
        grad_w_qkv,
        grad_w_out,
        grad_w_up,
        grad_w_down,
        grad_w_proj,
    )


def solution(mesh):
    in_specs = (
        P(("ent", "rep"), None, None),
        P(("ent", "rep")),
        P(("ent", "rep")),
        P(),
        P(),
        P(),
        P(),
        P(),
        P(),
        P(),
        P(None, "ent"),
        P("rep", None),
        P("ent", "rep", None),
    )
    out_specs = (
        P("ent", "rep", None),
        P(("ent", "rep"), None, None),
        P(),
        P(),
        P(),
        P(),
        P(),
        P(),
        P(),
        P(None, "ent"),
    )
    return jax.shard_map(
        per_device, mesh=mesh, in_specs=in_specs, out_specs=out_specs, check_vma=False
    )
```

```python
import functools
import math

import jax
import jax.numpy as jnp
import numpy as np
from jax import lax
from jax.experimental import pallas as pl
from jax.experimental.pallas import tpu as pltpu
from jax.sharding import PartitionSpec as P

HEADS = 8
HEAD_DIM = 64
F32 = jnp.float32
BF16 = jnp.bfloat16
highest = lax.Precision.HIGHEST
MIB = 1024 * 1024


def make_levels(ent_count, rep_count):
    levels = [("rep", rep_count, 0)]
    bit, total = 0, ent_count.bit_length() - 1
    while bit < total:
        width = 1 if bit < 2 else min(2, total - bit)
        levels.append(("ent", 1 << width, bit))
        bit += width
    return levels


def slot_of(number, levels):
    rep_count = levels[0][1]
    slot = number % rep_count
    ent = number // rep_count
    for _, size, shift in levels[1:]:
        slot = slot * size + (ent >> shift) % size
    return slot


def swap(value, level, k):
    name, size, shift = level
    count = lax.axis_size(name)
    return lax.ppermute(value, name, [(i, i ^ (k << shift)) for i in range(count)])


def merge(value):
    return value.reshape((-1,) + value.shape[-2:])


class Line:
    def __init__(self):
        self.last = []

    def run(self, body, name, micros, grid, ins, outs, prefetch=(), alias=None, room=32 * MIB):
        count = len(prefetch) + len(ins)
        extra = self.last + ([] if alias is None else [alias])

        def wrapped(*refs):
            body(*refs[:count], *refs[count + len(extra) :])

        results = pl.pallas_call(
            wrapped,
            grid_spec=pltpu.PrefetchScalarGridSpec(
                num_scalar_prefetch=len(prefetch),
                grid=grid,
                in_specs=[spec for _, spec in ins] + [pl.BlockSpec(memory_space=pl.ANY)] * len(extra),
                out_specs=[spec for _, _, spec in outs],
            ),
            out_shape=[jax.ShapeDtypeStruct(shape, dtype) for shape, dtype, _ in outs],
            input_output_aliases={} if alias is None else {count + len(extra) - 1: 0},
            compiler_params=pltpu.CompilerParams(vmem_limit_bytes=room),
            cost_estimate=pl.CostEstimate(
                flops=int(micros * 1e9), bytes_accessed=int(micros * 3e6), transcendentals=0
            ),
            name=name,
        )(*prefetch, *(value for value, _ in ins), *extra)
        self.last = [min(results, key=lambda value: value.size)]
        return results


def swap(value, level, k=1):
    name, size, shift = level
    count = lax.axis_size(name)
    return lax.ppermute(value, name, [(i, i ^ (k << shift)) for i in range(count)])


def swaps(values, level):
    return [swap(value, level, k) for k, value in enumerate(values, 1)]


def stage_body(layout, cuts, *refs):
    sums, position = [], 0
    for number in layout:
        sums.append(refs[position : position + number])
        position += number

    def piece(number, index, cols):
        total = sums[number][0][index][:, cols]
        for ref in sums[number][1:]:
            total = total.astype(F32) + ref[index][:, cols].astype(F32)
        return total

    for out_ref, sources in zip(refs[position:], cuts):
        for target, parts in sources:
            for number, index, cols, row, col in parts:
                value = piece(number, index, cols).astype(out_ref.dtype)
                where = target + (slice(row, row + value.shape[0]), slice(col, col + value.shape[1]))
                out_ref[where] = value


def stage(line, sums, outs, steps=1):
    values = [value for kept, received in sums for value in [kept, *received]]

    def spec(shape):
        return pl.BlockSpec(memory_space=pltpu.VMEM)

    cuts = [
        [(target, source(target)) for target in np.ndindex(*lead)] for lead, _, _, _, source in outs
    ]
    shapes = [(lead + (rows, cols), dtype) for lead, rows, cols, dtype, _ in outs]
    held = [(value.shape, value.dtype) for value in values] + [(shape, jnp.dtype(dtype)) for shape, dtype in shapes]
    return line.run(
        functools.partial(stage_body, [1 + len(received) for _, received in sums], cuts),
        "exchange",
        2,
        (),
        [(value, spec(value.shape)) for value in values],
        [(shape, dtype, spec(shape)) for shape, dtype in shapes],
        room=2 * MIB + sum(math.prod(shape) * dtype.itemsize for shape, dtype in held),
    )


ALL = slice(None)


def split(number, value, axis, cols=ALL, width=None):
    lead = value.shape[:-2]
    rest = lead[:axis] + lead[axis + 1 :]
    outs = []
    for k in range(lead[axis]):

        def source(index, k=k):
            return [(number, index[:axis] + (k,) + index[axis:], cols, 0, 0)]

        outs.append((rest, value.shape[-2], width or value.shape[-1], F32 if k == 0 else BF16, source))
    return outs


def stacked(numbers, value, axis, rows=ALL):
    lead = value.shape[:-2]
    shape = lead[:axis] + (len(numbers),) + lead[axis:]

    def source(index):
        return [(numbers[index[axis]], index[:axis] + index[axis + 1 :], ALL, 0, 0)]

    return (shape, value.shape[-2], value.shape[-1], value.dtype, source)


def sum_halves(line, keep, send, levels, out):
    received = swap(send, levels[0])
    yield
    rows, width = keep.shape[-2:]
    half = width // 2
    left, right = slice(0, half), slice(half, width)
    steps = 4 if rows % 64 == 0 else 1
    outs = split(0, keep, 0, left, half) + split(0, keep, 1, right, half)
    keep_a, send_a, keep_b, send_b = stage(line, [(keep, [received])], outs, steps)
    got_a, got_b = swap(send_a, levels[1]), swap(send_b, levels[2])
    yield
    outs = split(0, keep_a, 0) + split(1, keep_b, 0)
    sums = [(keep_a, [got_a]), (keep_b, [got_b])]
    keep_a, send_a, keep_b, send_b = stage(line, sums, outs, steps)
    sums = [(keep_a, [swap(send_a, levels[2])]), (keep_b, [swap(send_b, levels[1])])]
    yield
    for place, level in enumerate(levels[3:]):
        if place == 0:
            lead = keep_a.shape[1:-2]

            def source(index, k):
                return [(0, (k,) + index, ALL, 0, 0), (1, (k,) + index, ALL, 0, half)]

            outs = [
                (lead, rows, width, F32 if k == 0 else BF16, functools.partial(source, k=k))
                for k in range(level[1])
            ]
        else:
            outs = split(0, keep, 0)
        keep, *sends = stage(line, sums, outs)
        sums = [(keep, swaps(sends, level))]
        yield
    out += stage(line, sums, [((), rows, width, F32, lambda index: [(0, (), ALL, 0, 0)])])
    yield


def finish(line, sums, far, rows):
    for level in far:
        outs = [((), rows, PANEL, dtype, lambda index: [(0, (), ALL, 0, 0)]) for dtype in (F32, BF16)]
        keep, send = stage(line, sums, outs)
        sums = [(keep, [swap(send, level, k) for k in range(1, level[1])])]
        yield
    yield stage(line, sums, [((), rows, PANEL, BF16, lambda index: [(0, (), ALL, 0, 0)])])[0]


def all_sum(line, keep, send, near, far, out):
    received = swap(send, near[0])
    yield
    rows = keep.shape[-2]
    sums = [(keep, [received])]
    for level in near[1:]:
        keep, *sends = stage(line, sums, split(0, keep, 0))
        sums = [(keep, swaps(sends, level))]
        yield
    for value in finish(line, sums, far, rows):
        if value is None:
            yield
    for level in near[:0:-1]:
        got = [swap(value, level, k) for k in range(1, level[1])]
        yield
        numbers = list(range(level[1]))
        value = stage(line, [(part, []) for part in [value, *got]], [stacked(numbers, value, 0)])[0]
    out += [value, swap(value, near[0])]
    yield


def all_sum_two(line, keep_a, send_a, keep_b, send_b, near, far, out):
    got_a, got_b = swap(send_a, near[0]), swap(send_b, near[0])
    yield
    rows = keep_a.shape[-2]
    outs = split(0, keep_a, 0) + split(1, keep_b, 1)
    keep_a, send_a, keep_b, send_b = stage(line, [(keep_a, [got_a]), (keep_b, [got_b])], outs)
    got_a, got_b = swap(send_a, near[1]), swap(send_b, near[2])
    yield
    outs = split(0, keep_a, 0) + split(1, keep_b, 0)
    keep_a, send_a, keep_b, send_b = stage(line, [(keep_a, [got_a]), (keep_b, [got_b])], outs)
    sums = [(keep_a, [swap(send_a, near[2])]), (keep_b, [swap(send_b, near[1])])]
    yield
    for place, level in enumerate(near[3:]):
        if place == 0:
            lead = keep_a.shape[1:-2]

            def source(index, k):
                return [(0, (k,) + index, ALL, 0, 0), (1, (k,) + index, ALL, rows, 0)]

            outs = [
                (lead, 2 * rows, PANEL, F32 if k == 0 else BF16, functools.partial(source, k=k))
                for k in range(level[1])
            ]
        else:
            outs = split(0, keep, 0)
        keep, *sends = stage(line, sums, outs)
        sums = [(keep, swaps(sends, level))]
        yield
    for value in finish(line, sums, far, 2 * rows):
        if value is None:
            yield
    for place, level in reversed(list(enumerate(near[3:]))):
        got = [swap(value, level, k) for k in range(1, level[1])]
        yield
        numbers = list(range(level[1]))
        value = stage(line, [(part, []) for part in [value, *got]], [stacked(numbers, value, 0)])[0]
    value_a, value_b = value[..., :rows, :], value[..., rows:, :]
    got_a, got_b = swap(value_a, near[2]), swap(value_b, near[1])
    yield
    sums = [(part, []) for part in (value_a, got_a, value_b, got_b)]
    outs = [stacked([0, 1], value_a, 0), stacked([2, 3], value_b, 0)]
    value_a, value_b = stage(line, sums, outs)
    got_a, got_b = swap(value_a, near[1]), swap(value_b, near[2])
    yield
    sums = [(part, []) for part in (value_a, got_a, value_b, got_b)]
    outs = [stacked([0, 1], value_a, 0), stacked([2, 3], value_b, 1)]
    value_a, value_b = stage(line, sums, outs)
    out += [value_a, swap(value_a, near[0]), value_b, swap(value_b, near[0])]
    yield


def fixed(shape):
    return pl.BlockSpec(shape, lambda i, *_: (0,) * len(shape))


def rows_of(rows, width):
    return pl.BlockSpec((rows, width), lambda i, *_: (i, 0))


def selector(ids, base, rows):
    entry = lax.broadcasted_iota(jnp.int32, (rows, 1), 0).astype(jnp.int16)
    return jnp.where(entry == (ids - base).astype(jnp.int16), jnp.ones((), BF16), jnp.zeros((), BF16))


def nt(left, right):
    return lax.dot_general(left, right, (((1,), (1,)), ((), ())), preferred_element_type=F32)


def tn(left, right):
    return lax.dot_general(left, right, (((0,), (0,)), ((), ())), preferred_element_type=F32)


def mm(left, right):
    return jnp.dot(left, right, preferred_element_type=F32)


def scatter_some(first, ids_ref, grad, proj_ref, table_ref, pooled_ref):
    rows = table_ref.shape[0]
    part = nt(selector(ids_ref[...], first + pl.program_id(0) * rows, rows), grad).astype(BF16)
    table_ref[...] = part
    pooled_ref[...] = nt(part, proj_ref[...]).astype(pooled_ref.dtype)


def scatter_first_body(first, ids_ref, grad_ref, proj_ref, table_ref, pooled_ref, flat_ref):
    @pl.when(pl.program_id(0) == 0)
    def _():
        flat_ref[...] = grad_ref[...].reshape(flat_ref.shape)

    scatter_some(first, ids_ref, flat_ref[...], proj_ref, table_ref, pooled_ref)


def scatter_body(first, ids_ref, flat_ref, proj_ref, table_ref, pooled_ref):
    scatter_some(first, ids_ref, flat_ref[...], proj_ref, table_ref, pooled_ref)


def scatter_rows(line, ids, grad, w_proj, first, count, dtype):
    features = grad.shape[0]
    tokens = ids.shape[1]
    width = w_proj.shape[0]
    rows = min(512, count)
    flat = (features, tokens)
    fresh = grad.ndim == 3
    return line.run(
        functools.partial(scatter_first_body if fresh else scatter_body, first),
        "scatter_rows",
        14,
        (count // rows,),
        [(ids, fixed((1, tokens))), (grad, fixed(grad.shape)), (w_proj, fixed(w_proj.shape))],
        [
            ((count, features), BF16, rows_of(rows, features)),
            ((count, width), dtype, rows_of(rows, width)),
        ]
        + ([(flat, BF16, fixed(flat))] if fresh else []),
        room=44 * MIB,
    )


def table_body(steps, each, owners_ref, pooled_ref, proj_ref, own_ref, other_ref, table_ref, grad_ref):
    step = pl.program_id(0)
    slots = own_ref.shape[0] // each

    @pl.when(step == 0)
    def _():
        grad_ref[...] = jnp.zeros_like(grad_ref)

    parts = []
    for j in range(slots):
        base = pl.multiple_of(owners_ref[step * slots + j] * each, each)
        parts.append(pooled_ref[pl.ds(base, each)])
    pooled = jnp.concatenate(parts, axis=0)
    cols = lax.dot_general(
        proj_ref[...], pooled, (((0,), (1,)), ((), ())), preferred_element_type=F32
    )
    table_ref[...] = cols.astype(BF16)

    @pl.when(step < steps)
    def _():
        grad_ref[...] += tn(pooled, own_ref[...])

    @pl.when(step >= steps)
    def _():
        grad_ref[...] += tn(pooled, other_ref[...])


def table_and_grad(line, owners, pooled, w_proj, part_own, part_other):
    vocab, width = pooled.shape
    features = w_proj.shape[1]
    rows = min(1024, vocab // 2)
    steps = vocab // 2 // rows
    return line.run(
        functools.partial(table_body, steps, vocab // owners.shape[0]),
        "table_and_grad",
        7,
        (2 * steps,),
        [
            (pooled, fixed(pooled.shape)),
            (w_proj, fixed(w_proj.shape)),
            (part_own, pl.BlockSpec((rows, features), lambda i, *_: (jnp.minimum(i, steps - 1), 0))),
            (part_other, pl.BlockSpec((rows, features), lambda i, *_: (jnp.maximum(i - steps, 0), 0))),
        ],
        [
            ((features, vocab), BF16, pl.BlockSpec((features, rows), lambda i, *_: (0, i))),
            ((width, features), F32, fixed((width, features))),
        ],
        [owners],
    )


def lookup_body(chunk, ids_ref, *refs):
    table_refs, out_ref = refs[:-1], refs[-1]
    rows = ids_ref.shape[0]

    def find(base, table):
        picks = [selector(ids_ref[row : row + 1], base, chunk) for row in range(rows)]
        return mm(table, jnp.concatenate(picks, axis=1))

    total = None
    for index, table_ref in enumerate(table_refs):
        vocab = table_ref.shape[1]
        for inner in range(0, vocab, chunk):
            part = find(index * vocab + inner, table_ref[:, inner : inner + chunk])
            total = part if total is None else total + part
    out_ref[...] = total.astype(BF16).reshape(out_ref.shape)


def lookup(line, ids, tables, half, before=None):
    rows, text_len = ids.shape
    features, vocab = tables[0].shape
    block = math.gcd(text_len // 2, 256)
    steps = text_len // 2 // block
    return line.run(
        functools.partial(lookup_body, min(vocab, 4096)),
        "lookup",
        13,
        (steps,),
        [(ids, pl.BlockSpec((rows, block), lambda i, *_: (0, i + half * steps)))]
        + [(table, fixed(table.shape)) for table in tables],
        [
            (
                (features, rows, text_len),
                BF16,
                pl.BlockSpec((features, rows, block), lambda i, *_: (0, 0, i + half * steps)),
            )
        ],
        alias=before,
    )[0]


PANEL = 512


def store_slots(slots_ref, first, part, keep_ref, send_ref):
    rows = keep_ref.shape[1]
    half = keep_ref.shape[0]
    for j in range(part.shape[0] // rows):
        slot = slots_ref[first + j]
        piece = part[j * rows : (j + 1) * rows]

        @pl.when(slot < half)
        def _():
            keep_ref[slot] = piece

        @pl.when(slot >= half)
        def _():
            send_ref[slot - half] = piece.astype(BF16)


def weight_body(slots_ref, left_ref, right_ref, keep_ref, send_ref):
    part = tn(left_ref[...], right_ref[...])
    store_slots(slots_ref, pl.program_id(0) * (part.shape[0] // keep_ref.shape[1]), part, keep_ref, send_ref)


def two_weights_body(last, slots_ref, left_ref, right_ref, left2_ref, right2_ref, keep_ref, send_ref):
    step = pl.program_id(0)
    each = left_ref.shape[1] // keep_ref.shape[1]

    @pl.when(step < last)
    def _():
        store_slots(slots_ref, step * each, tn(left_ref[...], right_ref[...]), keep_ref, send_ref)

    @pl.when(step == last)
    def _():
        store_slots(slots_ref, step * each, tn(left2_ref[...], right2_ref[...]), keep_ref, send_ref)


def slot_outs(count, rows):
    shape = (count // 2, rows, PANEL)
    return [(shape, F32, fixed(shape)), (shape, BF16, fixed(shape))]


def panel_of(depth):
    return pl.BlockSpec((depth, PANEL), lambda i, *_: (0, i))


def tall_weight(line, slots, left, right):
    depth, height = left.shape
    return line.run(
        weight_body,
        "tall_weight",
        6,
        (height // PANEL,),
        [(left, panel_of(depth)), (right, fixed(right.shape))],
        slot_outs(slots.shape[0], height // slots.shape[0]),
        [slots],
    )


def wide_weight(line, slots, left, right):
    depth, cols = right.shape
    return line.run(
        weight_body,
        "wide_weight",
        8,
        (cols // PANEL,),
        [(left, fixed(left.shape)), (right, panel_of(depth))],
        slot_outs(slots.shape[0], cols // PANEL * left.shape[1] // slots.shape[0]),
        [slots],
    )


def two_weights(line, slots, left, right, left2, right2):
    depth, cols = right.shape
    last = cols // PANEL
    return line.run(
        functools.partial(two_weights_body, last),
        "two_weights",
        8,
        (last + 1,),
        [
            (left, fixed(left.shape)),
            (right, pl.BlockSpec((depth, PANEL), lambda i, *_: (0, jnp.minimum(i, last - 1)))),
            (left2, fixed(left2.shape)),
            (right2, fixed(right2.shape)),
        ],
        slot_outs(slots.shape[0], (last + 1) * left.shape[1] // slots.shape[0]),
        [slots],
    )


def load_slots(slots_ref, first, own_ref, other_ref, out_ref):
    half, rows, _ = own_ref.shape
    for j in range(out_ref.shape[0] // rows):
        slot = slots_ref[first + j]

        @pl.when(slot < half)
        def _():
            out_ref[j * rows : (j + 1) * rows] = own_ref[slot].astype(F32)

        @pl.when(slot >= half)
        def _():
            out_ref[j * rows : (j + 1) * rows] = other_ref[slot - half].astype(F32)


def unpack_body(slots_ref, own_ref, other_ref, out_ref):
    each = out_ref.shape[0] // own_ref.shape[1]
    load_slots(slots_ref, pl.program_id(0) * each, own_ref, other_ref, out_ref)


def unpack_two_body(last, slots_ref, own_ref, other_ref, out_ref, out2_ref):
    step = pl.program_id(0)
    each = out_ref.shape[0] // own_ref.shape[1]

    @pl.when(step < last)
    def _():
        load_slots(slots_ref, step * each, own_ref, other_ref, out_ref)

    @pl.when(step == last)
    def _():
        load_slots(slots_ref, step * each, own_ref, other_ref, out2_ref)


def unpack(line, slots, own, other, height, cols):
    tall = cols == PANEL
    tile = 512
    index = (lambda i, *_: (i, 0)) if tall else (lambda i, *_: (0, i))
    return line.run(
        unpack_body,
        "unpack",
        5,
        (height * cols // (tile * PANEL),),
        [(own, fixed(own.shape)), (other, fixed(other.shape))],
        [((height, cols), F32, pl.BlockSpec((tile if tall else height, PANEL), index))],
        [slots],
    )[0]


def unpack_two(line, slots, own, other, height, cols):
    last = cols // PANEL
    return line.run(
        functools.partial(unpack_two_body, last),
        "unpack_two",
        5,
        (last + 1,),
        [(own, fixed(own.shape)), (other, fixed(other.shape))],
        [
            (
                (height, cols),
                F32,
                pl.BlockSpec((height, PANEL), lambda i, *_: (0, jnp.minimum(i, last - 1))),
            ),
            ((height, PANEL), F32, fixed((height, PANEL))),
        ],
        [slots],
    )


GROUP = 128
PAIR = 2 * HEAD_DIM
GELU_SCALE = 0.7978845608028654
GELU_CUBE = 0.044715


def center(values):
    centered = values - jnp.mean(values, axis=-1, keepdims=True)
    spread = jnp.mean(centered * centered, axis=-1, keepdims=True)
    rate = lax.rsqrt(spread + 1e-05)
    return centered * rate, rate


def center_back(grad, gain, unit, rate):
    gain_grad = jnp.sum(grad * unit, axis=0, keepdims=True)
    grad = grad * gain
    mean_grad = jnp.mean(grad, axis=-1, keepdims=True)
    mean_unit = jnp.mean(grad * unit, axis=-1, keepdims=True)
    return rate * (grad - mean_grad - unit * mean_unit), gain_grad


def start_of(pieces_ref, scripts_ref, script_table_ref):
    entries, slots, width = pieces_ref.shape
    groups = script_table_ref.shape[0]
    pieces = pieces_ref[...].astype(F32).reshape(entries * slots, width)
    onehot = (scripts_ref[...] == lax.broadcasted_iota(jnp.int32, (1, groups), 1)).astype(F32)
    return pieces + jnp.dot(onehot, script_table_ref[...], precision=highest), onehot


def slot_weights(lengths, slots):
    rows = lengths.shape[0]
    slot = lax.broadcasted_iota(jnp.int32, (rows, 1), 0) % slots
    return jnp.where(slot <= lengths, 1.0 / (lengths + 1).astype(F32), 0.0)


def split_heads(pair):
    first = lax.broadcasted_iota(jnp.int32, pair.shape, 1) < HEAD_DIM
    zero = jnp.zeros_like(pair)
    return jnp.concatenate([jnp.where(first, pair, zero), jnp.where(first, zero, pair)], axis=0)


def join_heads(stacked):
    first = lax.broadcasted_iota(jnp.int32, (GROUP, PAIR), 1) < HEAD_DIM
    return jnp.where(first, stacked[:GROUP], stacked[GROUP:])


def attn_body(
    slots,
    pieces_ref,
    scripts_ref,
    lengths_ref,
    script_table_ref,
    gain_attn_ref,
    gain_ffn_ref,
    w_qkv_ref,
    w_out_ref,
    normed_ref,
    mixed_ref,
    context_ref,
    middle_ref,
    normed_ffn_ref,
):
    start, _ = start_of(pieces_ref, scripts_ref, script_table_ref)
    rows, width = start.shape
    lengths = lengths_ref[...]
    normed = (center(start)[0] * gain_attn_ref[...]).astype(BF16)
    normed_ref[...] = normed
    mixed = mm(normed, w_qkv_ref[...]).astype(BF16)
    mixed_ref[...] = mixed
    row = lax.broadcasted_iota(jnp.int32, (GROUP, GROUP), 0)
    col = lax.broadcasted_iota(jnp.int32, (GROUP, GROUP), 1)
    groups = []
    for base in range(0, rows, GROUP):
        part = mixed[base : base + GROUP]
        valid = (row // slots == col // slots) & (col % slots <= lengths[base : base + GROUP])
        lows = range(0, width, PAIR)
        raws = [
            nt(part[:, low : low + PAIR], split_heads(part[:, width + low : width + low + PAIR]))
            for low in lows
        ]
        heads = [raw[:, side : side + GROUP] for raw in raws for side in (0, GROUP)]
        heads = [jnp.where(valid, head * HEAD_DIM ** (-0.5), -1000000000.0) for head in heads]
        heads = [jnp.exp(head - jnp.max(head, axis=1, keepdims=True)) for head in heads]
        heads = [(head * (1.0 / jnp.sum(head, axis=1, keepdims=True))).astype(BF16) for head in heads]
        pairs = [
            mm(
                jnp.concatenate(heads[2 * j : 2 * j + 2], axis=1),
                split_heads(part[:, 2 * width + low : 2 * width + low + PAIR]),
            )
            for j, low in enumerate(lows)
        ]
        groups.append(jnp.concatenate(pairs, axis=1).astype(BF16))
    context = jnp.concatenate(groups, axis=0)
    context_ref[...] = context
    middle = start + mm(context, w_out_ref[...])
    middle_ref[...] = middle
    normed_ffn_ref[...] = (center(middle)[0] * gain_ffn_ref[...]).astype(BF16)


def attn_forward(
    line, pieces, scripts, lengths, script_table, gain_attn, gain_ffn, w_qkv, w_out
):
    entries, slots, width = pieces.shape
    total = entries * slots
    rows = math.gcd(total, 256)
    some = rows // slots
    whole = (script_table, gain_attn, gain_ffn, w_qkv, w_out)
    return line.run(
        functools.partial(attn_body, slots),
        "attn_forward",
        12,
        (total // rows,),
        [
            (pieces, pl.BlockSpec((some, slots, width), lambda i, *_: (i, 0, 0))),
            (scripts, rows_of(rows, 1)),
            (lengths, rows_of(rows, 1)),
        ]
        + [(value, fixed(value.shape)) for value in whole],
        [
            ((total, width), BF16, rows_of(rows, width)),
            ((total, 3 * width), BF16, rows_of(rows, 3 * width)),
            ((total, width), BF16, rows_of(rows, width)),
            ((total, width), F32, rows_of(rows, width)),
            ((total, width), BF16, rows_of(rows, width)),
        ],
    )


def ffn_body(
    slots,
    length_rows_ref,
    lengths_ref,
    middle_ref,
    normed_ref,
    w_up_ref,
    w_down_ref,
    slope_ref,
    hidden_ref,
    pooled_ref,
):
    rows, width = middle_ref.shape
    some = rows // slots
    weights = slot_weights(length_rows_ref[...], slots)
    row = lax.broadcasted_iota(jnp.int32, (some, rows), 1)
    entry = lax.broadcasted_iota(jnp.int32, (some, rows), 0)
    lengths = lengths_ref[...]
    valid = (row // slots == entry) & (row % slots <= lengths)
    valid = jnp.where(valid, 1.0, 0.0).astype(BF16)
    scale = 1.0 / (lengths + 1).astype(F32)
    pooled = jnp.sum((middle_ref[...] * weights).reshape(some, slots, width), axis=1)
    ff = w_up_ref.shape[1]
    step = ff // 4
    for low in range(0, ff, step):
        up = mm(normed_ref[...], w_up_ref[:, low : low + step])
        square = up * up
        tanh = jnp.tanh(up * (GELU_SCALE + GELU_SCALE * GELU_CUBE * square))
        half_up = 0.5 * up
        hidden = (half_up + half_up * tanh).astype(BF16)
        slope_ref[:, low : low + step] = (0.5 + 0.5 * tanh) + half_up * (1.0 - tanh * tanh) * (
            GELU_SCALE + 3.0 * GELU_SCALE * GELU_CUBE * square
        )
        mean_hidden = mm(valid, hidden) * scale
        high = mean_hidden.astype(BF16)
        rest = (mean_hidden - high.astype(F32)).astype(BF16)
        hidden_ref[:, low : low + step] = high
        w_down = w_down_ref[low : low + step]
        pooled += mm(high, w_down) + mm(rest, w_down)
    pooled_ref[...] = pooled.astype(BF16)


def ffn_forward(line, length_rows, lengths, middle, normed, w_up, w_down):
    total, width = middle.shape
    entries = lengths.shape[0]
    slots = total // entries
    rows = math.gcd(total, 256)
    some = rows // slots
    ff = w_up.shape[1]
    return line.run(
        functools.partial(ffn_body, slots),
        "ffn_forward",
        12,
        (total // rows,),
        [
            (length_rows, rows_of(rows, 1)),
            (lengths, rows_of(some, 1)),
            (middle, rows_of(rows, width)),
            (normed, rows_of(rows, width)),
            (w_up, fixed(w_up.shape)),
            (w_down, fixed(w_down.shape)),
        ],
        [
            ((total, ff), F32, rows_of(rows, ff)),
            ((entries, ff), BF16, rows_of(some, ff)),
            ((entries, width), BF16, rows_of(some, width)),
        ],
    )


def ffn_back_body(
    slots,
    pooled_grad_ref,
    lengths_ref,
    slope_ref,
    middle_ref,
    gain_ffn_ref,
    w_up_ref,
    w_down_ref,
    grad_up_ref,
    grad_middle_ref,
    grad_branch_ref,
    gain_grad_ref,
):
    pooled_grad = pooled_grad_ref[...]
    rows, width = middle_ref.shape
    some = rows // slots
    wide = jnp.broadcast_to(pooled_grad[:, None, :], (some, slots, width)).reshape(rows, width)
    grad_final = wide * slot_weights(lengths_ref[...], slots)
    grad_ffn = grad_final.astype(BF16)
    ff = w_up_ref.shape[1]
    step = ff // 4
    grad_normed = jnp.zeros((rows, width), F32)
    for low in range(0, ff, step):
        grad_hidden = nt(grad_ffn, w_down_ref[low : low + step])
        grad_up = (slope_ref[:, low : low + step] * grad_hidden).astype(BF16)
        grad_up_ref[:, low : low + step] = grad_up
        grad_normed += nt(grad_up, w_up_ref[:, low : low + step])
    unit, rate = center(middle_ref[...])
    grad, gain_grad = center_back(grad_normed, gain_ffn_ref[...], unit, rate)
    grad_middle = grad_final + grad
    grad_middle_ref[...] = grad_middle
    grad_branch_ref[...] = grad_middle.astype(BF16)

    @pl.when(pl.program_id(0) == 0)
    def _():
        gain_grad_ref[...] = jnp.zeros_like(gain_grad_ref)

    gain_grad_ref[...] += gain_grad


def ffn_back(line, pooled_grad, lengths, slope, middle, gain_ffn, w_up, w_down):
    total, width = middle.shape
    entries = pooled_grad.shape[0]
    slots = total // entries
    rows = math.gcd(total, 256)
    some = rows // slots
    ff = w_up.shape[1]
    return line.run(
        functools.partial(ffn_back_body, slots),
        "ffn_back",
        15,
        (total // rows,),
        [
            (pooled_grad, rows_of(some, width)),
            (lengths, rows_of(rows, 1)),
            (slope, rows_of(rows, ff)),
            (middle, rows_of(rows, width)),
            (gain_ffn, fixed(gain_ffn.shape)),
            (w_up, fixed(w_up.shape)),
            (w_down, fixed(w_down.shape)),
        ],
        [
            ((total, ff), BF16, rows_of(rows, ff)),
            ((total, width), F32, rows_of(rows, width)),
            ((total, width), BF16, rows_of(rows, width)),
            ((1, width), F32, fixed((1, width))),
        ],
    )


def heads_back_body(slots, lengths_ref, w_out_ref, mixed_ref, grad_branch_ref, grad_mixed_ref):
    rows, width = grad_branch_ref.shape
    lengths = lengths_ref[...]
    grad_ctx = nt(grad_branch_ref[...], w_out_ref[...]).astype(BF16)
    row = lax.broadcasted_iota(jnp.int32, (GROUP, GROUP), 0)
    col = lax.broadcasted_iota(jnp.int32, (GROUP, GROUP), 1)
    same = row // slots == col // slots
    lows = range(0, width, PAIR)
    for base in range(0, rows, GROUP):
        span = slice(base, base + GROUP)
        valid = same & (row % slots <= lengths[span])
        queries = [mixed_ref[span, low : low + PAIR] for low in lows]
        keys = [split_heads(mixed_ref[span, width + low : width + low + PAIR]) for low in lows]
        values = [split_heads(mixed_ref[span, 2 * width + low : 2 * width + low + PAIR]) for low in lows]
        grad_pairs = [grad_ctx[span, low : low + PAIR] for low in lows]
        raws = [nt(key, query) for key, query in zip(keys, queries)]
        grad_raws = [nt(value, grad_pair) for value, grad_pair in zip(values, grad_pairs)]
        sides = (slice(0, GROUP), slice(GROUP, 2 * GROUP))
        heads = [raw[side] for raw in raws for side in sides]
        heads = [jnp.where(valid, head * HEAD_DIM ** (-0.5), -1000000000.0) for head in heads]
        heads = [jnp.exp(head - jnp.max(head, axis=0, keepdims=True)) for head in heads]
        probs = [head * (1.0 / jnp.sum(head, axis=0, keepdims=True)) for head in heads]
        grads = [grad_raw[side] for grad_raw in grad_raws for side in sides]
        grads = [
            prob * (grad - jnp.sum(grad * prob, axis=0, keepdims=True)) for prob, grad in zip(probs, grads)
        ]
        probs = [prob.astype(BF16) for prob in probs]
        grads = [(grad * HEAD_DIM ** (-0.5)).astype(BF16) for grad in grads]
        for j, low in enumerate(lows):
            scores_grad = jnp.concatenate(grads[2 * j : 2 * j + 2], axis=0)
            prob = jnp.concatenate(probs[2 * j : 2 * j + 2], axis=0)
            grad_mixed_ref[span, low : low + PAIR] = tn(scores_grad, keys[j]).astype(BF16)
            grad_keys = join_heads(mm(scores_grad, queries[j]))
            grad_mixed_ref[span, width + low : width + low + PAIR] = grad_keys.astype(BF16)
            grad_values = join_heads(mm(prob, grad_pairs[j]))
            grad_mixed_ref[span, 2 * width + low : 2 * width + low + PAIR] = grad_values.astype(BF16)


def heads_back(line, lengths, w_out, mixed, grad_branch, slots):
    total, width = grad_branch.shape
    rows = math.gcd(total, 256)
    return line.run(
        functools.partial(heads_back_body, slots),
        "heads_back",
        13,
        (total // rows,),
        [
            (lengths, rows_of(rows, 1)),
            (w_out, fixed(w_out.shape)),
            (mixed, rows_of(rows, 3 * width)),
            (grad_branch, rows_of(rows, width)),
        ],
        [((total, 3 * width), BF16, rows_of(rows, 3 * width))],
    )[0]


def attn_back_body(
    pieces_ref,
    scripts_ref,
    script_table_ref,
    gain_attn_ref,
    w_qkv_ref,
    grad_mixed_ref,
    grad_middle_ref,
    grad_pieces_ref,
    gain_grad_ref,
    script_grad_ref,
):
    start, onehot = start_of(pieces_ref, scripts_ref, script_table_ref)
    grad_normed = nt(grad_mixed_ref[...], w_qkv_ref[...])
    unit, rate = center(start)
    grad, gain_grad = center_back(grad_normed, gain_attn_ref[...], unit, rate)
    grad_pieces = grad_middle_ref[...] + grad
    grad_pieces_ref[...] = grad_pieces.reshape(grad_pieces_ref.shape)

    @pl.when(pl.program_id(0) == 0)
    def _():
        gain_grad_ref[...] = jnp.zeros_like(gain_grad_ref)
        script_grad_ref[...] = jnp.zeros_like(script_grad_ref)

    gain_grad_ref[...] += gain_grad
    script_grad_ref[...] += lax.dot_general(
        onehot, grad_pieces, (((0,), (0,)), ((), ())), precision=highest
    )


def attn_back(
    line, pieces, scripts, script_table, gain_attn, w_qkv, grad_mixed, grad_middle
):
    entries, slots, width = pieces.shape
    total = entries * slots
    rows = math.gcd(total, 256)
    some = rows // slots
    return line.run(
        attn_back_body,
        "attn_back",
        9,
        (total // rows,),
        [
            (pieces, pl.BlockSpec((some, slots, width), lambda i, *_: (i, 0, 0))),
            (scripts, rows_of(rows, 1)),
            (script_table, fixed(script_table.shape)),
            (gain_attn, fixed(gain_attn.shape)),
            (w_qkv, fixed(w_qkv.shape)),
            (grad_mixed, rows_of(rows, 3 * width)),
            (grad_middle, rows_of(rows, width)),
        ],
        [
            ((entries, slots, width), F32, pl.BlockSpec((some, slots, width), lambda i, *_: (i, 0, 0))),
            ((1, width), F32, fixed((1, width))),
            (script_table.shape, F32, fixed(script_table.shape)),
        ],
    )


def per_device(
    pieces,
    lengths,
    scripts,
    script_table,
    gain_attn,
    gain_ffn,
    w_qkv,
    w_out,
    w_up,
    w_down,
    w_proj,
    token_ids,
    out_grad,
):
    entries, slots, width = pieces.shape
    ent_count = lax.axis_size("ent")
    rep_count = lax.axis_size("rep")
    devices = ent_count * rep_count
    features = w_proj.shape[1]
    vocab = entries * devices
    rows_dev, text_len = token_ids.shape
    tokens = rows_dev * text_len
    levels = make_levels(ent_count, rep_count)
    sizes = tuple(size for _, size, _ in levels)
    me = lax.axis_index("ent") * rep_count + lax.axis_index("rep")
    chunks = 1 if devices <= 32 else 8
    each = entries // chunks
    span = vocab // chunks
    slot = slot_of(token_ids // entries ^ me, levels)
    within = token_ids % entries
    slot_ids = within // each * span + slot * each + within % each
    script_rows = jnp.repeat(scripts, slots)[:, None]
    length_rows = jnp.repeat(lengths, slots)[:, None]
    gain_attn, gain_ffn = gain_attn[None], gain_ffn[None]

    cut = len(levels)
    while math.prod(sizes[:cut]) * 16 > w_down.shape[0]:
        cut -= 1
    near, far = levels[:cut], levels[cut:]
    count = math.prod(sizes[:cut])
    slot_index = jnp.arange(count, dtype=jnp.int32) ^ slot_of(me, near)
    line = Line()

    def cut_up(keep, send, some):
        shape = tuple(size for _, size, _ in some[1:]) + keep.shape[-2:]
        return keep.reshape(shape), send.reshape(shape)

    flat_ids = slot_ids.reshape(1, tokens)
    flat_grad = out_grad
    parts, pooled_grads = [], []
    for chunk in range(chunks):
        first = chunk * span
        part_send, send, *flat = scatter_rows(
            line, flat_ids, flat_grad, w_proj, first + span // 2, span // 2, BF16
        )
        flat_grad = flat[0] if flat else flat_grad
        part_keep, keep = scatter_rows(line, flat_ids, flat_grad, w_proj, first, span // 2, F32)
        parts.append((part_keep, part_send))
        shape = sizes[1:] + (each, width)
        pooling = sum_halves(line, keep.reshape(shape), send.reshape(shape), levels, pooled_grads)
        if chunks > 1:
            for _ in pooling:
                pass
    next(pooling, None)
    next(pooling, None)
    normed, mixed, context, middle, normed_ffn = attn_forward(
        line, pieces, script_rows, length_rows, script_table, gain_attn, gain_ffn, w_qkv, w_out
    )
    next(pooling, None)
    slope, hidden, pooled = ffn_forward(
        line, length_rows, lengths[:, None], middle, normed_ffn, w_up, w_down
    )
    gathered = [
        lax.all_gather(pooled[chunk * each :][:each], ("ent", "rep"), axis=0, tiled=True)
        for chunk in range(chunks)
    ]
    for _ in pooling:
        pass
    grad_pooled = jnp.concatenate(pooled_grads, axis=0) if chunks > 1 else pooled_grads[0]

    down = tall_weight(line, slot_index, hidden, grad_pooled.astype(BF16))
    grad_up, grad_middle, grad_branch, part_gain_ffn = ffn_back(
        line, grad_pooled, length_rows, slope, middle, gain_ffn, w_up, w_down
    )
    up = wide_weight(line, slot_index, normed_ffn, grad_up)
    ffn_all, two_all = [], []
    ffn_sum = all_sum_two(line, *cut_up(*down, near), *cut_up(*up, near), near, far, ffn_all)
    next(ffn_sum)
    grad_mixed = heads_back(line, length_rows, w_out, mixed, grad_branch, slots)
    next(ffn_sum)
    two = two_weights(line, slot_index, normed, grad_mixed, context, grad_branch)
    two_sum = all_sum(line, *cut_up(*two, near), near, far, two_all)
    next(two_sum)
    next(ffn_sum)
    grad_pieces, part_gain_attn, part_script = attn_back(
        line, pieces, script_rows, script_table, gain_attn, w_qkv, grad_mixed, grad_middle
    )
    small = lax.all_gather(
        jnp.concatenate([part_script, part_gain_attn, part_gain_ffn], axis=0), ("ent", "rep"), axis=0
    )
    small = jnp.sum(small, axis=0)
    next(ffn_sum)
    next(two_sum)
    numbers = np.argsort(slot_of(np.arange(devices), levels)).astype(np.int32)
    owners = jnp.asarray(numbers) ^ me
    tables, part_proj = [], None
    for chunk in range(chunks):
        table, part = table_and_grad(line, owners, gathered[chunk], w_proj, *parts[chunk])
        tables.append(table)
        part_proj = part if part_proj is None else part_proj + part
    grad_w_proj = part_proj + swap(part_proj, levels[0])
    next(ffn_sum)
    next(two_sum)
    looked_up = lookup(line, slot_ids, tables, 0)
    next(ffn_sum)
    next(two_sum)
    looked_up = lookup(line, slot_ids, tables, 1, looked_up)
    going = [ffn_sum, two_sum]
    while going:
        going = [steps for steps in going if next(steps, 0) is None]
    grad_w_down = unpack(line, slot_index, merge(ffn_all[0]), merge(ffn_all[1]), *w_down.shape)
    grad_w_up = unpack(line, slot_index, merge(ffn_all[2]), merge(ffn_all[3]), *w_up.shape)
    grad_w_qkv, grad_w_out = unpack_two(line, slot_index, *map(merge, two_all), *w_qkv.shape)
    groups = script_table.shape[0]
    return (
        looked_up,
        grad_pieces,
        small[:groups],
        small[groups],
        small[groups + 1],
        grad_w_qkv,
        grad_w_out,
        grad_w_up,
        grad_w_down,
        grad_w_proj,
    )


def solution(mesh):
    in_specs = (
        P(("ent", "rep"), None, None),
        P(("ent", "rep")),
        P(("ent", "rep")),
        P(),
        P(),
        P(),
        P(),
        P(),
        P(),
        P(),
        P(None, "ent"),
        P("rep", None),
        P("ent", "rep", None),
    )
    out_specs = (
        P("ent", "rep", None),
        P(("ent", "rep"), None, None),
        P(),
        P(),
        P(),
        P(),
        P(),
        P(),
        P(),
        P(None, "ent"),
    )
    return jax.shard_map(
        per_device, mesh=mesh, in_specs=in_specs, out_specs=out_specs, check_vma=False
    )
```

```python
import functools
import math

import jax
import jax.numpy as jnp
import numpy as np
from jax import lax
from jax.experimental import pallas as pl
from jax.experimental.pallas import tpu as pltpu
from jax.sharding import PartitionSpec as P

HEADS = 8
HEAD_DIM = 64
F32 = jnp.float32
BF16 = jnp.bfloat16
highest = lax.Precision.HIGHEST
MIB = 1024 * 1024


def make_levels(ent_count, rep_count):
    levels = [("rep", rep_count, 0)]
    bit, total = 0, ent_count.bit_length() - 1
    while bit < total:
        width = 1 if bit < 2 else min(2, total - bit)
        levels.append(("ent", 1 << width, bit))
        bit += width
    return levels


def slot_of(number, levels):
    rep_count = levels[0][1]
    slot = number % rep_count
    ent = number // rep_count
    for _, size, shift in levels[1:]:
        slot = slot * size + (ent >> shift) % size
    return slot


def swap(value, level, k):
    name, size, shift = level
    count = lax.axis_size(name)
    return lax.ppermute(value, name, [(i, i ^ (k << shift)) for i in range(count)])


def merge(value):
    return value.reshape((-1,) + value.shape[-2:])


FAR = True


class Line:
    def __init__(self):
        self.last = []

    def run(self, body, name, micros, grid, ins, outs, prefetch=(), alias=None, room=32 * MIB):
        count = len(prefetch) + len(ins)
        extra = self.last + ([] if alias is None else [alias])
        token = (8, 128)

        def wrapped(*refs):
            refs[-1][...] = jnp.zeros(token, F32)
            body(*refs[:count], *refs[count + len(extra) : -1])

        *results, last = pl.pallas_call(
            wrapped,
            grid_spec=pltpu.PrefetchScalarGridSpec(
                num_scalar_prefetch=len(prefetch),
                grid=grid,
                in_specs=[spec for _, spec in ins] + [pl.BlockSpec(memory_space=pl.ANY)] * len(extra),
                out_specs=[spec for _, _, spec, *_ in outs] + [pl.BlockSpec(token, lambda *_: (0, 0))],
            ),
            out_shape=[
                pltpu.HBM(shape, dtype) if far else jax.ShapeDtypeStruct(shape, dtype)
                for shape, dtype, _, *far in outs
            ]
            + [jax.ShapeDtypeStruct(token, F32)],
            input_output_aliases={} if alias is None else {count + len(extra) - 1: 0},
            compiler_params=pltpu.CompilerParams(vmem_limit_bytes=room),
            cost_estimate=pl.CostEstimate(
                flops=int(micros * 3e9), bytes_accessed=int(micros * 9e6), transcendentals=0
            ),
            name=name,
        )(*prefetch, *(value for value, _ in ins), *extra)
        self.last = [last]
        return results


def swap(value, level, k=1):
    name, size, shift = level
    count = lax.axis_size(name)
    return lax.ppermute(value, name, [(i, i ^ (k << shift)) for i in range(count)])


def swaps(values, level):
    return [swap(value, level, k) for k, value in enumerate(values, 1)]


def stage_body(layout, cuts, *refs):
    sums, position = [], 0
    for number in layout:
        sums.append(refs[position : position + number])
        position += number

    def piece(number, index, cols):
        total = sums[number][0][index][:, cols]
        for ref in sums[number][1:]:
            total = total.astype(F32) + ref[index][:, cols].astype(F32)
        return total

    for out_ref, sources in zip(refs[position:], cuts):
        for target, parts in sources:
            for number, index, cols, row, col in parts:
                value = piece(number, index, cols).astype(out_ref.dtype)
                where = target + (slice(row, row + value.shape[0]), slice(col, col + value.shape[1]))
                out_ref[where] = value


def stage(line, sums, outs, steps=1):
    values = [value for kept, received in sums for value in [kept, *received]]

    def spec(shape):
        return pl.BlockSpec(memory_space=pltpu.VMEM)

    cuts = [
        [(target, source(target)) for target in np.ndindex(*lead)] for lead, _, _, _, source in outs
    ]
    shapes = [(lead + (rows, cols), dtype) for lead, rows, cols, dtype, _ in outs]
    held = [(value.shape, value.dtype) for value in values] + [(shape, jnp.dtype(dtype)) for shape, dtype in shapes]
    return line.run(
        functools.partial(stage_body, [1 + len(received) for _, received in sums], cuts),
        "exchange",
        0.5,
        (),
        [(value, spec(value.shape)) for value in values],
        [(shape, dtype, spec(shape)) for shape, dtype in shapes],
        room=2 * MIB + sum(math.prod(shape) * dtype.itemsize for shape, dtype in held),
    )


ALL = slice(None)


def split(number, value, axis, cols=ALL, width=None):
    lead = value.shape[:-2]
    rest = lead[:axis] + lead[axis + 1 :]
    outs = []
    for k in range(lead[axis]):

        def source(index, k=k):
            return [(number, index[:axis] + (k,) + index[axis:], cols, 0, 0)]

        outs.append((rest, value.shape[-2], width or value.shape[-1], F32 if k == 0 else BF16, source))
    return outs


def stacked(numbers, value, axis, rows=ALL):
    lead = value.shape[:-2]
    shape = lead[:axis] + (len(numbers),) + lead[axis:]

    def source(index):
        return [(numbers[index[axis]], index[:axis] + index[axis + 1 :], ALL, 0, 0)]

    return (shape, value.shape[-2], value.shape[-1], value.dtype, source)


def sum_halves(line, keep, send, levels, out):
    received = swap(send, levels[0])
    yield
    rows, width = keep.shape[-2:]
    half = width // 2
    left, right = slice(0, half), slice(half, width)
    steps = 4 if rows % 64 == 0 else 1
    outs = split(0, keep, 0, left, half) + split(0, keep, 1, right, half)
    keep_a, send_a, keep_b, send_b = stage(line, [(keep, [received])], outs, steps)
    got_a, got_b = swap(send_a, levels[1]), swap(send_b, levels[2])
    yield
    outs = split(0, keep_a, 0) + split(1, keep_b, 0)
    sums = [(keep_a, [got_a]), (keep_b, [got_b])]
    keep_a, send_a, keep_b, send_b = stage(line, sums, outs, steps)
    sums = [(keep_a, [swap(send_a, levels[2])]), (keep_b, [swap(send_b, levels[1])])]
    yield
    for place, level in enumerate(levels[3:]):
        if place == 0:
            lead = keep_a.shape[1:-2]

            def source(index, k):
                return [(0, (k,) + index, ALL, 0, 0), (1, (k,) + index, ALL, 0, half)]

            outs = [
                (lead, rows, width, F32 if k == 0 else BF16, functools.partial(source, k=k))
                for k in range(level[1])
            ]
        else:
            outs = split(0, keep, 0)
        keep, *sends = stage(line, sums, outs)
        sums = [(keep, swaps(sends, level))]
        yield
    out += stage(line, sums, [((), rows, width, F32, lambda index: [(0, (), ALL, 0, 0)])])
    yield


def gather_halves(line, value, levels, out):
    rows, width = value.shape
    half = width // 2
    for place, level in reversed(list(enumerate(levels[3:]))):
        got = [swap(value, level, k) for k in range(1, level[1])]
        yield
        parts = [(part, []) for part in [value, *got]]
        numbers = list(range(level[1]))
        if place:
            value = stage(line, parts, [stacked(numbers, value, 0)])[0]
        else:
            lead = (level[1],) + value.shape[:-2]

            def source(index, cols):
                return [(index[0], index[1:], cols, 0, 0)]

            outs = [
                (lead, rows, half, BF16, functools.partial(source, cols=cols))
                for cols in (slice(0, half), slice(half, width))
            ]
            value_a, value_b = stage(line, parts, outs)
    got_a, got_b = swap(value_a, levels[2]), swap(value_b, levels[1])
    yield
    sums = [(part, []) for part in (value_a, got_a, value_b, got_b)]
    outs = [stacked([0, 1], value_a, 0), stacked([2, 3], value_b, 0)]
    value_a, value_b = stage(line, sums, outs)
    got_a, got_b = swap(value_a, levels[1]), swap(value_b, levels[2])
    yield
    sums = [(part, []) for part in (value_a, got_a, value_b, got_b)]
    lead = (2,) + value_a.shape[:-2]

    def joined(index):
        left, right = index[0], index[1]
        return [(left, index[1:], ALL, 0, 0), (2 + right, (left,) + index[2:], ALL, 0, half)]

    value = stage(line, sums, [(lead, rows, width, BF16, joined)])[0]
    out += [value, swap(value, levels[0])]
    yield


def finish(line, sums, far, rows):
    for level in far:
        outs = [((), rows, PANEL, dtype, lambda index: [(0, (), ALL, 0, 0)]) for dtype in (F32, BF16)]
        keep, send = stage(line, sums, outs)
        sums = [(keep, [swap(send, level, k) for k in range(1, level[1])])]
        yield
    yield stage(line, sums, [((), rows, PANEL, BF16, lambda index: [(0, (), ALL, 0, 0)])])[0]


def all_sum(line, keep, send, near, far, out):
    received = swap(send, near[0])
    yield
    rows = keep.shape[-2]
    sums = [(keep, [received])]
    for level in near[1:]:
        keep, *sends = stage(line, sums, split(0, keep, 0))
        sums = [(keep, swaps(sends, level))]
        yield
    for value in finish(line, sums, far, rows):
        if value is None:
            yield
    yield from gather_halves(line, value, near, out)


def all_sum_two(line, keep_a, send_a, keep_b, send_b, near, far, out):
    got_a, got_b = swap(send_a, near[0]), swap(send_b, near[0])
    yield
    rows = keep_a.shape[-2]
    outs = split(0, keep_a, 0) + split(1, keep_b, 1)
    keep_a, send_a, keep_b, send_b = stage(line, [(keep_a, [got_a]), (keep_b, [got_b])], outs)
    got_a, got_b = swap(send_a, near[1]), swap(send_b, near[2])
    yield
    outs = split(0, keep_a, 0) + split(1, keep_b, 0)
    keep_a, send_a, keep_b, send_b = stage(line, [(keep_a, [got_a]), (keep_b, [got_b])], outs)
    sums = [(keep_a, [swap(send_a, near[2])]), (keep_b, [swap(send_b, near[1])])]
    yield
    for place, level in enumerate(near[3:]):
        if place == 0:
            lead = keep_a.shape[1:-2]

            def source(index, k):
                return [(0, (k,) + index, ALL, 0, 0), (1, (k,) + index, ALL, rows, 0)]

            outs = [
                (lead, 2 * rows, PANEL, F32 if k == 0 else BF16, functools.partial(source, k=k))
                for k in range(level[1])
            ]
        else:
            outs = split(0, keep, 0)
        keep, *sends = stage(line, sums, outs)
        sums = [(keep, swaps(sends, level))]
        yield
    for value in finish(line, sums, far, 2 * rows):
        if value is None:
            yield
    for place, level in reversed(list(enumerate(near[3:]))):
        got = [swap(value, level, k) for k in range(1, level[1])]
        yield
        numbers = list(range(level[1]))
        value = stage(line, [(part, []) for part in [value, *got]], [stacked(numbers, value, 0)])[0]
    value_a, value_b = value[..., :rows, :], value[..., rows:, :]
    got_a, got_b = swap(value_a, near[2]), swap(value_b, near[1])
    yield
    sums = [(part, []) for part in (value_a, got_a, value_b, got_b)]
    outs = [stacked([0, 1], value_a, 0), stacked([2, 3], value_b, 0)]
    value_a, value_b = stage(line, sums, outs)
    got_a, got_b = swap(value_a, near[1]), swap(value_b, near[2])
    yield
    sums = [(part, []) for part in (value_a, got_a, value_b, got_b)]
    outs = [stacked([0, 1], value_a, 0), stacked([2, 3], value_b, 1)]
    value_a, value_b = stage(line, sums, outs)
    out += [value_a, swap(value_a, near[0]), value_b, swap(value_b, near[0])]
    yield


def fixed(shape):
    return pl.BlockSpec(shape, lambda i, *_: (0,) * len(shape))


def rows_of(rows, width):
    return pl.BlockSpec((rows, width), lambda i, *_: (i, 0))


def selector(ids, base, rows):
    entry = lax.broadcasted_iota(jnp.int32, (rows, 1), 0).astype(jnp.int16)
    return jnp.where(entry == (ids - base).astype(jnp.int16), jnp.ones((), BF16), jnp.zeros((), BF16))


def nt(left, right):
    return lax.dot_general(left, right, (((1,), (1,)), ((), ())), preferred_element_type=F32)


def tn(left, right):
    return lax.dot_general(left, right, (((0,), (0,)), ((), ())), preferred_element_type=F32)


def mm(left, right):
    return jnp.dot(left, right, preferred_element_type=F32)


def scatter_some(first, ids_ref, grad, proj_ref, table_ref, pooled_ref):
    rows = table_ref.shape[0]
    base = first + pl.program_id(0) * rows
    picks = [selector(ids_ref[row : row + 1], base, rows) for row in range(ids_ref.shape[0])]
    part = nt(jnp.concatenate(picks, axis=1), grad).astype(BF16)
    table_ref[...] = part
    pooled_ref[...] = nt(part, proj_ref[...]).astype(pooled_ref.dtype)


def scatter_first_body(first, ids_ref, grad_ref, proj_ref, table_ref, pooled_ref, flat_ref):
    @pl.when(pl.program_id(0) == 0)
    def _():
        flat_ref[...] = grad_ref[...].reshape(flat_ref.shape)

    scatter_some(first, ids_ref, flat_ref[...], proj_ref, table_ref, pooled_ref)


def scatter_body(first, ids_ref, flat_ref, proj_ref, table_ref, pooled_ref):
    scatter_some(first, ids_ref, flat_ref[...], proj_ref, table_ref, pooled_ref)


def scatter_rows(line, ids, grad, w_proj, first, count, dtype):
    features = grad.shape[0]
    tokens = ids.size
    width = w_proj.shape[0]
    rows = min(512, count)
    flat = (features, tokens)
    fresh = grad.ndim == 3
    return line.run(
        functools.partial(scatter_first_body if fresh else scatter_body, first),
        "scatter_rows",
        14,
        (count // rows,),
        [(ids, fixed(ids.shape)), (grad, pl.BlockSpec(memory_space=pltpu.VMEM)), (w_proj, fixed(w_proj.shape))],
        [
            ((count, features), BF16, rows_of(rows, features), FAR),
            ((count, width), dtype, rows_of(rows, width)),
        ]
        + ([(flat, BF16, pl.BlockSpec(memory_space=pltpu.VMEM))] if fresh else []),
        room=44 * MIB,
    )


def table_body(steps, own_ref, other_ref, proj_ref, part_own_ref, part_other_ref, table_ref, grad_ref):
    step = pl.program_id(0)

    @pl.when(step == 0)
    def _():
        grad_ref[...] = jnp.zeros_like(grad_ref)

    def one(pooled_ref, part_ref):
        pooled = pooled_ref[...]
        cols = lax.dot_general(
            proj_ref[...], pooled, (((0,), (1,)), ((), ())), preferred_element_type=F32
        )
        table_ref[...] = cols.astype(BF16)
        grad_ref[...] += tn(pooled, part_ref[...])

    @pl.when(step < steps)
    def _():
        one(own_ref, part_own_ref)

    @pl.when(step >= steps)
    def _():
        one(other_ref, part_other_ref)


def table_and_grad(line, own, other, w_proj, part_own, part_other):
    count, width = own.shape
    features = w_proj.shape[1]
    rows = min(1024, count)
    steps = count // rows

    def first(cols):
        return pl.BlockSpec((rows, cols), lambda i, *_: (jnp.minimum(i, steps - 1), 0))

    def second(cols):
        return pl.BlockSpec((rows, cols), lambda i, *_: (jnp.maximum(i - steps, 0), 0))

    return line.run(
        functools.partial(table_body, steps),
        "table_and_grad",
        5,
        (2 * steps,),
        [
            (own, first(width)),
            (other, second(width)),
            (w_proj, fixed(w_proj.shape)),
            (part_own, first(features)),
            (part_other, second(features)),
        ],
        [
            ((features, 2 * count), BF16, pl.BlockSpec((features, rows), lambda i, *_: (0, i))),
            ((width, features), F32, fixed((width, features))),
        ],
    )


def lookup_body(chunk, ids_ref, *refs):
    table_refs, out_ref = refs[:-1], refs[-1]
    rows = ids_ref.shape[0]

    def find(base, table):
        picks = [selector(ids_ref[row : row + 1], base, chunk) for row in range(rows)]
        return mm(table, jnp.concatenate(picks, axis=1))

    total = None
    for index, table_ref in enumerate(table_refs):
        vocab = table_ref.shape[1]
        for inner in range(0, vocab, chunk):
            part = find(index * vocab + inner, table_ref[:, inner : inner + chunk])
            total = part if total is None else total + part
    out_ref[...] = total.astype(BF16).reshape(out_ref.shape)


def lookup(line, ids, tables, part, count, before=None):
    rows, text_len = ids.shape
    features, vocab = tables[0].shape
    block = math.gcd(text_len // count, 256)
    steps = text_len // count // block
    return line.run(
        functools.partial(lookup_body, min(vocab, 4096)),
        "lookup",
        6,
        (steps,),
        [(ids, pl.BlockSpec((rows, block), lambda i, *_: (0, i + part * steps)))]
        + [(table, fixed(table.shape)) for table in tables],
        [
            (
                (features, rows, text_len),
                BF16,
                pl.BlockSpec((features, rows, block), lambda i, *_: (0, 0, i + part * steps)),
                FAR,
            )
        ],
        alias=before,
    )[0]


PANEL = 512
EXTRA = 16


def store_slots(slots_ref, first, part, keep_ref, send_ref, rows=None, base=0):
    rows = rows or keep_ref.shape[1]
    half = keep_ref.shape[0]
    where = slice(base, base + rows)
    for j in range(part.shape[0] // rows):
        slot = slots_ref[first + j]
        piece = part[j * rows : (j + 1) * rows]

        @pl.when(slot < half)
        def _():
            keep_ref[slot, where] = piece

        @pl.when(slot >= half)
        def _():
            send_ref[slot - half, where] = piece.astype(BF16)


def weight_body(slots_ref, left_ref, right_ref, keep_ref, send_ref):
    part = tn(left_ref[...], right_ref[...])
    store_slots(slots_ref, pl.program_id(0) * (part.shape[0] // keep_ref.shape[1]), part, keep_ref, send_ref)


def tall_body(steps, slots_ref, first_ref, second_ref, right_ref, keep_ref, send_ref):
    step = pl.program_id(0)
    each = PANEL // keep_ref.shape[1]

    @pl.when(step < steps)
    def _():
        store_slots(slots_ref, step * each, tn(first_ref[...], right_ref[...]), keep_ref, send_ref)

    @pl.when(step >= steps)
    def _():
        store_slots(slots_ref, step * each, tn(second_ref[...], right_ref[...]), keep_ref, send_ref)


def two_weights_body(
    last, slots_ref, left_ref, right_ref, left2_ref, right2_ref, small_ref, keep_ref, send_ref
):
    step = pl.program_id(0)
    rows = keep_ref.shape[1] - EXTRA
    each = left_ref.shape[1] // rows

    @pl.when(step < last)
    def _():
        store_slots(slots_ref, step * each, tn(left_ref[...], right_ref[...]), keep_ref, send_ref, rows)

    @pl.when(step == last)
    def _():
        part = tn(left2_ref[...], right2_ref[...])
        store_slots(slots_ref, step * each, part, keep_ref, send_ref, rows)
        top = lax.broadcasted_iota(jnp.int32, (EXTRA, 1), 0) == 0
        for chunk in range(2 * keep_ref.shape[0]):
            piece = jnp.zeros((EXTRA, PANEL), F32)
            if chunk < small_ref.shape[0]:
                piece = jnp.where(top, small_ref[chunk : chunk + 1], 0.0)
            store_slots(slots_ref, chunk, piece, keep_ref, send_ref, EXTRA, rows)


def slot_outs(count, rows):
    shape = (count // 2, rows, PANEL)
    return [(shape, F32, fixed(shape)), (shape, BF16, fixed(shape))]


def panel_of(depth):
    return pl.BlockSpec((depth, PANEL), lambda i, *_: (0, i))


def tall_weight(line, slots, lefts, right):
    depth, half = lefts[0].shape
    steps = half // PANEL
    return line.run(
        functools.partial(tall_body, steps),
        "tall_weight",
        3,
        (2 * steps,),
        [
            (lefts[0], pl.BlockSpec((depth, PANEL), lambda i, *_: (0, jnp.minimum(i, steps - 1)))),
            (lefts[1], pl.BlockSpec((depth, PANEL), lambda i, *_: (0, jnp.maximum(i - steps, 0)))),
            (right, fixed(right.shape)),
        ],
        slot_outs(slots.shape[0], 2 * half // slots.shape[0]),
        [slots],
    )


def wide_weight(line, slots, left, right):
    depth, cols = right.shape
    return line.run(
        weight_body,
        "wide_weight",
        8,
        (cols // PANEL,),
        [(left, fixed(left.shape)), (right, panel_of(depth))],
        slot_outs(slots.shape[0], cols // PANEL * left.shape[1] // slots.shape[0]),
        [slots],
    )


def two_weights(line, slots, left, right, left2, right2, small):
    depth, cols = right.shape
    last = cols // PANEL
    return line.run(
        functools.partial(two_weights_body, last),
        "two_weights",
        5,
        (last + 1,),
        [
            (left, fixed(left.shape)),
            (right, pl.BlockSpec((depth, PANEL), lambda i, *_: (0, jnp.minimum(i, last - 1)))),
            (left2, fixed(left2.shape)),
            (right2, fixed(right2.shape)),
            (small, fixed(small.shape)),
        ],
        slot_outs(slots.shape[0], (last + 1) * left.shape[1] // slots.shape[0] + EXTRA),
        [slots],
    )


def load_slots(slots_ref, first, own_ref, other_ref, out_ref, rows):
    half = own_ref.shape[0]
    for j in range(out_ref.shape[0] // rows):
        slot = slots_ref[first + j]

        @pl.when(slot < half)
        def _():
            out_ref[j * rows : (j + 1) * rows] = own_ref[slot, :rows].astype(F32)

        @pl.when(slot >= half)
        def _():
            out_ref[j * rows : (j + 1) * rows] = other_ref[slot - half, :rows].astype(F32)


def unpack_body(slots_ref, own_ref, other_ref, out_ref):
    rows = own_ref.shape[1]
    each = out_ref.shape[0] // rows
    load_slots(slots_ref, pl.program_id(0) * each, own_ref, other_ref, out_ref, rows)


def unpack_two_body(last, slots_ref, own_ref, other_ref, out_ref, out2_ref, small_ref):
    step = pl.program_id(0)
    half, rows, _ = own_ref.shape
    rows -= EXTRA
    each = out_ref.shape[0] // rows

    @pl.when(step < last)
    def _():
        load_slots(slots_ref, step * each, own_ref, other_ref, out_ref, rows)

    @pl.when(step == last)
    def _():
        load_slots(slots_ref, step * each, own_ref, other_ref, out2_ref, rows)
        for chunk in range(small_ref.shape[0]):
            slot = slots_ref[chunk]

            @pl.when(slot < half)
            def _():
                small_ref[chunk : chunk + 1] = own_ref[slot, rows:].astype(F32)[:1]

            @pl.when(slot >= half)
            def _():
                small_ref[chunk : chunk + 1] = other_ref[slot - half, rows:].astype(F32)[:1]


def unpack(line, slots, own, other, height, cols):
    tall = cols == PANEL
    tile = 512
    index = (lambda i, *_: (i, 0)) if tall else (lambda i, *_: (0, i))
    return line.run(
        unpack_body,
        "unpack",
        5,
        (height * cols // (tile * PANEL),),
        [(own, fixed(own.shape)), (other, fixed(other.shape))],
        [((height, cols), F32, pl.BlockSpec((tile if tall else height, PANEL), index), FAR)],
        [slots],
    )[0]


def unpack_two(line, slots, own, other, height, cols, small):
    last = cols // PANEL
    return line.run(
        functools.partial(unpack_two_body, last),
        "unpack_two",
        5,
        (last + 1,),
        [(own, fixed(own.shape)), (other, fixed(other.shape))],
        [
            (
                (height, cols),
                F32,
                pl.BlockSpec((height, PANEL), lambda i, *_: (0, jnp.minimum(i, last - 1))),
                FAR,
            ),
            ((height, PANEL), F32, fixed((height, PANEL)), FAR),
            (small, F32, fixed(small)),
        ],
        [slots],
    )


GROUP = 128
PAIR = 2 * HEAD_DIM
GELU_SCALE = 0.7978845608028654
GELU_CUBE = 0.044715


def center(values):
    centered = values - jnp.mean(values, axis=-1, keepdims=True)
    spread = jnp.mean(centered * centered, axis=-1, keepdims=True)
    rate = lax.rsqrt(spread + 1e-05)
    return centered * rate, rate


def center_back(grad, gain, unit, rate):
    gain_grad = jnp.sum(grad * unit, axis=0, keepdims=True)
    grad = grad * gain
    mean_grad = jnp.mean(grad, axis=-1, keepdims=True)
    mean_unit = jnp.mean(grad * unit, axis=-1, keepdims=True)
    return rate * (grad - mean_grad - unit * mean_unit), gain_grad


def start_of(pieces_ref, scripts_ref, script_table_ref):
    entries, slots, width = pieces_ref.shape
    groups = script_table_ref.shape[0]
    pieces = pieces_ref[...].astype(F32).reshape(entries * slots, width)
    onehot = (scripts_ref[...] == lax.broadcasted_iota(jnp.int32, (1, groups), 1)).astype(F32)
    return pieces + jnp.dot(onehot, script_table_ref[...], precision=highest), onehot


def slot_weights(lengths, slots):
    rows = lengths.shape[0]
    slot = lax.broadcasted_iota(jnp.int32, (rows, 1), 0) % slots
    return jnp.where(slot <= lengths, 1.0 / (lengths + 1).astype(F32), 0.0)


def split_heads(pair):
    first = lax.broadcasted_iota(jnp.int32, pair.shape, 1) < HEAD_DIM
    zero = jnp.zeros_like(pair)
    return jnp.concatenate([jnp.where(first, pair, zero), jnp.where(first, zero, pair)], axis=0)


def join_heads(stacked):
    first = lax.broadcasted_iota(jnp.int32, (GROUP, PAIR), 1) < HEAD_DIM
    return jnp.where(first, stacked[:GROUP], stacked[GROUP:])


def attn_body(
    slots,
    pieces_ref,
    scripts_ref,
    lengths_ref,
    script_table_ref,
    gain_attn_ref,
    gain_ffn_ref,
    w_qkv_ref,
    w_out_ref,
    normed_ref,
    mixed_ref,
    context_ref,
    middle_ref,
    normed_ffn_ref,
):
    start, _ = start_of(pieces_ref, scripts_ref, script_table_ref)
    rows, width = start.shape
    lengths = lengths_ref[...]
    normed = (center(start)[0] * gain_attn_ref[...]).astype(BF16)
    normed_ref[...] = normed
    mixed = mm(normed, w_qkv_ref[...]).astype(BF16)
    mixed_ref[...] = mixed
    row = lax.broadcasted_iota(jnp.int32, (GROUP, GROUP), 0)
    col = lax.broadcasted_iota(jnp.int32, (GROUP, GROUP), 1)
    groups = []
    for base in range(0, rows, GROUP):
        part = mixed[base : base + GROUP]
        valid = (row // slots == col // slots) & (col % slots <= lengths[base : base + GROUP])
        lows = range(0, width, PAIR)
        raws = [
            nt(part[:, low : low + PAIR], split_heads(part[:, width + low : width + low + PAIR]))
            for low in lows
        ]
        heads = [raw[:, side : side + GROUP] for raw in raws for side in (0, GROUP)]
        heads = [jnp.where(valid, head * HEAD_DIM ** (-0.5), -1000000000.0) for head in heads]
        heads = [jnp.exp(head - jnp.max(head, axis=1, keepdims=True)) for head in heads]
        heads = [(head * (1.0 / jnp.sum(head, axis=1, keepdims=True))).astype(BF16) for head in heads]
        pairs = [
            mm(
                jnp.concatenate(heads[2 * j : 2 * j + 2], axis=1),
                split_heads(part[:, 2 * width + low : 2 * width + low + PAIR]),
            )
            for j, low in enumerate(lows)
        ]
        groups.append(jnp.concatenate(pairs, axis=1).astype(BF16))
    context = jnp.concatenate(groups, axis=0)
    context_ref[...] = context
    middle = start + mm(context, w_out_ref[...])
    middle_ref[...] = middle
    normed_ffn_ref[...] = (center(middle)[0] * gain_ffn_ref[...]).astype(BF16)


def attn_forward(
    line, pieces, scripts, lengths, script_table, gain_attn, gain_ffn, w_qkv, w_out
):
    entries, slots, width = pieces.shape
    total = entries * slots
    rows = math.gcd(total, 256)
    some = rows // slots
    whole = (script_table, gain_attn, gain_ffn, w_qkv, w_out)
    return line.run(
        functools.partial(attn_body, slots),
        "attn_forward",
        12,
        (total // rows,),
        [
            (pieces, pl.BlockSpec((some, slots, width), lambda i, *_: (i, 0, 0))),
            (scripts, rows_of(rows, 1)),
            (lengths, rows_of(rows, 1)),
        ]
        + [(value, fixed(value.shape)) for value in whole],
        [
            ((total, width), BF16, rows_of(rows, width)),
            ((total, 3 * width), BF16, rows_of(rows, 3 * width), FAR),
            ((total, width), BF16, rows_of(rows, width)),
            ((total, width), F32, rows_of(rows, width)),
            ((total, width), BF16, rows_of(rows, width)),
        ],
    )


def ffn_body(
    slots,
    last,
    length_rows_ref,
    lengths_ref,
    before_ref,
    normed_ref,
    w_up_ref,
    w_down_ref,
    slope_ref,
    hidden_ref,
    pooled_ref,
):
    rows, width = normed_ref.shape
    some = rows // slots
    row = lax.broadcasted_iota(jnp.int32, (some, rows), 1)
    entry = lax.broadcasted_iota(jnp.int32, (some, rows), 0)
    lengths = lengths_ref[...]
    valid = (row // slots == entry) & (row % slots <= lengths)
    valid = jnp.where(valid, 1.0, 0.0).astype(BF16)
    scale = 1.0 / (lengths + 1).astype(F32)
    pooled = before_ref[...]
    if not last:
        weights = slot_weights(length_rows_ref[...], slots)
        pooled = jnp.sum((pooled * weights).reshape(some, slots, width), axis=1)
    ff = w_up_ref.shape[1]
    step = ff // 2
    for low in range(0, ff, step):
        up = mm(normed_ref[...], w_up_ref[:, low : low + step])
        square = up * up
        tanh = jnp.tanh(up * (GELU_SCALE + GELU_SCALE * GELU_CUBE * square))
        half_up = 0.5 * up
        hidden = (half_up + half_up * tanh).astype(BF16)
        slope_ref[:, low : low + step] = (0.5 + 0.5 * tanh) + half_up * (1.0 - tanh * tanh) * (
            GELU_SCALE + 3.0 * GELU_SCALE * GELU_CUBE * square
        )
        mean_hidden = mm(valid, hidden) * scale
        high = mean_hidden.astype(BF16)
        rest = (mean_hidden - high.astype(F32)).astype(BF16)
        hidden_ref[:, low : low + step] = high
        w_down = w_down_ref[low : low + step]
        pooled += mm(high, w_down) + mm(rest, w_down)
    pooled_ref[...] = pooled.astype(pooled_ref.dtype)


def ffn_forward(line, length_rows, lengths, before, normed, w_up, w_down, last):
    total, width = normed.shape
    entries = lengths.shape[0]
    slots = total // entries
    rows = math.gcd(total, 256)
    some = rows // slots
    ff = w_up.shape[1] // 2
    return line.run(
        functools.partial(ffn_body, slots, last),
        "ffn_forward",
        7,
        (total // rows,),
        [
            (length_rows, rows_of(rows, 1)),
            (lengths, rows_of(some, 1)),
            (before, rows_of(some if last else rows, width)),
            (normed, rows_of(rows, width)),
            (w_up, pl.BlockSpec((width, ff), lambda i, *_: (0, int(last)))),
            (w_down, pl.BlockSpec((ff, width), lambda i, *_: (int(last), 0))),
        ],
        [
            ((total, ff), F32, rows_of(rows, ff), FAR),
            ((entries, ff), BF16, rows_of(some, ff)),
            ((entries, width), BF16 if last else F32, rows_of(some, width)),
        ],
    )


def ffn_back_body(
    slots,
    pooled_grad_ref,
    lengths_ref,
    slope_a_ref,
    slope_b_ref,
    middle_ref,
    gain_ffn_ref,
    w_up_ref,
    w_down_ref,
    grad_up_ref,
    grad_middle_ref,
    grad_branch_ref,
    gain_grad_ref,
):
    pooled_grad = pooled_grad_ref[...]
    rows, width = middle_ref.shape
    some = rows // slots
    wide = jnp.broadcast_to(pooled_grad[:, None, :], (some, slots, width)).reshape(rows, width)
    grad_final = wide * slot_weights(lengths_ref[...], slots)
    grad_ffn = grad_final.astype(BF16)
    ff = w_up_ref.shape[1]
    step = ff // 4
    grad_normed = jnp.zeros((rows, width), F32)
    for low in range(0, ff, step):
        grad_hidden = nt(grad_ffn, w_down_ref[low : low + step])
        slope_ref, inner = (slope_a_ref, low) if low < ff // 2 else (slope_b_ref, low - ff // 2)
        grad_up = (slope_ref[:, inner : inner + step] * grad_hidden).astype(BF16)
        grad_up_ref[:, low : low + step] = grad_up
        grad_normed += nt(grad_up, w_up_ref[:, low : low + step])
    unit, rate = center(middle_ref[...])
    grad, gain_grad = center_back(grad_normed, gain_ffn_ref[...], unit, rate)
    grad_middle = grad_final + grad
    grad_middle_ref[...] = grad_middle
    grad_branch_ref[...] = grad_middle.astype(BF16)

    @pl.when(pl.program_id(0) == 0)
    def _():
        gain_grad_ref[...] = jnp.zeros_like(gain_grad_ref)

    gain_grad_ref[...] += gain_grad


def ffn_back(line, pooled_grad, lengths, slopes, middle, gain_ffn, w_up, w_down):
    total, width = middle.shape
    entries = pooled_grad.shape[0]
    slots = total // entries
    rows = math.gcd(total, 256)
    some = rows // slots
    ff = w_up.shape[1]
    return line.run(
        functools.partial(ffn_back_body, slots),
        "ffn_back",
        15,
        (total // rows,),
        [
            (pooled_grad, rows_of(some, width)),
            (lengths, rows_of(rows, 1)),
            *((slope, rows_of(rows, ff // 2)) for slope in slopes),
            (middle, rows_of(rows, width)),
            (gain_ffn, fixed(gain_ffn.shape)),
            (w_up, fixed(w_up.shape)),
            (w_down, fixed(w_down.shape)),
        ],
        [
            ((total, ff), BF16, rows_of(rows, ff)),
            ((total, width), F32, rows_of(rows, width)),
            ((total, width), BF16, rows_of(rows, width)),
            ((1, width), F32, fixed((1, width))),
        ],
    )


def heads_back_body(slots, lengths_ref, w_out_ref, mixed_ref, grad_branch_ref, grad_mixed_ref):
    rows, width = grad_branch_ref.shape
    lengths = lengths_ref[...]
    grad_ctx = nt(grad_branch_ref[...], w_out_ref[...]).astype(BF16)
    row = lax.broadcasted_iota(jnp.int32, (GROUP, GROUP), 0)
    col = lax.broadcasted_iota(jnp.int32, (GROUP, GROUP), 1)
    same = row // slots == col // slots
    lows = range(0, width, PAIR)
    for base in range(0, rows, GROUP):
        span = slice(base, base + GROUP)
        valid = same & (row % slots <= lengths[span])
        queries = [mixed_ref[span, low : low + PAIR] for low in lows]
        keys = [split_heads(mixed_ref[span, width + low : width + low + PAIR]) for low in lows]
        values = [split_heads(mixed_ref[span, 2 * width + low : 2 * width + low + PAIR]) for low in lows]
        grad_pairs = [grad_ctx[span, low : low + PAIR] for low in lows]
        raws = [nt(key, query) for key, query in zip(keys, queries)]
        grad_raws = [nt(value, grad_pair) for value, grad_pair in zip(values, grad_pairs)]
        sides = (slice(0, GROUP), slice(GROUP, 2 * GROUP))
        heads = [raw[side] for raw in raws for side in sides]
        heads = [jnp.where(valid, head * HEAD_DIM ** (-0.5), -1000000000.0) for head in heads]
        heads = [jnp.exp(head - jnp.max(head, axis=0, keepdims=True)) for head in heads]
        probs = [head * (1.0 / jnp.sum(head, axis=0, keepdims=True)) for head in heads]
        grads = [grad_raw[side] for grad_raw in grad_raws for side in sides]
        grads = [
            prob * (grad - jnp.sum(grad * prob, axis=0, keepdims=True)) for prob, grad in zip(probs, grads)
        ]
        probs = [prob.astype(BF16) for prob in probs]
        grads = [(grad * HEAD_DIM ** (-0.5)).astype(BF16) for grad in grads]
        for j, low in enumerate(lows):
            scores_grad = jnp.concatenate(grads[2 * j : 2 * j + 2], axis=0)
            prob = jnp.concatenate(probs[2 * j : 2 * j + 2], axis=0)
            grad_mixed_ref[span, low : low + PAIR] = tn(scores_grad, keys[j]).astype(BF16)
            grad_keys = join_heads(mm(scores_grad, queries[j]))
            grad_mixed_ref[span, width + low : width + low + PAIR] = grad_keys.astype(BF16)
            grad_values = join_heads(mm(prob, grad_pairs[j]))
            grad_mixed_ref[span, 2 * width + low : 2 * width + low + PAIR] = grad_values.astype(BF16)


def heads_back(line, lengths, w_out, mixed, grad_branch, slots):
    total, width = grad_branch.shape
    rows = math.gcd(total, 256)
    return line.run(
        functools.partial(heads_back_body, slots),
        "heads_back",
        13,
        (total // rows,),
        [
            (lengths, rows_of(rows, 1)),
            (w_out, fixed(w_out.shape)),
            (mixed, rows_of(rows, 3 * width)),
            (grad_branch, rows_of(rows, width)),
        ],
        [((total, 3 * width), BF16, rows_of(rows, 3 * width))],
    )[0]


def attn_back_body(
    pieces_ref,
    scripts_ref,
    script_table_ref,
    gain_attn_ref,
    w_qkv_ref,
    grad_mixed_ref,
    grad_middle_ref,
    gain_ffn_grad_ref,
    grad_pieces_ref,
    small_ref,
):
    start, onehot = start_of(pieces_ref, scripts_ref, script_table_ref)
    grad_normed = nt(grad_mixed_ref[...], w_qkv_ref[...])
    unit, rate = center(start)
    grad, gain_grad = center_back(grad_normed, gain_attn_ref[...], unit, rate)
    grad_pieces = grad_middle_ref[...] + grad
    grad_pieces_ref[...] = grad_pieces.reshape(grad_pieces_ref.shape)

    groups = onehot.shape[1]

    @pl.when(pl.program_id(0) == 0)
    def _():
        small_ref[...] = jnp.zeros_like(small_ref)
        small_ref[groups + 1 : groups + 2] = gain_ffn_grad_ref[...]

    small_ref[groups : groups + 1] += gain_grad
    small_ref[:groups] += lax.dot_general(
        onehot, grad_pieces, (((0,), (0,)), ((), ())), precision=highest
    )


def attn_back(
    line, pieces, scripts, script_table, gain_attn, w_qkv, grad_mixed, grad_middle, gain_ffn_grad
):
    entries, slots, width = pieces.shape
    total = entries * slots
    rows = math.gcd(total, 256)
    some = rows // slots
    small = ((script_table.shape[0] + 2 + 7) // 8 * 8, width)
    return line.run(
        attn_back_body,
        "attn_back",
        9,
        (total // rows,),
        [
            (pieces, pl.BlockSpec((some, slots, width), lambda i, *_: (i, 0, 0))),
            (scripts, rows_of(rows, 1)),
            (script_table, fixed(script_table.shape)),
            (gain_attn, fixed(gain_attn.shape)),
            (w_qkv, fixed(w_qkv.shape)),
            (grad_mixed, rows_of(rows, 3 * width)),
            (grad_middle, rows_of(rows, width)),
            (gain_ffn_grad, fixed(gain_ffn_grad.shape)),
        ],
        [
            ((entries, slots, width), F32, pl.BlockSpec((some, slots, width), lambda i, *_: (i, 0, 0)), FAR),
            (small, F32, fixed(small)),
        ],
    )


def per_device(
    pieces,
    lengths,
    scripts,
    script_table,
    gain_attn,
    gain_ffn,
    w_qkv,
    w_out,
    w_up,
    w_down,
    w_proj,
    token_ids,
    out_grad,
):
    entries, slots, width = pieces.shape
    ent_count = lax.axis_size("ent")
    rep_count = lax.axis_size("rep")
    devices = ent_count * rep_count
    features = w_proj.shape[1]
    vocab = entries * devices
    rows_dev, text_len = token_ids.shape
    tokens = rows_dev * text_len
    levels = make_levels(ent_count, rep_count)
    sizes = tuple(size for _, size, _ in levels)
    me = lax.axis_index("ent") * rep_count + lax.axis_index("rep")
    chunks = 1 if devices <= 32 else 8
    each = entries // chunks
    span = vocab // chunks
    slot = slot_of(token_ids // entries ^ me, levels)
    within = token_ids % entries
    slot_ids = within // each * span + slot * each + within % each
    script_rows = jnp.repeat(scripts, slots)[:, None]
    length_rows = jnp.repeat(lengths, slots)[:, None]
    gain_attn, gain_ffn = gain_attn[None], gain_ffn[None]

    cut = len(levels)
    while math.prod(sizes[:cut]) * 16 > w_down.shape[0]:
        cut -= 1
    near, far = levels[:cut], levels[cut:]
    count = math.prod(sizes[:cut])
    slot_index = jnp.arange(count, dtype=jnp.int32) ^ slot_of(me, near)
    line = Line()

    def cut_up(keep, send, some):
        shape = tuple(size for _, size, _ in some[1:]) + keep.shape[-2:]
        return keep.reshape(shape), send.reshape(shape)

    flat_grad = out_grad
    parts, pooled_grads = [], []
    for chunk in range(chunks):
        first = chunk * span
        part_send, send, *flat = scatter_rows(
            line, slot_ids, flat_grad, w_proj, first + span // 2, span // 2, BF16
        )
        flat_grad = flat[0] if flat else flat_grad
        part_keep, keep = scatter_rows(line, slot_ids, flat_grad, w_proj, first, span // 2, F32)
        parts.append((part_keep, part_send))
        shape = sizes[1:] + (each, width)
        pooling = sum_halves(line, keep.reshape(shape), send.reshape(shape), levels, pooled_grads)
        if chunks > 1:
            for _ in pooling:
                pass
    next(pooling, None)
    next(pooling, None)
    normed, mixed, context, middle, normed_ffn = attn_forward(
        line, pieces, script_rows, length_rows, script_table, gain_attn, gain_ffn, w_qkv, w_out
    )
    next(pooling, None)
    length_cols = lengths[:, None]
    slope_a, hidden_a, pooled = ffn_forward(
        line, length_rows, length_cols, middle, normed_ffn, w_up, w_down, False
    )
    next(pooling, None)
    slope_b, hidden_b, pooled = ffn_forward(
        line, length_rows, length_cols, pooled, normed_ffn, w_up, w_down, True
    )
    for _ in pooling:
        pass
    grad_pooled = jnp.concatenate(pooled_grads, axis=0) if chunks > 1 else pooled_grads[0]

    held = [((), each, width, BF16, lambda index: [(0, (), ALL, 0, 0)])]
    halves = [[] for _ in range(chunks)]
    spreads = [
        gather_halves(
            line, stage(line, [(pooled[chunk * each :][:each], [])], held)[0], levels, halves[chunk]
        )
        for chunk in range(chunks)
    ]

    def spread_on():
        if chunks == 1:
            next(spreads[0])

    spread_on()
    down = tall_weight(line, slot_index, (hidden_a, hidden_b), grad_pooled.astype(BF16))
    grad_up, grad_middle, grad_branch, part_gain_ffn = ffn_back(
        line, grad_pooled, length_rows, (slope_a, slope_b), middle, gain_ffn, w_up, w_down
    )
    spread_on()
    up = wide_weight(line, slot_index, normed_ffn, grad_up)
    ffn_all, two_all = [], []
    ffn_sum = all_sum_two(line, *cut_up(*down, near), *cut_up(*up, near), near, far, ffn_all)
    next(ffn_sum)
    spread_on()
    grad_mixed = heads_back(line, length_rows, w_out, mixed, grad_branch, slots)
    next(ffn_sum)
    grad_pieces, small = attn_back(
        line,
        pieces,
        script_rows,
        script_table,
        gain_attn,
        w_qkv,
        grad_mixed,
        grad_middle,
        part_gain_ffn,
    )
    spread_on()
    two = two_weights(line, slot_index, normed, grad_mixed, context, grad_branch, small)
    two_sum = all_sum(line, *cut_up(*two, near), near, far, two_all)
    next(two_sum)
    tables, part_proj = [], None
    for chunk in range(chunks):
        for _ in spreads[chunk]:
            pass
        own, other = halves[chunk]
        table, part = table_and_grad(
            line, own.reshape(span // 2, width), other.reshape(span // 2, width), w_proj, *parts[chunk]
        )
        tables.append(table)
        part_proj = part if part_proj is None else part_proj + part
    grad_w_proj = part_proj + swap(part_proj, levels[0])
    looked_up = None
    order = [(ffn_sum, two_sum), (ffn_sum,), (two_sum,), (ffn_sum, two_sum), (ffn_sum,)]
    for part, going in enumerate(order):
        for steps in going:
            next(steps, 0)
        if part < 4:
            looked_up = lookup(line, slot_ids, tables, part, 4, looked_up)
    next(two_sum, 0)
    next(ffn_sum, 0)
    next(two_sum, 0)
    for _ in ffn_sum:
        pass
    next(two_sum, 0)
    grad_w_down = unpack(line, slot_index, merge(ffn_all[0]), merge(ffn_all[1]), *w_down.shape)
    grad_w_up = unpack(line, slot_index, merge(ffn_all[2]), merge(ffn_all[3]), *w_up.shape)
    for _ in two_sum:
        pass
    grad_w_qkv, grad_w_out, small = unpack_two(
        line, slot_index, *map(merge, two_all), *w_qkv.shape, small.shape
    )
    groups = script_table.shape[0]
    return (
        looked_up,
        grad_pieces,
        small[:groups],
        small[groups],
        small[groups + 1],
        grad_w_qkv,
        grad_w_out,
        grad_w_up,
        grad_w_down,
        grad_w_proj,
    )


def solution(mesh):
    in_specs = (
        P(("ent", "rep"), None, None),
        P(("ent", "rep")),
        P(("ent", "rep")),
        P(),
        P(),
        P(),
        P(),
        P(),
        P(),
        P(),
        P(None, "ent"),
        P("rep", None),
        P("ent", "rep", None),
    )
    out_specs = (
        P("ent", "rep", None),
        P(("ent", "rep"), None, None),
        P(),
        P(),
        P(),
        P(),
        P(),
        P(),
        P(),
        P(None, "ent"),
    )
    return jax.shard_map(
        per_device, mesh=mesh, in_specs=in_specs, out_specs=out_specs, check_vma=False
    )
```

```python
import functools
import math

import jax
import jax.numpy as jnp
import numpy as np
from jax import lax
from jax.experimental import pallas as pl
from jax.experimental.pallas import tpu as pltpu
from jax.sharding import PartitionSpec as P

HEADS = 8
HEAD_DIM = 64
F32 = jnp.float32
BF16 = jnp.bfloat16
highest = lax.Precision.HIGHEST
MIB = 1024 * 1024


def make_levels(ent_count, rep_count):
    levels = [("rep", rep_count, 0)]
    bit, total = 0, ent_count.bit_length() - 1
    while bit < total:
        width = 1 if bit < 2 else min(2, total - bit)
        levels.append(("ent", 1 << width, bit))
        bit += width
    return levels


def slot_of(number, levels):
    rep_count = levels[0][1]
    slot = number % rep_count
    ent = number // rep_count
    for _, size, shift in levels[1:]:
        slot = slot * size + (ent >> shift) % size
    return slot


def swap(value, level, k):
    name, size, shift = level
    count = lax.axis_size(name)
    return lax.ppermute(value, name, [(i, i ^ (k << shift)) for i in range(count)])


def merge(value):
    return value.reshape((-1,) + value.shape[-2:])


FAR = True


class Line:
    def __init__(self):
        self.last = []

    def run(self, body, name, micros, grid, ins, outs, prefetch=(), alias=None, room=24 * MIB, scratch=()):
        count = len(prefetch) + len(ins)
        extra = self.last + ([] if alias is None else [alias])
        token = (8, 128)

        def wrapped(*refs):
            held = len(refs) - len(scratch)
            refs[held - 1][...] = jnp.zeros(token, F32)
            body(*refs[:count], *refs[count + len(extra) : held - 1], *refs[held:])

        *results, last = pl.pallas_call(
            wrapped,
            grid_spec=pltpu.PrefetchScalarGridSpec(
                num_scalar_prefetch=len(prefetch),
                grid=grid,
                in_specs=[spec for _, spec in ins] + [pl.BlockSpec(memory_space=pl.ANY)] * len(extra),
                out_specs=[spec for _, _, spec, *_ in outs] + [pl.BlockSpec(token, lambda *_: (0, 0))],
                scratch_shapes=scratch,
            ),
            out_shape=[
                pltpu.HBM(shape, dtype) if far else jax.ShapeDtypeStruct(shape, dtype)
                for shape, dtype, _, *far in outs
            ]
            + [jax.ShapeDtypeStruct(token, F32)],
            input_output_aliases={} if alias is None else {count + len(extra) - 1: 0},
            compiler_params=pltpu.CompilerParams(vmem_limit_bytes=room),
            cost_estimate=pl.CostEstimate(
                flops=int(micros * 3e9), bytes_accessed=int(micros * 9e6), transcendentals=0
            ),
            name=name,
        )(*prefetch, *(value for value, _ in ins), *extra)
        self.last = [last]
        return results


def swap(value, level, k=1):
    name, size, shift = level
    count = lax.axis_size(name)
    return lax.ppermute(value, name, [(i, i ^ (k << shift)) for i in range(count)])


def swaps(values, level):
    return [swap(value, level, k) for k, value in enumerate(values, 1)]


ALL = slice(None)
BELOW = 16


def stage_body(layout, cuts, *refs):
    sums, position = [], 0
    for number in layout:
        sums.append(refs[position : position + number])
        position += number

    def piece(number, index, cols, rows=ALL):
        total = sums[number][0][index][rows, cols]
        for ref in sums[number][1:]:
            total = total.astype(F32) + ref[index][rows, cols].astype(F32)
        return total

    for out_ref, sources in zip(refs[position:], cuts):
        for target, parts in sources:
            for number, index, cols, row, col, *rows in parts:
                value = piece(number, index, cols, *rows).astype(out_ref.dtype)
                where = target + (slice(row, row + value.shape[0]), slice(col, col + value.shape[1]))
                out_ref[where] = value


def stage(line, sums, outs, steps=1):
    values = [value for kept, received in sums for value in [kept, *received]]

    def spec(shape):
        return pl.BlockSpec(memory_space=pltpu.VMEM)

    cuts = [
        [(target, source(target)) for target in np.ndindex(*lead)] for lead, _, _, _, source in outs
    ]
    shapes = [(lead + (rows, cols), dtype) for lead, rows, cols, dtype, _ in outs]
    held = [(value.shape, value.dtype) for value in values] + [(shape, jnp.dtype(dtype)) for shape, dtype in shapes]
    return line.run(
        functools.partial(stage_body, [1 + len(received) for _, received in sums], cuts),
        "exchange",
        0.5,
        (),
        [(value, spec(value.shape)) for value in values],
        [(shape, dtype, spec(shape)) for shape, dtype in shapes],
        room=2 * MIB + sum(math.prod(shape) * dtype.itemsize for shape, dtype in held),
    )


def split(number, value, axis, cols=ALL, width=None):
    lead = value.shape[:-2]
    rest = lead[:axis] + lead[axis + 1 :]
    outs = []
    for k in range(lead[axis]):

        def source(index, k=k):
            return [(number, index[:axis] + (k,) + index[axis:], cols, 0, 0)]

        outs.append((rest, value.shape[-2], width or value.shape[-1], F32 if k == 0 else BF16, source))
    return outs


def stacked(numbers, value, axis, rows=ALL):
    lead = value.shape[:-2]
    shape = lead[:axis] + (len(numbers),) + lead[axis:]

    def source(index):
        return [(numbers[index[axis]], index[:axis] + index[axis + 1 :], ALL, 0, 0)]

    return (shape, value.shape[-2], value.shape[-1], value.dtype, source)


def finish(line, sums, far, shape, dtype):
    whole = [(0, (), ALL, 0, 0)]
    for level in far:
        outs = [((), *shape, kind, lambda index: whole) for kind in (F32, BF16)]
        keep, send = stage(line, sums, outs)
        sums = [(keep, [swap(send, level, k) for k in range(1, level[1])])]
        yield
    yield stage(line, sums, [((), *shape, dtype, lambda index: whole)])[0]


def sum_halves(line, keep, send, levels, out, far=(), dtype=F32):
    received = swap(send, levels[0])
    yield
    rows, width = keep.shape[-2:]
    half = width // 2
    left, right = slice(0, half), slice(half, width)
    steps = 4 if rows % 64 == 0 else 1
    outs = split(0, keep, 0, left, half) + split(0, keep, 1, right, half)
    keep_a, send_a, keep_b, send_b = stage(line, [(keep, [received])], outs, steps)
    got_a, got_b = swap(send_a, levels[1]), swap(send_b, levels[2])
    yield
    outs = split(0, keep_a, 0) + split(1, keep_b, 0)
    sums = [(keep_a, [got_a]), (keep_b, [got_b])]
    keep_a, send_a, keep_b, send_b = stage(line, sums, outs, steps)
    sums = [(keep_a, [swap(send_a, levels[2])]), (keep_b, [swap(send_b, levels[1])])]
    yield
    for place, level in enumerate(levels[3:]):
        if place == 0:
            lead = keep_a.shape[1:-2]

            def source(index, k):
                return [(0, (k,) + index, ALL, 0, 0), (1, (k,) + index, ALL, 0, half)]

            outs = [
                (lead, rows, width, F32 if k == 0 else BF16, functools.partial(source, k=k))
                for k in range(level[1])
            ]
        else:
            outs = split(0, keep, 0)
        keep, *sends = stage(line, sums, outs)
        sums = [(keep, swaps(sends, level))]
        yield
    for value in finish(line, sums, far, (rows, width), dtype):
        if value is None:
            yield
    out.append(value)


def gather_halves(line, value, levels, out):
    rows, width = value.shape
    half = width // 2
    for place, level in reversed(list(enumerate(levels[3:]))):
        got = [swap(value, level, k) for k in range(1, level[1])]
        yield
        parts = [(part, []) for part in [value, *got]]
        numbers = list(range(level[1]))
        if place:
            value = stage(line, parts, [stacked(numbers, value, 0)])[0]
        else:
            lead = (level[1],) + value.shape[:-2]

            def source(index, cols):
                return [(index[0], index[1:], cols, 0, 0)]

            outs = [
                (lead, rows, half, BF16, functools.partial(source, cols=cols))
                for cols in (slice(0, half), slice(half, width))
            ]
            value_a, value_b = stage(line, parts, outs)
    got_a, got_b = swap(value_a, levels[2]), swap(value_b, levels[1])
    yield
    sums = [(part, []) for part in (value_a, got_a, value_b, got_b)]
    outs = [stacked([0, 1], value_a, 0), stacked([2, 3], value_b, 0)]
    value_a, value_b = stage(line, sums, outs)
    got_a, got_b = swap(value_a, levels[1]), swap(value_b, levels[2])
    yield
    sums = [(part, []) for part in (value_a, got_a, value_b, got_b)]
    lead = (2,) + value_a.shape[:-2]

    def joined(index):
        left, right = index[0], index[1]
        return [(left, index[1:], ALL, 0, 0), (2 + right, (left,) + index[2:], ALL, 0, half)]

    value = stage(line, sums, [(lead, rows, width, BF16, joined)])[0]
    out += [value, swap(value, levels[0])]
    yield


def all_sum(line, keep, send, near, far, out):
    mine = []
    yield from sum_halves(line, keep, send, near, mine, far, BF16)
    yield from gather_halves(line, mine[0], near, out)


def all_sum_two(line, keep_a, send_a, keep_b, send_b, extra, near, far, out):
    got_a, got_b = swap(send_a, near[0]), swap(send_b, near[0])
    yield
    rows = keep_a.shape[-2]
    outs = split(0, keep_a, 0) + split(1, keep_b, 1)
    keep_a, send_a, keep_b, send_b = stage(line, [(keep_a, [got_a]), (keep_b, [got_b])], outs)
    got_a, got_b = swap(send_a, near[1]), swap(send_b, near[2])
    yield
    outs = split(0, keep_a, 0) + split(1, keep_b, 0)
    keep_a, send_a, keep_b, send_b = stage(line, [(keep_a, [got_a]), (keep_b, [got_b])], outs)
    sums = [(keep_a, [swap(send_a, near[2])]), (keep_b, [swap(send_b, near[1])])]
    yield
    below = extra()
    added = below.shape[0]
    for place, level in enumerate(near[3:]):
        if place == 0:
            lead = keep_a.shape[1:-2]
            sums = sums + [(below, [])]

            def source(index, k):
                places = [(0, (k,) + index, 0), (1, (k,) + index, rows), (2, (), 2 * rows)]
                return [(number, where, ALL, row, 0) for number, where, row in places]

            outs = [
                (lead, 2 * rows + added, PANEL, F32 if k == 0 else BF16, functools.partial(source, k=k))
                for k in range(level[1])
            ]
        else:
            outs = split(0, keep, 0)
        keep, *sends = stage(line, sums, outs)
        sums = [(keep, swaps(sends, level))]
        yield
    for level in far:
        outs = [((), 2 * rows + added, PANEL, kind, lambda index: [(0, (), ALL, 0, 0)]) for kind in (F32, BF16)]
        keep, send = stage(line, sums, outs)
        sums = [(keep, [swap(send, level, k) for k in range(1, level[1])])]
        yield
    outs = [
        ((), size, PANEL, BF16, lambda index, part=part: [(0, (), ALL, 0, 0, part)])
        for size, part in ((2 * rows, slice(0, 2 * rows)), (added, slice(2 * rows, 2 * rows + added)))
    ]
    value, below = stage(line, sums, outs)
    for place, level in reversed(list(enumerate(near[3:]))):
        got = [swap(value, level, k) for k in range(1, level[1])]
        yield
        numbers = list(range(level[1]))
        parts = [(part, []) for part in [value, *got]]
        if place:
            value = stage(line, parts, [stacked(numbers, value, 0)])[0]
            continue
        lead = (level[1],) + value.shape[:-2]

        def first(index):
            return [(index[0], index[1:], ALL, 0, 0, slice(0, rows))]

        def second(index):
            number = int(np.ravel_multi_index(index, lead)) * BELOW % added
            return [
                (index[0], index[1:], ALL, 0, 0, slice(rows, 2 * rows)),
                (len(numbers), (), ALL, rows, 0, slice(number, number + BELOW)),
            ]

        outs = [(lead, rows, PANEL, BF16, first), (lead, rows + BELOW, PANEL, BF16, second)]
        value_a, value_b = stage(line, parts + [(below, [])], outs)
    got_a, got_b = swap(value_a, near[2]), swap(value_b, near[1])
    yield
    sums = [(part, []) for part in (value_a, got_a, value_b, got_b)]
    outs = [stacked([0, 1], value_a, 0), stacked([2, 3], value_b, 0)]
    value_a, value_b = stage(line, sums, outs)
    got_a, got_b = swap(value_a, near[1]), swap(value_b, near[2])
    yield
    sums = [(part, []) for part in (value_a, got_a, value_b, got_b)]
    outs = [stacked([0, 1], value_a, 0), stacked([2, 3], value_b, 1)]
    value_a, value_b = stage(line, sums, outs)
    out += [value_a, swap(value_a, near[0]), value_b, swap(value_b, near[0])]
    yield


def fixed(shape):
    return pl.BlockSpec(shape, lambda i, *_: (0,) * len(shape))


def rows_of(rows, width):
    return pl.BlockSpec((rows, width), lambda i, *_: (i, 0))


def selector(ids, base, rows):
    entry = lax.broadcasted_iota(jnp.int32, (rows, 1), 0).astype(jnp.int16)
    return jnp.where(entry == (ids - base).astype(jnp.int16), jnp.ones((), BF16), jnp.zeros((), BF16))


def nt(left, right):
    return lax.dot_general(left, right, (((1,), (1,)), ((), ())), preferred_element_type=F32)


def tn(left, right):
    return lax.dot_general(left, right, (((0,), (0,)), ((), ())), preferred_element_type=F32)


def mm(left, right):
    return jnp.dot(left, right, preferred_element_type=F32)


def scatter_body(first, ids_ref, grad_ref, proj_ref, table_ref, pooled_ref, flat_ref):
    @pl.when(pl.program_id(0) == 0)
    def _():
        flat_ref[...] = grad_ref[...].reshape(flat_ref.shape)

    rows = table_ref.shape[0]
    base = first + pl.program_id(0) * rows
    picks = [selector(ids_ref[row : row + 1], base, rows) for row in range(ids_ref.shape[0])]
    part = nt(jnp.concatenate(picks, axis=1), flat_ref[...]).astype(BF16)
    table_ref[...] = part
    pooled_ref[...] = nt(part, proj_ref[...]).astype(pooled_ref.dtype)


def scatter_rows(line, ids, grad, w_proj, first, count, dtype):
    features = grad.shape[0]
    width = w_proj.shape[0]
    rows = min(512, count)
    return line.run(
        functools.partial(scatter_body, first),
        "scatter_rows",
        14,
        (count // rows,),
        [
            (ids, fixed(ids.shape)),
            (grad, pl.BlockSpec(memory_space=pltpu.VMEM)),
            (w_proj, fixed(w_proj.shape)),
        ],
        [
            ((count, features), BF16, rows_of(rows, features), FAR),
            ((count, width), dtype, rows_of(rows, width)),
        ],
        room=28 * MIB,
        scratch=[pltpu.VMEM((features, ids.size), BF16)],
    )


def table_body(steps, own_ref, other_ref, proj_ref, part_own_ref, part_other_ref, table_ref, grad_ref):
    step = pl.program_id(0)

    @pl.when(step == 0)
    def _():
        grad_ref[...] = jnp.zeros_like(grad_ref)

    def one(pooled_ref, part_ref):
        pooled = pooled_ref[...]
        cols = lax.dot_general(
            proj_ref[...], pooled, (((0,), (1,)), ((), ())), preferred_element_type=F32
        )
        table_ref[...] = cols.astype(BF16)
        grad_ref[...] += tn(pooled, part_ref[...])

    @pl.when(step < steps)
    def _():
        one(own_ref, part_own_ref)

    @pl.when(step >= steps)
    def _():
        one(other_ref, part_other_ref)


def table_and_grad(line, own, other, w_proj, part_own, part_other):
    count, width = own.shape
    features = w_proj.shape[1]
    rows = min(1024, count)
    steps = count // rows

    def first(cols):
        return pl.BlockSpec((rows, cols), lambda i, *_: (jnp.minimum(i, steps - 1), 0))

    def second(cols):
        return pl.BlockSpec((rows, cols), lambda i, *_: (jnp.maximum(i - steps, 0), 0))

    return line.run(
        functools.partial(table_body, steps),
        "table_and_grad",
        5,
        (2 * steps,),
        [
            (own, first(width)),
            (other, second(width)),
            (w_proj, fixed(w_proj.shape)),
            (part_own, first(features)),
            (part_other, second(features)),
        ],
        [
            ((features, 2 * count), BF16, pl.BlockSpec((features, rows), lambda i, *_: (0, i))),
            ((width, features), F32, fixed((width, features))),
        ],
    )


def lookup_body(chunk, ids_ref, *refs):
    table_refs, out_ref = refs[:-1], refs[-1]
    rows = ids_ref.shape[0]

    def find(base, table):
        picks = [selector(ids_ref[row : row + 1], base, chunk) for row in range(rows)]
        return mm(table, jnp.concatenate(picks, axis=1))

    total = None
    for index, table_ref in enumerate(table_refs):
        vocab = table_ref.shape[1]
        for inner in range(0, vocab, chunk):
            part = find(index * vocab + inner, table_ref[:, inner : inner + chunk])
            total = part if total is None else total + part
    out_ref[...] = total.astype(BF16).reshape(out_ref.shape)


def lookup(line, ids, tables, part, before=None):
    rows, text_len = ids.shape
    features, vocab = tables[0].shape
    block = text_len // 8
    first, last = part
    return line.run(
        functools.partial(lookup_body, min(vocab, 4096)),
        "lookup",
        3 * (last - first),
        (last - first,),
        [(ids, pl.BlockSpec((rows, block), lambda i, *_: (0, i + first)))]
        + [(table, fixed(table.shape)) for table in tables],
        [
            (
                (features, rows, text_len),
                BF16,
                pl.BlockSpec((features, rows, block), lambda i, *_: (0, 0, i + first)),
                FAR,
            )
        ],
        alias=before,
    )[0]


PANEL = 512


def store_slots(slots_ref, first, part, keep_ref, send_ref):
    half, rows, _ = keep_ref.shape
    for j in range(part.shape[0] // rows):
        slot = slots_ref[first + j]
        piece = part[j * rows : (j + 1) * rows]

        @pl.when(slot < half)
        def _():
            keep_ref[slot] = piece

        @pl.when(slot >= half)
        def _():
            send_ref[slot - half] = piece.astype(BF16)


def weight_body(slots_ref, left_ref, right_ref, keep_ref, send_ref):
    part = tn(left_ref[...], right_ref[...])
    store_slots(slots_ref, pl.program_id(0) * (part.shape[0] // keep_ref.shape[1]), part, keep_ref, send_ref)


def tall_body(steps, slots_ref, first_ref, second_ref, right_ref, keep_ref, send_ref):
    step = pl.program_id(0)
    each = PANEL // keep_ref.shape[1]

    @pl.when(step < steps)
    def _():
        store_slots(slots_ref, step * each, tn(first_ref[...], right_ref[...]), keep_ref, send_ref)

    @pl.when(step >= steps)
    def _():
        store_slots(slots_ref, step * each, tn(second_ref[...], right_ref[...]), keep_ref, send_ref)


def two_weights_body(last, slots_ref, left_ref, right_ref, left2_ref, right2_ref, keep_ref, send_ref):
    step = pl.program_id(0)
    each = left_ref.shape[1] // keep_ref.shape[1]

    @pl.when(step < last)
    def _():
        store_slots(slots_ref, step * each, tn(left_ref[...], right_ref[...]), keep_ref, send_ref)

    @pl.when(step == last)
    def _():
        store_slots(slots_ref, step * each, tn(left2_ref[...], right2_ref[...]), keep_ref, send_ref)


def slot_outs(count, rows):
    shape = (count // 2, rows, PANEL)
    return [(shape, F32, fixed(shape)), (shape, BF16, fixed(shape))]


def panel_of(depth):
    return pl.BlockSpec((depth, PANEL), lambda i, *_: (0, i))


def tall_weight(line, slots, lefts, right):
    depth, half = lefts[0].shape
    steps = half // PANEL
    return line.run(
        functools.partial(tall_body, steps),
        "tall_weight",
        3,
        (2 * steps,),
        [
            (lefts[0], pl.BlockSpec((depth, PANEL), lambda i, *_: (0, jnp.minimum(i, steps - 1)))),
            (lefts[1], pl.BlockSpec((depth, PANEL), lambda i, *_: (0, jnp.maximum(i - steps, 0)))),
            (right, fixed(right.shape)),
        ],
        slot_outs(slots.shape[0], 2 * half // slots.shape[0]),
        [slots],
    )


def wide_weight(line, slots, left, right):
    depth, cols = right.shape
    return line.run(
        weight_body,
        "wide_weight",
        8,
        (cols // PANEL,),
        [(left, fixed(left.shape)), (right, panel_of(depth))],
        slot_outs(slots.shape[0], cols // PANEL * left.shape[1] // slots.shape[0]),
        [slots],
    )


def two_weights(line, slots, left, right, left2, right2):
    depth, cols = right.shape
    last = cols // PANEL
    return line.run(
        functools.partial(two_weights_body, last),
        "two_weights",
        5,
        (last + 1,),
        [
            (left, fixed(left.shape)),
            (right, pl.BlockSpec((depth, PANEL), lambda i, *_: (0, jnp.minimum(i, last - 1)))),
            (left2, fixed(left2.shape)),
            (right2, fixed(right2.shape)),
        ],
        slot_outs(slots.shape[0], (last + 1) * left.shape[1] // slots.shape[0]),
        [slots],
    )


def load_slots(slots_ref, first, own_ref, other_ref, out_ref, rows):
    half = own_ref.shape[0]
    for j in range(out_ref.shape[0] // rows):
        slot = slots_ref[first + j]

        @pl.when(slot < half)
        def _():
            out_ref[j * rows : (j + 1) * rows] = own_ref[slot, :rows].astype(F32)

        @pl.when(slot >= half)
        def _():
            out_ref[j * rows : (j + 1) * rows] = other_ref[slot - half, :rows].astype(F32)


def unpack_body(slots_ref, own_ref, other_ref, out_ref):
    rows = own_ref.shape[1]
    each = out_ref.shape[0] // rows
    load_slots(slots_ref, pl.program_id(0) * each, own_ref, other_ref, out_ref, rows)


def unpack(line, slots, own, other, height):
    tile = min(512, height)
    return line.run(
        unpack_body,
        "unpack",
        5,
        (height // tile,),
        [(own, fixed(own.shape)), (other, fixed(other.shape))],
        [((height, PANEL), F32, pl.BlockSpec((tile, PANEL), lambda i, *_: (i, 0)), FAR)],
        [slots],
    )[0]


def unpack_extra_body(rows, inner, slots_ref, own_ref, other_ref, out_ref, *extra_refs):
    each = out_ref.shape[0] // rows
    load_slots(slots_ref, pl.program_id(0) * each, own_ref, other_ref, out_ref, rows)

    @pl.when(pl.program_id(0) == 0)
    def _():
        needed = sum(ref.shape[0] for ref in extra_refs)
        sums = []
        for place in range((needed + BELOW - 1) // BELOW):
            total = jnp.zeros((BELOW, PANEL), F32)
            for ref in (own_ref, other_ref):
                for slot in range(place, ref.shape[0], inner):
                    total += ref[slot, rows:].astype(F32)
            sums.append(total)
        total = jnp.concatenate(sums, axis=0)
        first = 0
        for ref in extra_refs:
            ref[...] = total[first : first + ref.shape[0]]
            first += ref.shape[0]


def unpack_extra(line, slots, own, other, height, cols, extra, inner):
    return line.run(
        functools.partial(unpack_extra_body, height * cols // PANEL // slots.shape[0], inner),
        "unpack",
        5,
        (cols // PANEL,),
        [(own, fixed(own.shape)), (other, fixed(other.shape))],
        [((height, cols), F32, pl.BlockSpec((height, PANEL), lambda i, *_: (0, i)), FAR)]
        + [((rows, PANEL), F32, fixed((rows, PANEL))) for rows in extra],
        [slots],
    )


def unpack_two_body(last, slots_ref, own_ref, other_ref, out_ref, out2_ref):
    step = pl.program_id(0)
    rows = own_ref.shape[1]
    each = out_ref.shape[0] // rows

    @pl.when(step < last)
    def _():
        load_slots(slots_ref, step * each, own_ref, other_ref, out_ref, rows)

    @pl.when(step == last)
    def _():
        load_slots(slots_ref, step * each, own_ref, other_ref, out2_ref, rows)


def unpack_two(line, slots, own, other, height, cols):
    last = cols // PANEL
    return line.run(
        functools.partial(unpack_two_body, last),
        "unpack_two",
        5,
        (last + 1,),
        [(own, fixed(own.shape)), (other, fixed(other.shape))],
        [
            (
                (height, cols),
                F32,
                pl.BlockSpec((height, PANEL), lambda i, *_: (0, jnp.minimum(i, last - 1))),
                FAR,
            ),
            ((height, PANEL), F32, fixed((height, PANEL)), FAR),
        ],
        [slots],
    )


GROUP = 128
PAIR = 2 * HEAD_DIM
GELU_SCALE = 0.7978845608028654
GELU_CUBE = 0.044715


def center(values):
    centered = values - jnp.mean(values, axis=-1, keepdims=True)
    spread = jnp.mean(centered * centered, axis=-1, keepdims=True)
    rate = lax.rsqrt(spread + 1e-05)
    return centered * rate, rate


def center_back(grad, gain, unit, rate):
    gain_grad = jnp.sum(grad * unit, axis=0, keepdims=True)
    grad = grad * gain
    mean_grad = jnp.mean(grad, axis=-1, keepdims=True)
    mean_unit = jnp.mean(grad * unit, axis=-1, keepdims=True)
    return rate * (grad - mean_grad - unit * mean_unit), gain_grad


def start_of(pieces_ref, scripts_ref, script_table_ref):
    entries, slots, width = pieces_ref.shape
    groups = script_table_ref.shape[0]
    pieces = pieces_ref[...].astype(F32).reshape(entries * slots, width)
    onehot = (scripts_ref[...] == lax.broadcasted_iota(jnp.int32, (1, groups), 1)).astype(F32)
    return pieces + jnp.dot(onehot, script_table_ref[...], precision=highest), onehot


def slot_weights(lengths, slots):
    rows = lengths.shape[0]
    slot = lax.broadcasted_iota(jnp.int32, (rows, 1), 0) % slots
    return jnp.where(slot <= lengths, 1.0 / (lengths + 1).astype(F32), 0.0)


def split_heads(pair):
    first = lax.broadcasted_iota(jnp.int32, pair.shape, 1) < HEAD_DIM
    zero = jnp.zeros_like(pair)
    return jnp.concatenate([jnp.where(first, pair, zero), jnp.where(first, zero, pair)], axis=0)


def join_heads(stacked):
    first = lax.broadcasted_iota(jnp.int32, (GROUP, PAIR), 1) < HEAD_DIM
    return jnp.where(first, stacked[:GROUP], stacked[GROUP:])


def attn_body(
    slots,
    pieces_ref,
    scripts_ref,
    lengths_ref,
    script_table_ref,
    gain_attn_ref,
    gain_ffn_ref,
    w_qkv_ref,
    w_out_ref,
    normed_ref,
    mixed_ref,
    context_ref,
    middle_ref,
    normed_ffn_ref,
):
    start, _ = start_of(pieces_ref, scripts_ref, script_table_ref)
    rows, width = start.shape
    lengths = lengths_ref[...]
    normed = (center(start)[0] * gain_attn_ref[...]).astype(BF16)
    normed_ref[...] = normed
    mixed = mm(normed, w_qkv_ref[...]).astype(BF16)
    mixed_ref[...] = mixed
    row = lax.broadcasted_iota(jnp.int32, (GROUP, GROUP), 0)
    col = lax.broadcasted_iota(jnp.int32, (GROUP, GROUP), 1)
    groups = []
    for base in range(0, rows, GROUP):
        part = mixed[base : base + GROUP]
        valid = (row // slots == col // slots) & (col % slots <= lengths[base : base + GROUP])
        lows = range(0, width, PAIR)
        raws = [
            nt(part[:, low : low + PAIR], split_heads(part[:, width + low : width + low + PAIR]))
            for low in lows
        ]
        heads = [raw[:, side : side + GROUP] for raw in raws for side in (0, GROUP)]
        heads = [jnp.where(valid, head * HEAD_DIM ** (-0.5), -1000000000.0) for head in heads]
        heads = [jnp.exp(head - jnp.max(head, axis=1, keepdims=True)) for head in heads]
        heads = [(head * (1.0 / jnp.sum(head, axis=1, keepdims=True))).astype(BF16) for head in heads]
        pairs = [
            mm(
                jnp.concatenate(heads[2 * j : 2 * j + 2], axis=1),
                split_heads(part[:, 2 * width + low : 2 * width + low + PAIR]),
            )
            for j, low in enumerate(lows)
        ]
        groups.append(jnp.concatenate(pairs, axis=1).astype(BF16))
    context = jnp.concatenate(groups, axis=0)
    context_ref[...] = context
    middle = start + mm(context, w_out_ref[...])
    middle_ref[...] = middle
    normed_ffn_ref[...] = (center(middle)[0] * gain_ffn_ref[...]).astype(BF16)


def attn_forward(
    line, pieces, scripts, lengths, script_table, gain_attn, gain_ffn, w_qkv, w_out
):
    entries, slots, width = pieces.shape
    total = entries * slots
    rows = math.gcd(total, 256)
    some = rows // slots
    whole = (script_table, gain_attn, gain_ffn, w_qkv, w_out)
    return line.run(
        functools.partial(attn_body, slots),
        "attn_forward",
        12,
        (total // rows,),
        [
            (pieces, pl.BlockSpec((some, slots, width), lambda i, *_: (i, 0, 0))),
            (scripts, rows_of(rows, 1)),
            (lengths, rows_of(rows, 1)),
        ]
        + [(value, fixed(value.shape)) for value in whole],
        [
            ((total, width), BF16, rows_of(rows, width)),
            ((total, 3 * width), BF16, rows_of(rows, 3 * width), FAR),
            ((total, width), BF16, rows_of(rows, width)),
            ((total, width), F32, rows_of(rows, width)),
            ((total, width), BF16, rows_of(rows, width)),
        ],
    )


def ffn_body(
    slots,
    last,
    length_rows_ref,
    lengths_ref,
    before_ref,
    normed_ref,
    w_up_ref,
    w_down_ref,
    slope_ref,
    hidden_ref,
    pooled_ref,
):
    rows, width = normed_ref.shape
    some = rows // slots
    row = lax.broadcasted_iota(jnp.int32, (some, rows), 1)
    entry = lax.broadcasted_iota(jnp.int32, (some, rows), 0)
    lengths = lengths_ref[...]
    valid = (row // slots == entry) & (row % slots <= lengths)
    valid = jnp.where(valid, 1.0, 0.0).astype(BF16)
    scale = 1.0 / (lengths + 1).astype(F32)
    pooled = before_ref[...]
    if not last:
        weights = slot_weights(length_rows_ref[...], slots)
        pooled = jnp.sum((pooled * weights).reshape(some, slots, width), axis=1)
    ff = w_up_ref.shape[1]
    step = ff // 2
    for low in range(0, ff, step):
        up = mm(normed_ref[...], w_up_ref[:, low : low + step])
        square = up * up
        tanh = jnp.tanh(up * (GELU_SCALE + GELU_SCALE * GELU_CUBE * square))
        half_up = 0.5 * up
        hidden = (half_up + half_up * tanh).astype(BF16)
        slope_ref[:, low : low + step] = (0.5 + 0.5 * tanh) + half_up * (1.0 - tanh * tanh) * (
            GELU_SCALE + 3.0 * GELU_SCALE * GELU_CUBE * square
        )
        mean_hidden = mm(valid, hidden) * scale
        high = mean_hidden.astype(BF16)
        rest = (mean_hidden - high.astype(F32)).astype(BF16)
        hidden_ref[:, low : low + step] = high
        w_down = w_down_ref[low : low + step]
        pooled += mm(high, w_down) + mm(rest, w_down)
    pooled_ref[...] = pooled.astype(pooled_ref.dtype)


def ffn_forward(line, length_rows, lengths, before, normed, w_up, w_down, last):
    total, width = normed.shape
    entries = lengths.shape[0]
    slots = total // entries
    rows = math.gcd(total, 256)
    some = rows // slots
    ff = w_up.shape[1] // 2
    return line.run(
        functools.partial(ffn_body, slots, last),
        "ffn_forward",
        7,
        (total // rows,),
        [
            (length_rows, rows_of(rows, 1)),
            (lengths, rows_of(some, 1)),
            (before, rows_of(some if last else rows, width)),
            (normed, rows_of(rows, width)),
            (w_up, pl.BlockSpec((width, ff), lambda i, *_: (0, int(last)))),
            (w_down, pl.BlockSpec((ff, width), lambda i, *_: (int(last), 0))),
        ],
        [
            ((total, ff), F32, rows_of(rows, ff), FAR),
            ((entries, ff), BF16, rows_of(some, ff)),
            ((entries, width), BF16 if last else F32, rows_of(some, width)),
        ],
    )


def ffn_back_body(
    slots,
    pooled_grad_ref,
    lengths_ref,
    slope_a_ref,
    slope_b_ref,
    middle_ref,
    gain_ffn_ref,
    w_up_ref,
    w_down_ref,
    grad_up_ref,
    grad_middle_ref,
    grad_branch_ref,
    gain_grad_ref,
):
    pooled_grad = pooled_grad_ref[...]
    rows, width = middle_ref.shape
    some = rows // slots
    wide = jnp.broadcast_to(pooled_grad[:, None, :], (some, slots, width)).reshape(rows, width)
    grad_final = wide * slot_weights(lengths_ref[...], slots)
    grad_ffn = grad_final.astype(BF16)
    ff = w_up_ref.shape[1]
    step = ff // 4
    grad_normed = jnp.zeros((rows, width), F32)
    for low in range(0, ff, step):
        grad_hidden = nt(grad_ffn, w_down_ref[low : low + step])
        slope_ref, inner = (slope_a_ref, low) if low < ff // 2 else (slope_b_ref, low - ff // 2)
        grad_up = (slope_ref[:, inner : inner + step] * grad_hidden).astype(BF16)
        grad_up_ref[:, low : low + step] = grad_up
        grad_normed += nt(grad_up, w_up_ref[:, low : low + step])
    unit, rate = center(middle_ref[...])
    grad, gain_grad = center_back(grad_normed, gain_ffn_ref[...], unit, rate)
    grad_middle = grad_final + grad
    grad_middle_ref[...] = grad_middle
    grad_branch_ref[...] = grad_middle.astype(BF16)

    @pl.when(pl.program_id(0) == 0)
    def _():
        gain_grad_ref[...] = jnp.zeros_like(gain_grad_ref)

    gain_grad_ref[...] += gain_grad


def ffn_back(line, pooled_grad, lengths, slopes, middle, gain_ffn, w_up, w_down):
    total, width = middle.shape
    entries = pooled_grad.shape[0]
    slots = total // entries
    rows = math.gcd(total, 256)
    some = rows // slots
    ff = w_up.shape[1]
    return line.run(
        functools.partial(ffn_back_body, slots),
        "ffn_back",
        15,
        (total // rows,),
        [
            (pooled_grad, rows_of(some, width)),
            (lengths, rows_of(rows, 1)),
            *((slope, rows_of(rows, ff // 2)) for slope in slopes),
            (middle, rows_of(rows, width)),
            (gain_ffn, fixed(gain_ffn.shape)),
            (w_up, fixed(w_up.shape)),
            (w_down, fixed(w_down.shape)),
        ],
        [
            ((total, ff), BF16, rows_of(rows, ff)),
            ((total, width), F32, rows_of(rows, width)),
            ((total, width), BF16, rows_of(rows, width)),
            ((1, width), F32, fixed((1, width))),
        ],
    )


def heads_back_body(slots, lengths_ref, w_out_ref, mixed_ref, grad_branch_ref, grad_mixed_ref):
    rows, width = grad_branch_ref.shape
    lengths = lengths_ref[...]
    grad_ctx = nt(grad_branch_ref[...], w_out_ref[...]).astype(BF16)
    row = lax.broadcasted_iota(jnp.int32, (GROUP, GROUP), 0)
    col = lax.broadcasted_iota(jnp.int32, (GROUP, GROUP), 1)
    same = row // slots == col // slots
    lows = range(0, width, PAIR)
    for base in range(0, rows, GROUP):
        span = slice(base, base + GROUP)
        valid = same & (row % slots <= lengths[span])
        queries = [mixed_ref[span, low : low + PAIR] for low in lows]
        keys = [split_heads(mixed_ref[span, width + low : width + low + PAIR]) for low in lows]
        values = [split_heads(mixed_ref[span, 2 * width + low : 2 * width + low + PAIR]) for low in lows]
        grad_pairs = [grad_ctx[span, low : low + PAIR] for low in lows]
        raws = [nt(key, query) for key, query in zip(keys, queries)]
        grad_raws = [nt(value, grad_pair) for value, grad_pair in zip(values, grad_pairs)]
        sides = (slice(0, GROUP), slice(GROUP, 2 * GROUP))
        heads = [raw[side] for raw in raws for side in sides]
        heads = [jnp.where(valid, head * HEAD_DIM ** (-0.5), -1000000000.0) for head in heads]
        heads = [jnp.exp(head - jnp.max(head, axis=0, keepdims=True)) for head in heads]
        probs = [head * (1.0 / jnp.sum(head, axis=0, keepdims=True)) for head in heads]
        grads = [grad_raw[side] for grad_raw in grad_raws for side in sides]
        grads = [
            prob * (grad - jnp.sum(grad * prob, axis=0, keepdims=True)) for prob, grad in zip(probs, grads)
        ]
        probs = [prob.astype(BF16) for prob in probs]
        grads = [(grad * HEAD_DIM ** (-0.5)).astype(BF16) for grad in grads]
        for j, low in enumerate(lows):
            scores_grad = jnp.concatenate(grads[2 * j : 2 * j + 2], axis=0)
            prob = jnp.concatenate(probs[2 * j : 2 * j + 2], axis=0)
            grad_mixed_ref[span, low : low + PAIR] = tn(scores_grad, keys[j]).astype(BF16)
            grad_keys = join_heads(mm(scores_grad, queries[j]))
            grad_mixed_ref[span, width + low : width + low + PAIR] = grad_keys.astype(BF16)
            grad_values = join_heads(mm(prob, grad_pairs[j]))
            grad_mixed_ref[span, 2 * width + low : 2 * width + low + PAIR] = grad_values.astype(BF16)


def heads_back(line, lengths, w_out, mixed, grad_branch, slots):
    total, width = grad_branch.shape
    rows = math.gcd(total, 256)
    return line.run(
        functools.partial(heads_back_body, slots),
        "heads_back",
        13,
        (total // rows,),
        [
            (lengths, rows_of(rows, 1)),
            (w_out, fixed(w_out.shape)),
            (mixed, rows_of(rows, 3 * width)),
            (grad_branch, rows_of(rows, width)),
        ],
        [((total, 3 * width), BF16, rows_of(rows, 3 * width))],
    )[0]


def attn_back_body(
    pieces_ref,
    scripts_ref,
    script_table_ref,
    gain_attn_ref,
    w_qkv_ref,
    grad_mixed_ref,
    grad_middle_ref,
    gain_ffn_grad_ref,
    grad_pieces_ref,
    small_ref,
):
    start, onehot = start_of(pieces_ref, scripts_ref, script_table_ref)
    grad_normed = nt(grad_mixed_ref[...], w_qkv_ref[...])
    unit, rate = center(start)
    grad, gain_grad = center_back(grad_normed, gain_attn_ref[...], unit, rate)
    grad_pieces = grad_middle_ref[...] + grad
    grad_pieces_ref[...] = grad_pieces.reshape(grad_pieces_ref.shape)

    groups = onehot.shape[1]

    @pl.when(pl.program_id(0) == 0)
    def _():
        small_ref[...] = jnp.zeros_like(small_ref)
        small_ref[groups + 1 : groups + 2] = gain_ffn_grad_ref[...]

    small_ref[groups : groups + 1] += gain_grad
    small_ref[:groups] += lax.dot_general(
        onehot, grad_pieces, (((0,), (0,)), ((), ())), precision=highest
    )


def attn_back(
    line, pieces, scripts, script_table, gain_attn, w_qkv, grad_mixed, grad_middle, gain_ffn_grad
):
    entries, slots, width = pieces.shape
    total = entries * slots
    rows = math.gcd(total, 256)
    some = rows // slots
    small = ((script_table.shape[0] + 2 + 15) // 16 * 16, width)
    return line.run(
        attn_back_body,
        "attn_back",
        9,
        (total // rows,),
        [
            (pieces, pl.BlockSpec((some, slots, width), lambda i, *_: (i, 0, 0))),
            (scripts, rows_of(rows, 1)),
            (script_table, fixed(script_table.shape)),
            (gain_attn, fixed(gain_attn.shape)),
            (w_qkv, fixed(w_qkv.shape)),
            (grad_mixed, rows_of(rows, 3 * width)),
            (grad_middle, rows_of(rows, width)),
            (gain_ffn_grad, fixed(gain_ffn_grad.shape)),
        ],
        [
            ((entries, slots, width), F32, pl.BlockSpec((some, slots, width), lambda i, *_: (i, 0, 0)), FAR),
            (small, F32, fixed(small)),
        ],
    )


PLAN = ("f t T f", "03 t f", "36 t f", "68 t f t", "w t E F", "Q")


def per_device(
    pieces,
    lengths,
    scripts,
    script_table,
    gain_attn,
    gain_ffn,
    w_qkv,
    w_out,
    w_up,
    w_down,
    w_proj,
    token_ids,
    out_grad,
):
    entries, slots, width = pieces.shape
    ent_count = lax.axis_size("ent")
    rep_count = lax.axis_size("rep")
    devices = ent_count * rep_count
    features = w_proj.shape[1]
    vocab = entries * devices
    rows_dev, text_len = token_ids.shape
    tokens = rows_dev * text_len
    levels = make_levels(ent_count, rep_count)
    sizes = tuple(size for _, size, _ in levels)
    me = lax.axis_index("ent") * rep_count + lax.axis_index("rep")
    chunks = 1 if devices <= 32 else 8
    each = entries // chunks
    span = vocab // chunks
    slot = slot_of(token_ids // entries ^ me, levels)
    within = token_ids % entries
    slot_ids = within // each * span + slot * each + within % each
    script_rows = jnp.repeat(scripts, slots)[:, None]
    length_rows = jnp.repeat(lengths, slots)[:, None]
    gain_attn, gain_ffn = gain_attn[None], gain_ffn[None]

    cut = len(levels)
    while math.prod(sizes[:cut]) * 16 > w_down.shape[0]:
        cut -= 1
    near, far = levels[:cut], levels[cut:]
    count = math.prod(sizes[:cut])
    slot_index = jnp.arange(count, dtype=jnp.int32) ^ slot_of(me, near)
    line = Line()

    def cut_up(keep, send, some):
        shape = tuple(size for _, size, _ in some[1:]) + keep.shape[-2:]
        return keep.reshape(shape), send.reshape(shape)

    parts, pooled_grads = [], []
    for chunk in range(chunks):
        first = chunk * span
        part_send, send = scatter_rows(
            line, slot_ids, out_grad, w_proj, first + span // 2, span // 2, BF16
        )
        part_keep, keep = scatter_rows(line, slot_ids, out_grad, w_proj, first, span // 2, F32)
        parts.append((part_keep, part_send))
        shape = sizes[1:] + (each, width)
        pooling = sum_halves(line, keep.reshape(shape), send.reshape(shape), levels, pooled_grads)
        if chunks > 1:
            for _ in pooling:
                pass
    next(pooling, None)
    next(pooling, None)
    normed, mixed, context, middle, normed_ffn = attn_forward(
        line, pieces, script_rows, length_rows, script_table, gain_attn, gain_ffn, w_qkv, w_out
    )
    next(pooling, None)
    length_cols = lengths[:, None]
    slope_a, hidden_a, pooled = ffn_forward(
        line, length_rows, length_cols, middle, normed_ffn, w_up, w_down, False
    )
    next(pooling, None)
    slope_b, hidden_b, pooled = ffn_forward(
        line, length_rows, length_cols, pooled, normed_ffn, w_up, w_down, True
    )
    for _ in pooling:
        pass
    grad_pooled = jnp.concatenate(pooled_grads, axis=0) if chunks > 1 else pooled_grads[0]

    held = [((), each, width, BF16, lambda index: [(0, (), ALL, 0, 0)])]
    halves = [[] for _ in range(chunks)]
    spreads = [
        gather_halves(
            line, stage(line, [(pooled[chunk * each :][:each], [])], held)[0], levels, halves[chunk]
        )
        for chunk in range(chunks)
    ]

    def spread_on():
        if chunks == 1:
            next(spreads[0])

    spread_on()
    down = tall_weight(line, slot_index, (hidden_a, hidden_b), grad_pooled.astype(BF16))
    grad_up, grad_middle, grad_branch, part_gain_ffn = ffn_back(
        line, grad_pooled, length_rows, (slope_a, slope_b), middle, gain_ffn, w_up, w_down
    )
    spread_on()
    up = wide_weight(line, slot_index, normed_ffn, grad_up)
    small, ffn_all, two_all = [], [], []
    ffn_sum = all_sum_two(
        line, *cut_up(*down, near), *cut_up(*up, near), lambda: small[0], near, far, ffn_all
    )
    next(ffn_sum)
    spread_on()
    grad_mixed = heads_back(line, length_rows, w_out, mixed, grad_branch, slots)
    next(ffn_sum)
    two = two_weights(line, slot_index, normed, grad_mixed, context, grad_branch)
    two_sum = all_sum(line, *cut_up(*two, near), near, far, two_all)
    next(two_sum)
    spread_on()
    grad_pieces, part_small = attn_back(
        line,
        pieces,
        script_rows,
        script_table,
        gain_attn,
        w_qkv,
        grad_mixed,
        grad_middle,
        part_gain_ffn,
    )
    small.append(part_small)
    results = {}

    def make_table():
        tables, total = [], None
        for chunk in range(chunks):
            for _ in spreads[chunk]:
                pass
            own, other = (value.reshape(span // 2, width) for value in halves[chunk])
            table, part = table_and_grad(line, own, other, w_proj, *parts[chunk])
            tables.append(table)
            total = part if total is None else total + part
        results["tables"] = tables
        results["proj"] = total, swap(total, levels[0])

    def look_up(first, last):
        before = results.get("looked_up")
        results["looked_up"] = lookup(line, slot_ids, results["tables"], (first, last), before)

    def add_proj():
        total, other = results["proj"]
        whole = [((), width, features, F32, lambda index: [(0, (), ALL, 0, 0)])]
        results["w_proj"] = stage(line, [(total, [other])], whole)[0]

    def end_ffn():
        results["w_down"] = unpack(line, slot_index, *map(merge, ffn_all[:2]), w_down.shape[0])
        results["w_up"], *results["small"] = unpack_extra(
            line,
            slot_index,
            *map(merge, ffn_all[2:]),
            *w_up.shape,
            (script_table.shape[0], 1, 1),
            math.prod(sizes[3:cut]),
        )

    def end_two():
        for _ in two_sum:
            pass
        results["w_qkv"], results["w_out"] = unpack_two(
            line, slot_index, *map(merge, two_all), *w_qkv.shape
        )

    acts = {
        "f": lambda: next(ffn_sum, 0),
        "t": lambda: next(two_sum, 0),
        "T": make_table,
        "w": add_proj,
        "E": lambda: list(ffn_sum),
        "F": end_ffn,
        "Q": end_two,
    }
    for act in (act for part in PLAN for act in part.split()):
        if act.isdigit():
            look_up(int(act[0]), int(act[1]))
        else:
            acts[act]()
    looked_up, grad_w_proj = results["looked_up"], results["w_proj"]
    grad_w_down, grad_w_up = results["w_down"], results["w_up"]
    grad_w_qkv, grad_w_out = results["w_qkv"], results["w_out"]
    grad_script, grad_gain_attn, grad_gain_ffn = results["small"]
    return (
        looked_up,
        grad_pieces,
        grad_script,
        grad_gain_attn.reshape(width),
        grad_gain_ffn.reshape(width),
        grad_w_qkv,
        grad_w_out,
        grad_w_up,
        grad_w_down,
        grad_w_proj,
    )


def solution(mesh):
    in_specs = (
        P(("ent", "rep"), None, None),
        P(("ent", "rep")),
        P(("ent", "rep")),
        P(),
        P(),
        P(),
        P(),
        P(),
        P(),
        P(),
        P(None, "ent"),
        P("rep", None),
        P("ent", "rep", None),
    )
    out_specs = (
        P("ent", "rep", None),
        P(("ent", "rep"), None, None),
        P(),
        P(),
        P(),
        P(),
        P(),
        P(),
        P(),
        P(None, "ent"),
    )
    return jax.shard_map(
        per_device, mesh=mesh, in_specs=in_specs, out_specs=out_specs, check_vma=False
    )
```

```python
import functools
import math

import jax
import jax.numpy as jnp
import numpy as np
from jax import lax
from jax.experimental import pallas as pl
from jax.experimental.pallas import tpu as pltpu
from jax.sharding import PartitionSpec as P

HEADS = 8
HEAD_DIM = 64
F32 = jnp.float32
BF16 = jnp.bfloat16
highest = lax.Precision.HIGHEST
MIB = 1024 * 1024


def make_levels(ent_count, rep_count):
    levels = [("rep", rep_count, 0)]
    bit, total = 0, ent_count.bit_length() - 1
    while bit < total:
        width = 1 if bit < 2 else min(2, total - bit)
        levels.append(("ent", 1 << width, bit))
        bit += width
    return levels


def slot_of(number, levels):
    rep_count = levels[0][1]
    slot = number % rep_count
    ent = number // rep_count
    for _, size, shift in levels[1:]:
        slot = slot * size + (ent >> shift) % size
    return slot


def swap(value, level, k):
    name, size, shift = level
    count = lax.axis_size(name)
    return lax.ppermute(value, name, [(i, i ^ (k << shift)) for i in range(count)])


def merge(value):
    return value.reshape((-1,) + value.shape[-2:])


FAR = True


class Line:
    def __init__(self):
        self.last = []

    def run(self, body, name, micros, grid, ins, outs, prefetch=(), alias=None, room=24 * MIB, scratch=()):
        count = len(prefetch) + len(ins)
        extra = self.last + ([] if alias is None else [alias])
        token = (8, 128)

        def wrapped(*refs):
            held = len(refs) - len(scratch)
            refs[held - 1][...] = jnp.zeros(token, F32)
            body(*refs[:count], *refs[count + len(extra) : held - 1], *refs[held:])

        *results, last = pl.pallas_call(
            wrapped,
            grid_spec=pltpu.PrefetchScalarGridSpec(
                num_scalar_prefetch=len(prefetch),
                grid=grid,
                in_specs=[spec for _, spec in ins] + [pl.BlockSpec(memory_space=pl.ANY)] * len(extra),
                out_specs=[spec for _, _, spec, *_ in outs] + [pl.BlockSpec(token, lambda *_: (0, 0))],
                scratch_shapes=scratch,
            ),
            out_shape=[
                pltpu.HBM(shape, dtype) if far else jax.ShapeDtypeStruct(shape, dtype)
                for shape, dtype, _, *far in outs
            ]
            + [jax.ShapeDtypeStruct(token, F32)],
            input_output_aliases={} if alias is None else {count + len(extra) - 1: 0},
            compiler_params=pltpu.CompilerParams(vmem_limit_bytes=room),
            cost_estimate=pl.CostEstimate(
                flops=int(micros * 3e9), bytes_accessed=int(micros * 9e6), transcendentals=0
            ),
            name=name,
        )(*prefetch, *(value for value, _ in ins), *extra)
        self.last = [last]
        return results


def swap(value, level, k=1):
    name, size, shift = level
    count = lax.axis_size(name)
    return lax.ppermute(value, name, [(i, i ^ (k << shift)) for i in range(count)])


def swaps(values, level):
    return [swap(value, level, k) for k, value in enumerate(values, 1)]


ALL = slice(None)
BELOW = 16


def stage_body(layout, cuts, *refs):
    sums, position = [], 0
    for number in layout:
        sums.append(refs[position : position + number])
        position += number

    def piece(number, index, cols, rows=ALL):
        total = sums[number][0][index][rows, cols]
        for ref in sums[number][1:]:
            total = total.astype(F32) + ref[index][rows, cols].astype(F32)
        return total

    for out_ref, sources in zip(refs[position:], cuts):
        for target, parts in sources:
            for number, index, cols, row, col, *rows in parts:
                value = piece(number, index, cols, *rows).astype(out_ref.dtype)
                where = target + (slice(row, row + value.shape[0]), slice(col, col + value.shape[1]))
                out_ref[where] = value


def stage(line, sums, outs, steps=1):
    values = [value for kept, received in sums for value in [kept, *received]]

    def spec(shape):
        return pl.BlockSpec(memory_space=pltpu.VMEM)

    cuts = [
        [(target, source(target)) for target in np.ndindex(*lead)] for lead, _, _, _, source in outs
    ]
    shapes = [(lead + (rows, cols), dtype) for lead, rows, cols, dtype, _ in outs]
    held = [(value.shape, value.dtype) for value in values] + [(shape, jnp.dtype(dtype)) for shape, dtype in shapes]
    return line.run(
        functools.partial(stage_body, [1 + len(received) for _, received in sums], cuts),
        "exchange",
        0.5,
        (),
        [(value, spec(value.shape)) for value in values],
        [(shape, dtype, spec(shape)) for shape, dtype in shapes],
        room=2 * MIB + sum(math.prod(shape) * dtype.itemsize for shape, dtype in held),
    )


def split(number, value, axis, cols=ALL, width=None):
    lead = value.shape[:-2]
    rest = lead[:axis] + lead[axis + 1 :]
    outs = []
    for k in range(lead[axis]):

        def source(index, k=k):
            return [(number, index[:axis] + (k,) + index[axis:], cols, 0, 0)]

        outs.append((rest, value.shape[-2], width or value.shape[-1], F32 if k == 0 else BF16, source))
    return outs


def stacked(numbers, value, axis, rows=ALL):
    lead = value.shape[:-2]
    shape = lead[:axis] + (len(numbers),) + lead[axis:]

    def source(index):
        return [(numbers[index[axis]], index[:axis] + index[axis + 1 :], ALL, 0, 0)]

    return (shape, value.shape[-2], value.shape[-1], value.dtype, source)


def finish(line, sums, far, shape, dtype):
    whole = [(0, (), ALL, 0, 0)]
    for level in far:
        outs = [((), *shape, kind, lambda index: whole) for kind in (F32, BF16)]
        keep, send = stage(line, sums, outs)
        sums = [(keep, [swap(send, level, k) for k in range(1, level[1])])]
        yield
    yield stage(line, sums, [((), *shape, dtype, lambda index: whole)])[0]


def sum_halves(line, keep, send, levels, out, far=(), dtype=F32):
    received = swap(send, levels[0])
    yield
    rows, width = keep.shape[-2:]
    half = width // 2
    left, right = slice(0, half), slice(half, width)
    steps = 4 if rows % 64 == 0 else 1
    outs = split(0, keep, 0, left, half) + split(0, keep, 1, right, half)
    keep_a, send_a, keep_b, send_b = stage(line, [(keep, [received])], outs, steps)
    got_a, got_b = swap(send_a, levels[1]), swap(send_b, levels[2])
    yield
    outs = split(0, keep_a, 0) + split(1, keep_b, 0)
    sums = [(keep_a, [got_a]), (keep_b, [got_b])]
    keep_a, send_a, keep_b, send_b = stage(line, sums, outs, steps)
    sums = [(keep_a, [swap(send_a, levels[2])]), (keep_b, [swap(send_b, levels[1])])]
    yield
    for place, level in enumerate(levels[3:]):
        if place == 0:
            lead = keep_a.shape[1:-2]

            def source(index, k):
                return [(0, (k,) + index, ALL, 0, 0), (1, (k,) + index, ALL, 0, half)]

            outs = [
                (lead, rows, width, F32 if k == 0 else BF16, functools.partial(source, k=k))
                for k in range(level[1])
            ]
        else:
            outs = split(0, keep, 0)
        keep, *sends = stage(line, sums, outs)
        sums = [(keep, swaps(sends, level))]
        yield
    for value in finish(line, sums, far, (rows, width), dtype):
        if value is None:
            yield
    out.append(value)


def gather_halves(line, value, levels, out):
    rows, width = value.shape
    half = width // 2
    for place, level in reversed(list(enumerate(levels[3:]))):
        got = [swap(value, level, k) for k in range(1, level[1])]
        yield
        parts = [(part, []) for part in [value, *got]]
        numbers = list(range(level[1]))
        if place:
            value = stage(line, parts, [stacked(numbers, value, 0)])[0]
        else:
            lead = (level[1],) + value.shape[:-2]

            def source(index, cols):
                return [(index[0], index[1:], cols, 0, 0)]

            outs = [
                (lead, rows, half, BF16, functools.partial(source, cols=cols))
                for cols in (slice(0, half), slice(half, width))
            ]
            value_a, value_b = stage(line, parts, outs)
    got_a, got_b = swap(value_a, levels[2]), swap(value_b, levels[1])
    yield
    sums = [(part, []) for part in (value_a, got_a, value_b, got_b)]
    outs = [stacked([0, 1], value_a, 0), stacked([2, 3], value_b, 0)]
    value_a, value_b = stage(line, sums, outs)
    got_a, got_b = swap(value_a, levels[1]), swap(value_b, levels[2])
    yield
    sums = [(part, []) for part in (value_a, got_a, value_b, got_b)]
    lead = (2,) + value_a.shape[:-2]

    def joined(index):
        left, right = index[0], index[1]
        return [(left, index[1:], ALL, 0, 0), (2 + right, (left,) + index[2:], ALL, 0, half)]

    value = stage(line, sums, [(lead, rows, width, BF16, joined)])[0]
    out += [value, swap(value, levels[0])]
    yield


def all_sum(line, keep, send, near, far, out):
    mine = []
    yield from sum_halves(line, keep, send, near, mine, far, BF16)
    yield from gather_halves(line, mine[0], near, out)


def all_sum_two(line, keep_a, send_a, keep_b, send_b, extra, near, far, out):
    got_a, got_b = swap(send_a, near[0]), swap(send_b, near[0])
    yield
    rows = keep_a.shape[-2]
    outs = split(0, keep_a, 0) + split(1, keep_b, 1)
    keep_a, send_a, keep_b, send_b = stage(line, [(keep_a, [got_a]), (keep_b, [got_b])], outs)
    got_a, got_b = swap(send_a, near[1]), swap(send_b, near[2])
    yield
    outs = split(0, keep_a, 0) + split(1, keep_b, 0)
    keep_a, send_a, keep_b, send_b = stage(line, [(keep_a, [got_a]), (keep_b, [got_b])], outs)
    sums = [(keep_a, [swap(send_a, near[2])]), (keep_b, [swap(send_b, near[1])])]
    yield
    below = extra()
    added = below.shape[0]
    for place, level in enumerate(near[3:]):
        if place == 0:
            lead = keep_a.shape[1:-2]
            sums = sums + [(below, [])]

            def source(index, k):
                places = [(0, (k,) + index, 0), (1, (k,) + index, rows), (2, (), 2 * rows)]
                return [(number, where, ALL, row, 0) for number, where, row in places]

            outs = [
                (lead, 2 * rows + added, PANEL, F32 if k == 0 else BF16, functools.partial(source, k=k))
                for k in range(level[1])
            ]
        else:
            outs = split(0, keep, 0)
        keep, *sends = stage(line, sums, outs)
        sums = [(keep, swaps(sends, level))]
        yield
    for level in far:
        outs = [((), 2 * rows + added, PANEL, kind, lambda index: [(0, (), ALL, 0, 0)]) for kind in (F32, BF16)]
        keep, send = stage(line, sums, outs)
        sums = [(keep, [swap(send, level, k) for k in range(1, level[1])])]
        yield
    outs = [
        ((), size, PANEL, BF16, lambda index, part=part: [(0, (), ALL, 0, 0, part)])
        for size, part in ((2 * rows, slice(0, 2 * rows)), (added, slice(2 * rows, 2 * rows + added)))
    ]
    value, below = stage(line, sums, outs)
    for place, level in reversed(list(enumerate(near[3:]))):
        got = [swap(value, level, k) for k in range(1, level[1])]
        yield
        numbers = list(range(level[1]))
        parts = [(part, []) for part in [value, *got]]
        if place:
            value = stage(line, parts, [stacked(numbers, value, 0)])[0]
            continue
        lead = (level[1],) + value.shape[:-2]

        def first(index):
            return [(index[0], index[1:], ALL, 0, 0, slice(0, rows))]

        def second(index):
            number = int(np.ravel_multi_index(index, lead)) * BELOW % added
            return [
                (index[0], index[1:], ALL, 0, 0, slice(rows, 2 * rows)),
                (len(numbers), (), ALL, rows, 0, slice(number, number + BELOW)),
            ]

        outs = [(lead, rows, PANEL, BF16, first), (lead, rows + BELOW, PANEL, BF16, second)]
        value_a, value_b = stage(line, parts + [(below, [])], outs)
    got_a, got_b = swap(value_a, near[2]), swap(value_b, near[1])
    yield
    sums = [(part, []) for part in (value_a, got_a, value_b, got_b)]
    outs = [stacked([0, 1], value_a, 0), stacked([2, 3], value_b, 0)]
    value_a, value_b = stage(line, sums, outs)
    got_a, got_b = swap(value_a, near[1]), swap(value_b, near[2])
    yield
    sums = [(part, []) for part in (value_a, got_a, value_b, got_b)]
    outs = [stacked([0, 1], value_a, 0), stacked([2, 3], value_b, 1)]
    value_a, value_b = stage(line, sums, outs)
    out += [value_a, swap(value_a, near[0]), value_b, swap(value_b, near[0])]
    yield


def fixed(shape):
    return pl.BlockSpec(shape, lambda i, *_: (0,) * len(shape))


def rows_of(rows, width):
    return pl.BlockSpec((rows, width), lambda i, *_: (i, 0))


def selector(ids, base, rows):
    entry = lax.broadcasted_iota(jnp.int32, (rows, 1), 0).astype(jnp.int16)
    return jnp.where(entry == (ids - base).astype(jnp.int16), jnp.ones((), BF16), jnp.zeros((), BF16))


def nt(left, right):
    return lax.dot_general(left, right, (((1,), (1,)), ((), ())), preferred_element_type=F32)


def tn(left, right):
    return lax.dot_general(left, right, (((0,), (0,)), ((), ())), preferred_element_type=F32)


def mm(left, right):
    return jnp.dot(left, right, preferred_element_type=F32)


def scatter_body(first, ids_ref, grad_ref, proj_ref, table_ref, pooled_ref, flat_ref):
    @pl.when(pl.program_id(0) == 0)
    def _():
        flat_ref[...] = grad_ref[...].reshape(flat_ref.shape)

    rows = table_ref.shape[0]
    some = min(256, rows)
    parts = []
    for low in range(0, rows, some):
        base = first + pl.program_id(0) * rows + low
        picks = [selector(ids_ref[row : row + 1], base, some) for row in range(ids_ref.shape[0])]
        parts.append(nt(jnp.concatenate(picks, axis=1), flat_ref[...]))
    part = jnp.concatenate(parts, axis=0).astype(BF16)
    table_ref[...] = part
    pooled_ref[...] = nt(part, proj_ref[...]).astype(pooled_ref.dtype)


def scatter_rows(line, ids, grad, w_proj, first, count, dtype):
    features = grad.shape[0]
    width = w_proj.shape[0]
    rows = min(1024, count)
    return line.run(
        functools.partial(scatter_body, first),
        "scatter_rows",
        14,
        (count // rows,),
        [
            (ids, fixed(ids.shape)),
            (grad, pl.BlockSpec(memory_space=pltpu.VMEM)),
            (w_proj, fixed(w_proj.shape)),
        ],
        [
            ((count, features), BF16, rows_of(rows, features), FAR),
            ((count, width), dtype, rows_of(rows, width)),
        ],
        room=28 * MIB,
        scratch=[pltpu.VMEM((features, ids.size), BF16)],
    )


def table_body(steps, own_ref, other_ref, proj_ref, part_own_ref, part_other_ref, table_ref, grad_ref):
    step = pl.program_id(0)

    @pl.when(step == 0)
    def _():
        grad_ref[...] = jnp.zeros_like(grad_ref)

    def one(pooled_ref, part_ref):
        pooled = pooled_ref[...]
        cols = lax.dot_general(
            proj_ref[...], pooled, (((0,), (1,)), ((), ())), preferred_element_type=F32
        )
        table_ref[...] = cols.astype(BF16)
        grad_ref[...] += tn(pooled, part_ref[...])

    @pl.when(step < steps)
    def _():
        one(own_ref, part_own_ref)

    @pl.when(step >= steps)
    def _():
        one(other_ref, part_other_ref)


def table_and_grad(line, own, other, w_proj, part_own, part_other):
    count, width = own.shape
    features = w_proj.shape[1]
    rows = min(1024, count)
    steps = count // rows

    def first(cols):
        return pl.BlockSpec((rows, cols), lambda i, *_: (jnp.minimum(i, steps - 1), 0))

    def second(cols):
        return pl.BlockSpec((rows, cols), lambda i, *_: (jnp.maximum(i - steps, 0), 0))

    return line.run(
        functools.partial(table_body, steps),
        "table_and_grad",
        5,
        (2 * steps,),
        [
            (own, first(width)),
            (other, second(width)),
            (w_proj, fixed(w_proj.shape)),
            (part_own, first(features)),
            (part_other, second(features)),
        ],
        [
            ((features, 2 * count), BF16, pl.BlockSpec((features, rows), lambda i, *_: (0, i))),
            ((width, features), F32, fixed((width, features))),
        ],
    )


def lookup_body(chunk, ids_ref, *refs):
    table_refs, out_ref = refs[:-1], refs[-1]
    rows = ids_ref.shape[0]

    def find(base, table):
        picks = [selector(ids_ref[row : row + 1], base, chunk) for row in range(rows)]
        return mm(table, jnp.concatenate(picks, axis=1))

    total = None
    for index, table_ref in enumerate(table_refs):
        vocab = table_ref.shape[1]
        for inner in range(0, vocab, chunk):
            part = find(index * vocab + inner, table_ref[:, inner : inner + chunk])
            total = part if total is None else total + part
    out_ref[...] = total.astype(BF16).reshape(out_ref.shape)


def lookup(line, ids, tables, part, before=None):
    rows, text_len = ids.shape
    features, vocab = tables[0].shape
    block = text_len // 8
    first, last = part
    return line.run(
        functools.partial(lookup_body, min(vocab, 4096)),
        "lookup",
        3 * (last - first),
        (last - first,),
        [(ids, pl.BlockSpec((rows, block), lambda i, *_: (0, i + first)))]
        + [(table, fixed(table.shape)) for table in tables],
        [
            (
                (features, rows, text_len),
                BF16,
                pl.BlockSpec((features, rows, block), lambda i, *_: (0, 0, i + first)),
                FAR,
            )
        ],
        alias=before,
    )[0]


PANEL = 512


def store_slots(slots_ref, first, part, keep_ref, send_ref):
    half, rows, _ = keep_ref.shape
    for j in range(part.shape[0] // rows):
        slot = slots_ref[first + j]
        piece = part[j * rows : (j + 1) * rows]

        @pl.when(slot < half)
        def _():
            keep_ref[slot] = piece

        @pl.when(slot >= half)
        def _():
            send_ref[slot - half] = piece.astype(BF16)


def weight_body(slots_ref, left_ref, right_ref, keep_ref, send_ref):
    part = tn(left_ref[...], right_ref[...])
    store_slots(slots_ref, pl.program_id(0) * (part.shape[0] // keep_ref.shape[1]), part, keep_ref, send_ref)


def tall_body(steps, slots_ref, first_ref, second_ref, right_ref, keep_ref, send_ref):
    step = pl.program_id(0)
    each = PANEL // keep_ref.shape[1]

    @pl.when(step < steps)
    def _():
        store_slots(slots_ref, step * each, tn(first_ref[...], right_ref[...]), keep_ref, send_ref)

    @pl.when(step >= steps)
    def _():
        store_slots(slots_ref, step * each, tn(second_ref[...], right_ref[...]), keep_ref, send_ref)


def two_weights_body(last, slots_ref, left_ref, right_ref, left2_ref, right2_ref, keep_ref, send_ref):
    step = pl.program_id(0)
    each = left_ref.shape[1] // keep_ref.shape[1]

    @pl.when(step < last)
    def _():
        store_slots(slots_ref, step * each, tn(left_ref[...], right_ref[...]), keep_ref, send_ref)

    @pl.when(step == last)
    def _():
        store_slots(slots_ref, step * each, tn(left2_ref[...], right2_ref[...]), keep_ref, send_ref)


def slot_outs(count, rows):
    shape = (count // 2, rows, PANEL)
    return [(shape, F32, fixed(shape)), (shape, BF16, fixed(shape))]


def panel_of(depth):
    return pl.BlockSpec((depth, PANEL), lambda i, *_: (0, i))


def tall_weight(line, slots, lefts, right):
    depth, half = lefts[0].shape
    steps = half // PANEL
    return line.run(
        functools.partial(tall_body, steps),
        "tall_weight",
        3,
        (2 * steps,),
        [
            (lefts[0], pl.BlockSpec((depth, PANEL), lambda i, *_: (0, jnp.minimum(i, steps - 1)))),
            (lefts[1], pl.BlockSpec((depth, PANEL), lambda i, *_: (0, jnp.maximum(i - steps, 0)))),
            (right, fixed(right.shape)),
        ],
        slot_outs(slots.shape[0], 2 * half // slots.shape[0]),
        [slots],
    )


def wide_weight(line, slots, left, right):
    depth, cols = right.shape
    return line.run(
        weight_body,
        "wide_weight",
        8,
        (cols // PANEL,),
        [(left, fixed(left.shape)), (right, panel_of(depth))],
        slot_outs(slots.shape[0], cols // PANEL * left.shape[1] // slots.shape[0]),
        [slots],
    )


def two_weights(line, slots, left, right, left2, right2):
    depth, cols = right.shape
    last = cols // PANEL
    return line.run(
        functools.partial(two_weights_body, last),
        "two_weights",
        5,
        (last + 1,),
        [
            (left, fixed(left.shape)),
            (right, pl.BlockSpec((depth, PANEL), lambda i, *_: (0, jnp.minimum(i, last - 1)))),
            (left2, fixed(left2.shape)),
            (right2, fixed(right2.shape)),
        ],
        slot_outs(slots.shape[0], (last + 1) * left.shape[1] // slots.shape[0]),
        [slots],
    )


def load_slots(slots_ref, first, own_ref, other_ref, out_ref, rows):
    half = own_ref.shape[0]
    for j in range(out_ref.shape[0] // rows):
        slot = slots_ref[first + j]

        @pl.when(slot < half)
        def _():
            out_ref[j * rows : (j + 1) * rows] = own_ref[slot, :rows].astype(F32)

        @pl.when(slot >= half)
        def _():
            out_ref[j * rows : (j + 1) * rows] = other_ref[slot - half, :rows].astype(F32)


def unpack_body(slots_ref, own_ref, other_ref, out_ref):
    rows = own_ref.shape[1]
    each = out_ref.shape[0] // rows
    load_slots(slots_ref, pl.program_id(0) * each, own_ref, other_ref, out_ref, rows)


def unpack(line, slots, own, other, height):
    tile = min(512, height)
    return line.run(
        unpack_body,
        "unpack",
        5,
        (height // tile,),
        [(own, fixed(own.shape)), (other, fixed(other.shape))],
        [((height, PANEL), F32, pl.BlockSpec((tile, PANEL), lambda i, *_: (i, 0)), FAR)],
        [slots],
    )[0]


def unpack_extra_body(rows, inner, slots_ref, own_ref, other_ref, out_ref, *extra_refs):
    each = out_ref.shape[0] // rows
    load_slots(slots_ref, pl.program_id(0) * each, own_ref, other_ref, out_ref, rows)

    @pl.when(pl.program_id(0) == 0)
    def _():
        needed = sum(ref.shape[0] for ref in extra_refs)
        sums = []
        for place in range((needed + BELOW - 1) // BELOW):
            total = jnp.zeros((BELOW, PANEL), F32)
            for ref in (own_ref, other_ref):
                for slot in range(place, ref.shape[0], inner):
                    total += ref[slot, rows:].astype(F32)
            sums.append(total)
        total = jnp.concatenate(sums, axis=0)
        first = 0
        for ref in extra_refs:
            ref[...] = total[first : first + ref.shape[0]]
            first += ref.shape[0]


def unpack_extra(line, slots, own, other, height, cols, extra, inner):
    return line.run(
        functools.partial(unpack_extra_body, height * cols // PANEL // slots.shape[0], inner),
        "unpack",
        5,
        (cols // PANEL,),
        [(own, fixed(own.shape)), (other, fixed(other.shape))],
        [((height, cols), F32, pl.BlockSpec((height, PANEL), lambda i, *_: (0, i)), FAR)]
        + [((rows, PANEL), F32, fixed((rows, PANEL))) for rows in extra],
        [slots],
    )


def unpack_two_body(last, slots_ref, own_ref, other_ref, out_ref, out2_ref):
    step = pl.program_id(0)
    rows = own_ref.shape[1]
    each = out_ref.shape[0] // rows

    @pl.when(step < last)
    def _():
        load_slots(slots_ref, step * each, own_ref, other_ref, out_ref, rows)

    @pl.when(step == last)
    def _():
        load_slots(slots_ref, step * each, own_ref, other_ref, out2_ref, rows)


def unpack_two(line, slots, own, other, height, cols):
    last = cols // PANEL
    return line.run(
        functools.partial(unpack_two_body, last),
        "unpack_two",
        5,
        (last + 1,),
        [(own, fixed(own.shape)), (other, fixed(other.shape))],
        [
            (
                (height, cols),
                F32,
                pl.BlockSpec((height, PANEL), lambda i, *_: (0, jnp.minimum(i, last - 1))),
                FAR,
            ),
            ((height, PANEL), F32, fixed((height, PANEL)), FAR),
        ],
        [slots],
    )


GROUP = 128
PAIR = 2 * HEAD_DIM
GELU_SCALE = 0.7978845608028654
GELU_CUBE = 0.044715


def center(values):
    centered = values - jnp.mean(values, axis=-1, keepdims=True)
    spread = jnp.mean(centered * centered, axis=-1, keepdims=True)
    rate = lax.rsqrt(spread + 1e-05)
    return centered * rate, rate


def center_back(grad, gain, unit, rate):
    gain_grad = jnp.sum(grad * unit, axis=0, keepdims=True)
    grad = grad * gain
    mean_grad = jnp.mean(grad, axis=-1, keepdims=True)
    mean_unit = jnp.mean(grad * unit, axis=-1, keepdims=True)
    return rate * (grad - mean_grad - unit * mean_unit), gain_grad


def start_of(pieces_ref, scripts_ref, script_table_ref):
    entries, slots, width = pieces_ref.shape
    groups = script_table_ref.shape[0]
    pieces = pieces_ref[...].astype(F32).reshape(entries * slots, width)
    onehot = (scripts_ref[...] == lax.broadcasted_iota(jnp.int32, (1, groups), 1)).astype(F32)
    return pieces + jnp.dot(onehot, script_table_ref[...], precision=highest), onehot


def slot_weights(lengths, slots):
    rows = lengths.shape[0]
    slot = lax.broadcasted_iota(jnp.int32, (rows, 1), 0) % slots
    return jnp.where(slot <= lengths, 1.0 / (lengths + 1).astype(F32), 0.0)


def split_heads(pair):
    first = lax.broadcasted_iota(jnp.int32, pair.shape, 1) < HEAD_DIM
    zero = jnp.zeros_like(pair)
    return jnp.concatenate([jnp.where(first, pair, zero), jnp.where(first, zero, pair)], axis=0)


def join_heads(stacked):
    first = lax.broadcasted_iota(jnp.int32, (GROUP, PAIR), 1) < HEAD_DIM
    return jnp.where(first, stacked[:GROUP], stacked[GROUP:])


def attn_body(
    slots,
    pieces_ref,
    scripts_ref,
    lengths_ref,
    script_table_ref,
    gain_attn_ref,
    gain_ffn_ref,
    w_qkv_ref,
    w_out_ref,
    normed_ref,
    mixed_ref,
    context_ref,
    middle_ref,
    normed_ffn_ref,
):
    start, _ = start_of(pieces_ref, scripts_ref, script_table_ref)
    rows, width = start.shape
    lengths = lengths_ref[...]
    normed = (center(start)[0] * gain_attn_ref[...]).astype(BF16)
    normed_ref[...] = normed
    mixed = mm(normed, w_qkv_ref[...]).astype(BF16)
    mixed_ref[...] = mixed
    row = lax.broadcasted_iota(jnp.int32, (GROUP, GROUP), 0)
    col = lax.broadcasted_iota(jnp.int32, (GROUP, GROUP), 1)
    groups = []
    for base in range(0, rows, GROUP):
        part = mixed[base : base + GROUP]
        valid = (row // slots == col // slots) & (col % slots <= lengths[base : base + GROUP])
        lows = range(0, width, PAIR)
        raws = [
            nt(part[:, low : low + PAIR], split_heads(part[:, width + low : width + low + PAIR]))
            for low in lows
        ]
        heads = [raw[:, side : side + GROUP] for raw in raws for side in (0, GROUP)]
        heads = [jnp.where(valid, head * HEAD_DIM ** (-0.5), -1000000000.0) for head in heads]
        heads = [jnp.exp(head - jnp.max(head, axis=1, keepdims=True)) for head in heads]
        heads = [(head * (1.0 / jnp.sum(head, axis=1, keepdims=True))).astype(BF16) for head in heads]
        pairs = [
            mm(
                jnp.concatenate(heads[2 * j : 2 * j + 2], axis=1),
                split_heads(part[:, 2 * width + low : 2 * width + low + PAIR]),
            )
            for j, low in enumerate(lows)
        ]
        groups.append(jnp.concatenate(pairs, axis=1).astype(BF16))
    context = jnp.concatenate(groups, axis=0)
    context_ref[...] = context
    middle = start + mm(context, w_out_ref[...])
    middle_ref[...] = middle
    normed_ffn_ref[...] = (center(middle)[0] * gain_ffn_ref[...]).astype(BF16)


def attn_forward(
    line, pieces, scripts, lengths, script_table, gain_attn, gain_ffn, w_qkv, w_out
):
    entries, slots, width = pieces.shape
    total = entries * slots
    rows = math.gcd(total, 512)
    some = rows // slots
    whole = (script_table, gain_attn, gain_ffn, w_qkv, w_out)
    return line.run(
        functools.partial(attn_body, slots),
        "attn_forward",
        12,
        (total // rows,),
        [
            (pieces, pl.BlockSpec((some, slots, width), lambda i, *_: (i, 0, 0))),
            (scripts, rows_of(rows, 1)),
            (lengths, rows_of(rows, 1)),
        ]
        + [(value, fixed(value.shape)) for value in whole],
        [
            ((total, width), BF16, rows_of(rows, width)),
            ((total, 3 * width), BF16, rows_of(rows, 3 * width), FAR),
            ((total, width), BF16, rows_of(rows, width)),
            ((total, width), F32, rows_of(rows, width)),
            ((total, width), BF16, rows_of(rows, width)),
        ],
    )


def ffn_body(
    slots,
    last,
    length_rows_ref,
    lengths_ref,
    before_ref,
    normed_ref,
    w_up_ref,
    w_down_ref,
    slope_ref,
    hidden_ref,
    pooled_ref,
):
    rows, width = normed_ref.shape
    some = rows // slots
    row = lax.broadcasted_iota(jnp.int32, (some, rows), 1)
    entry = lax.broadcasted_iota(jnp.int32, (some, rows), 0)
    lengths = lengths_ref[...]
    valid = (row // slots == entry) & (row % slots <= lengths)
    valid = jnp.where(valid, 1.0, 0.0).astype(BF16)
    scale = 1.0 / (lengths + 1).astype(F32)
    pooled = before_ref[...]
    if not last:
        weights = slot_weights(length_rows_ref[...], slots)
        pooled = jnp.sum((pooled * weights).reshape(some, slots, width), axis=1)
    ff = w_up_ref.shape[1]
    step = ff // 2
    for low in range(0, ff, step):
        up = mm(normed_ref[...], w_up_ref[:, low : low + step])
        square = up * up
        tanh = jnp.tanh(up * (GELU_SCALE + GELU_SCALE * GELU_CUBE * square))
        half_up = 0.5 * up
        hidden = (half_up + half_up * tanh).astype(BF16)
        slope_ref[:, low : low + step] = (0.5 + 0.5 * tanh) + half_up * (1.0 - tanh * tanh) * (
            GELU_SCALE + 3.0 * GELU_SCALE * GELU_CUBE * square
        )
        mean_hidden = mm(valid, hidden) * scale
        high = mean_hidden.astype(BF16)
        rest = (mean_hidden - high.astype(F32)).astype(BF16)
        hidden_ref[:, low : low + step] = high
        w_down = w_down_ref[low : low + step]
        pooled += mm(high, w_down) + mm(rest, w_down)
    pooled_ref[...] = pooled.astype(pooled_ref.dtype)


def ffn_forward(line, length_rows, lengths, before, normed, w_up, w_down, last):
    total, width = normed.shape
    entries = lengths.shape[0]
    slots = total // entries
    rows = math.gcd(total, 512)
    some = rows // slots
    ff = w_up.shape[1] // 2
    return line.run(
        functools.partial(ffn_body, slots, last),
        "ffn_forward",
        7,
        (total // rows,),
        [
            (length_rows, rows_of(rows, 1)),
            (lengths, rows_of(some, 1)),
            (before, rows_of(some if last else rows, width)),
            (normed, rows_of(rows, width)),
            (w_up, pl.BlockSpec((width, ff), lambda i, *_: (0, int(last)))),
            (w_down, pl.BlockSpec((ff, width), lambda i, *_: (int(last), 0))),
        ],
        [
            ((total, ff), F32, rows_of(rows, ff), FAR),
            ((entries, ff), BF16, rows_of(some, ff)),
            ((entries, width), BF16 if last else F32, rows_of(some, width)),
        ],
    )


def ffn_back_body(
    slots,
    pooled_grad_ref,
    lengths_ref,
    slope_a_ref,
    slope_b_ref,
    middle_ref,
    gain_ffn_ref,
    w_up_ref,
    w_down_ref,
    grad_up_ref,
    grad_middle_ref,
    grad_branch_ref,
    gain_grad_ref,
):
    pooled_grad = pooled_grad_ref[...]
    rows, width = middle_ref.shape
    some = rows // slots
    wide = jnp.broadcast_to(pooled_grad[:, None, :], (some, slots, width)).reshape(rows, width)
    grad_final = wide * slot_weights(lengths_ref[...], slots)
    grad_ffn = grad_final.astype(BF16)
    ff = w_up_ref.shape[1]
    step = ff // 4
    grad_normed = jnp.zeros((rows, width), F32)
    for low in range(0, ff, step):
        grad_hidden = nt(grad_ffn, w_down_ref[low : low + step])
        slope_ref, inner = (slope_a_ref, low) if low < ff // 2 else (slope_b_ref, low - ff // 2)
        grad_up = (slope_ref[:, inner : inner + step] * grad_hidden).astype(BF16)
        grad_up_ref[:, low : low + step] = grad_up
        grad_normed += nt(grad_up, w_up_ref[:, low : low + step])
    unit, rate = center(middle_ref[...])
    grad, gain_grad = center_back(grad_normed, gain_ffn_ref[...], unit, rate)
    grad_middle = grad_final + grad
    grad_middle_ref[...] = grad_middle
    grad_branch_ref[...] = grad_middle.astype(BF16)

    @pl.when(pl.program_id(0) == 0)
    def _():
        gain_grad_ref[...] = jnp.zeros_like(gain_grad_ref)

    gain_grad_ref[...] += gain_grad


def ffn_back(line, pooled_grad, lengths, slopes, middle, gain_ffn, w_up, w_down):
    total, width = middle.shape
    entries = pooled_grad.shape[0]
    slots = total // entries
    rows = math.gcd(total, 512)
    some = rows // slots
    ff = w_up.shape[1]
    return line.run(
        functools.partial(ffn_back_body, slots),
        "ffn_back",
        15,
        (total // rows,),
        [
            (pooled_grad, rows_of(some, width)),
            (lengths, rows_of(rows, 1)),
            *((slope, rows_of(rows, ff // 2)) for slope in slopes),
            (middle, rows_of(rows, width)),
            (gain_ffn, fixed(gain_ffn.shape)),
            (w_up, fixed(w_up.shape)),
            (w_down, fixed(w_down.shape)),
        ],
        [
            ((total, ff), BF16, rows_of(rows, ff)),
            ((total, width), F32, rows_of(rows, width)),
            ((total, width), BF16, rows_of(rows, width)),
            ((1, width), F32, fixed((1, width))),
        ],
    )


def heads_back_body(slots, lengths_ref, w_out_ref, mixed_ref, grad_branch_ref, grad_mixed_ref):
    rows, width = grad_branch_ref.shape
    lengths = lengths_ref[...]
    grad_ctx = nt(grad_branch_ref[...], w_out_ref[...]).astype(BF16)
    row = lax.broadcasted_iota(jnp.int32, (GROUP, GROUP), 0)
    col = lax.broadcasted_iota(jnp.int32, (GROUP, GROUP), 1)
    same = row // slots == col // slots
    lows = range(0, width, PAIR)
    for base in range(0, rows, GROUP):
        span = slice(base, base + GROUP)
        valid = same & (row % slots <= lengths[span])
        queries = [mixed_ref[span, low : low + PAIR] for low in lows]
        keys = [split_heads(mixed_ref[span, width + low : width + low + PAIR]) for low in lows]
        values = [split_heads(mixed_ref[span, 2 * width + low : 2 * width + low + PAIR]) for low in lows]
        grad_pairs = [grad_ctx[span, low : low + PAIR] for low in lows]
        raws = [nt(key, query) for key, query in zip(keys, queries)]
        grad_raws = [nt(value, grad_pair) for value, grad_pair in zip(values, grad_pairs)]
        sides = (slice(0, GROUP), slice(GROUP, 2 * GROUP))
        heads = [raw[side] for raw in raws for side in sides]
        heads = [jnp.where(valid, head * HEAD_DIM ** (-0.5), -1000000000.0) for head in heads]
        heads = [jnp.exp(head - jnp.max(head, axis=0, keepdims=True)) for head in heads]
        probs = [head * (1.0 / jnp.sum(head, axis=0, keepdims=True)) for head in heads]
        grads = [grad_raw[side] for grad_raw in grad_raws for side in sides]
        grads = [
            prob * (grad - jnp.sum(grad * prob, axis=0, keepdims=True)) for prob, grad in zip(probs, grads)
        ]
        probs = [prob.astype(BF16) for prob in probs]
        grads = [(grad * HEAD_DIM ** (-0.5)).astype(BF16) for grad in grads]
        for j, low in enumerate(lows):
            scores_grad = jnp.concatenate(grads[2 * j : 2 * j + 2], axis=0)
            prob = jnp.concatenate(probs[2 * j : 2 * j + 2], axis=0)
            grad_mixed_ref[span, low : low + PAIR] = tn(scores_grad, keys[j]).astype(BF16)
            grad_keys = join_heads(mm(scores_grad, queries[j]))
            grad_mixed_ref[span, width + low : width + low + PAIR] = grad_keys.astype(BF16)
            grad_values = join_heads(mm(prob, grad_pairs[j]))
            grad_mixed_ref[span, 2 * width + low : 2 * width + low + PAIR] = grad_values.astype(BF16)


def heads_back(line, lengths, w_out, mixed, grad_branch, slots):
    total, width = grad_branch.shape
    rows = math.gcd(total, 512)
    return line.run(
        functools.partial(heads_back_body, slots),
        "heads_back",
        13,
        (total // rows,),
        [
            (lengths, rows_of(rows, 1)),
            (w_out, fixed(w_out.shape)),
            (mixed, rows_of(rows, 3 * width)),
            (grad_branch, rows_of(rows, width)),
        ],
        [((total, 3 * width), BF16, rows_of(rows, 3 * width))],
    )[0]


def attn_back_body(
    pieces_ref,
    scripts_ref,
    script_table_ref,
    gain_attn_ref,
    w_qkv_ref,
    grad_mixed_ref,
    grad_middle_ref,
    gain_ffn_grad_ref,
    grad_pieces_ref,
    small_ref,
):
    start, onehot = start_of(pieces_ref, scripts_ref, script_table_ref)
    grad_normed = nt(grad_mixed_ref[...], w_qkv_ref[...])
    unit, rate = center(start)
    grad, gain_grad = center_back(grad_normed, gain_attn_ref[...], unit, rate)
    grad_pieces = grad_middle_ref[...] + grad
    grad_pieces_ref[...] = grad_pieces.reshape(grad_pieces_ref.shape)

    groups = onehot.shape[1]

    @pl.when(pl.program_id(0) == 0)
    def _():
        small_ref[...] = jnp.zeros_like(small_ref)
        small_ref[groups + 1 : groups + 2] = gain_ffn_grad_ref[...]

    small_ref[groups : groups + 1] += gain_grad
    small_ref[:groups] += lax.dot_general(
        onehot, grad_pieces, (((0,), (0,)), ((), ())), precision=highest
    )


def attn_back(
    line, pieces, scripts, script_table, gain_attn, w_qkv, grad_mixed, grad_middle, gain_ffn_grad
):
    entries, slots, width = pieces.shape
    total = entries * slots
    rows = math.gcd(total, 512)
    some = rows // slots
    small = ((script_table.shape[0] + 2 + 15) // 16 * 16, width)
    return line.run(
        attn_back_body,
        "attn_back",
        9,
        (total // rows,),
        [
            (pieces, pl.BlockSpec((some, slots, width), lambda i, *_: (i, 0, 0))),
            (scripts, rows_of(rows, 1)),
            (script_table, fixed(script_table.shape)),
            (gain_attn, fixed(gain_attn.shape)),
            (w_qkv, fixed(w_qkv.shape)),
            (grad_mixed, rows_of(rows, 3 * width)),
            (grad_middle, rows_of(rows, width)),
            (gain_ffn_grad, fixed(gain_ffn_grad.shape)),
        ],
        [
            ((entries, slots, width), F32, pl.BlockSpec((some, slots, width), lambda i, *_: (i, 0, 0)), FAR),
            (small, F32, fixed(small)),
        ],
    )


PLAN = ("f t T f", "03 t f", "36 t f", "68 t f t", "w t E F", "Q")


def per_device(
    pieces,
    lengths,
    scripts,
    script_table,
    gain_attn,
    gain_ffn,
    w_qkv,
    w_out,
    w_up,
    w_down,
    w_proj,
    token_ids,
    out_grad,
):
    entries, slots, width = pieces.shape
    ent_count = lax.axis_size("ent")
    rep_count = lax.axis_size("rep")
    devices = ent_count * rep_count
    features = w_proj.shape[1]
    vocab = entries * devices
    rows_dev, text_len = token_ids.shape
    tokens = rows_dev * text_len
    levels = make_levels(ent_count, rep_count)
    sizes = tuple(size for _, size, _ in levels)
    me = lax.axis_index("ent") * rep_count + lax.axis_index("rep")
    chunks = 1 if devices <= 32 else 8
    each = entries // chunks
    span = vocab // chunks
    slot = slot_of(token_ids // entries ^ me, levels)
    within = token_ids % entries
    slot_ids = within // each * span + slot * each + within % each
    script_rows = jnp.repeat(scripts, slots)[:, None]
    length_rows = jnp.repeat(lengths, slots)[:, None]
    gain_attn, gain_ffn = gain_attn[None], gain_ffn[None]

    cut = len(levels)
    while math.prod(sizes[:cut]) * 16 > w_down.shape[0]:
        cut -= 1
    near, far = levels[:cut], levels[cut:]
    count = math.prod(sizes[:cut])
    slot_index = jnp.arange(count, dtype=jnp.int32) ^ slot_of(me, near)
    line = Line()

    def cut_up(keep, send, some):
        shape = tuple(size for _, size, _ in some[1:]) + keep.shape[-2:]
        return keep.reshape(shape), send.reshape(shape)

    parts, pooled_grads = [], []
    for chunk in range(chunks):
        first = chunk * span
        part_send, send = scatter_rows(
            line, slot_ids, out_grad, w_proj, first + span // 2, span // 2, BF16
        )
        part_keep, keep = scatter_rows(line, slot_ids, out_grad, w_proj, first, span // 2, F32)
        parts.append((part_keep, part_send))
        shape = sizes[1:] + (each, width)
        pooling = sum_halves(line, keep.reshape(shape), send.reshape(shape), levels, pooled_grads)
        if chunks > 1:
            for _ in pooling:
                pass
    next(pooling, None)
    next(pooling, None)
    normed, mixed, context, middle, normed_ffn = attn_forward(
        line, pieces, script_rows, length_rows, script_table, gain_attn, gain_ffn, w_qkv, w_out
    )
    next(pooling, None)
    length_cols = lengths[:, None]
    slope_a, hidden_a, pooled = ffn_forward(
        line, length_rows, length_cols, middle, normed_ffn, w_up, w_down, False
    )
    next(pooling, None)
    slope_b, hidden_b, pooled = ffn_forward(
        line, length_rows, length_cols, pooled, normed_ffn, w_up, w_down, True
    )
    for _ in pooling:
        pass
    grad_pooled = jnp.concatenate(pooled_grads, axis=0) if chunks > 1 else pooled_grads[0]

    held = [((), each, width, BF16, lambda index: [(0, (), ALL, 0, 0)])]
    halves = [[] for _ in range(chunks)]
    spreads = [
        gather_halves(
            line, stage(line, [(pooled[chunk * each :][:each], [])], held)[0], levels, halves[chunk]
        )
        for chunk in range(chunks)
    ]

    def spread_on():
        if chunks == 1:
            next(spreads[0])

    spread_on()
    down = tall_weight(line, slot_index, (hidden_a, hidden_b), grad_pooled.astype(BF16))
    grad_up, grad_middle, grad_branch, part_gain_ffn = ffn_back(
        line, grad_pooled, length_rows, (slope_a, slope_b), middle, gain_ffn, w_up, w_down
    )
    spread_on()
    up = wide_weight(line, slot_index, normed_ffn, grad_up)
    small, ffn_all, two_all = [], [], []
    ffn_sum = all_sum_two(
        line, *cut_up(*down, near), *cut_up(*up, near), lambda: small[0], near, far, ffn_all
    )
    next(ffn_sum)
    spread_on()
    grad_mixed = heads_back(line, length_rows, w_out, mixed, grad_branch, slots)
    next(ffn_sum)
    two = two_weights(line, slot_index, normed, grad_mixed, context, grad_branch)
    two_sum = all_sum(line, *cut_up(*two, near), near, far, two_all)
    next(two_sum)
    spread_on()
    grad_pieces, part_small = attn_back(
        line,
        pieces,
        script_rows,
        script_table,
        gain_attn,
        w_qkv,
        grad_mixed,
        grad_middle,
        part_gain_ffn,
    )
    small.append(part_small)
    results = {}

    def make_table():
        tables, total = [], None
        for chunk in range(chunks):
            for _ in spreads[chunk]:
                pass
            own, other = (value.reshape(span // 2, width) for value in halves[chunk])
            table, part = table_and_grad(line, own, other, w_proj, *parts[chunk])
            tables.append(table)
            total = part if total is None else total + part
        results["tables"] = tables
        results["proj"] = total, swap(total, levels[0])

    def look_up(first, last):
        before = results.get("looked_up")
        results["looked_up"] = lookup(line, slot_ids, results["tables"], (first, last), before)

    def add_proj():
        total, other = results["proj"]
        whole = [((), width, features, F32, lambda index: [(0, (), ALL, 0, 0)])]
        results["w_proj"] = stage(line, [(total, [other])], whole)[0]

    def end_ffn():
        results["w_down"] = unpack(line, slot_index, *map(merge, ffn_all[:2]), w_down.shape[0])
        results["w_up"], *results["small"] = unpack_extra(
            line,
            slot_index,
            *map(merge, ffn_all[2:]),
            *w_up.shape,
            (script_table.shape[0], 1, 1),
            math.prod(sizes[3:cut]),
        )

    def end_two():
        for _ in two_sum:
            pass
        results["w_qkv"], results["w_out"] = unpack_two(
            line, slot_index, *map(merge, two_all), *w_qkv.shape
        )

    acts = {
        "f": lambda: next(ffn_sum, 0),
        "t": lambda: next(two_sum, 0),
        "T": make_table,
        "w": add_proj,
        "E": lambda: list(ffn_sum),
        "F": end_ffn,
        "Q": end_two,
    }
    for act in (act for part in PLAN for act in part.split()):
        if act.isdigit():
            look_up(int(act[0]), int(act[1]))
        else:
            acts[act]()
    looked_up, grad_w_proj = results["looked_up"], results["w_proj"]
    grad_w_down, grad_w_up = results["w_down"], results["w_up"]
    grad_w_qkv, grad_w_out = results["w_qkv"], results["w_out"]
    grad_script, grad_gain_attn, grad_gain_ffn = results["small"]
    return (
        looked_up,
        grad_pieces,
        grad_script,
        grad_gain_attn.reshape(width),
        grad_gain_ffn.reshape(width),
        grad_w_qkv,
        grad_w_out,
        grad_w_up,
        grad_w_down,
        grad_w_proj,
    )


def solution(mesh):
    in_specs = (
        P(("ent", "rep"), None, None),
        P(("ent", "rep")),
        P(("ent", "rep")),
        P(),
        P(),
        P(),
        P(),
        P(),
        P(),
        P(),
        P(None, "ent"),
        P("rep", None),
        P("ent", "rep", None),
    )
    out_specs = (
        P("ent", "rep", None),
        P(("ent", "rep"), None, None),
        P(),
        P(),
        P(),
        P(),
        P(),
        P(),
        P(),
        P(None, "ent"),
    )
    return jax.shard_map(
        per_device, mesh=mesh, in_specs=in_specs, out_specs=out_specs, check_vma=False
    )
```

```python
import functools
import math

import jax
import jax.numpy as jnp
import numpy as np
from jax import lax
from jax.experimental import pallas as pl
from jax.experimental.pallas import tpu as pltpu
from jax.sharding import PartitionSpec as P

HEADS = 8
HEAD_DIM = 64
F32 = jnp.float32
BF16 = jnp.bfloat16
highest = lax.Precision.HIGHEST
MIB = 1024 * 1024


def make_levels(ent_count, rep_count):
    levels = [("rep", rep_count, 0)]
    bit, total = 0, ent_count.bit_length() - 1
    while bit < total:
        width = 1 if bit < 2 else min(2, total - bit)
        levels.append(("ent", 1 << width, bit))
        bit += width
    return levels


def slot_of(number, levels):
    rep_count = levels[0][1]
    slot = number % rep_count
    ent = number // rep_count
    for _, size, shift in levels[1:]:
        slot = slot * size + (ent >> shift) % size
    return slot


def swap(value, level, k):
    name, size, shift = level
    count = lax.axis_size(name)
    return lax.ppermute(value, name, [(i, i ^ (k << shift)) for i in range(count)])


def merge(value):
    return value.reshape((-1,) + value.shape[-2:])


FAR = True


class Line:
    def __init__(self):
        self.last = []

    def run(self, body, name, micros, grid, ins, outs, prefetch=(), alias=None, room=24 * MIB, scratch=()):
        count = len(prefetch) + len(ins)
        extra = self.last + ([] if alias is None else [alias])
        token = (8, 128)

        def wrapped(*refs):
            held = len(refs) - len(scratch)
            refs[held - 1][...] = jnp.zeros(token, F32)
            body(*refs[:count], *refs[count + len(extra) : held - 1], *refs[held:])

        *results, last = pl.pallas_call(
            wrapped,
            grid_spec=pltpu.PrefetchScalarGridSpec(
                num_scalar_prefetch=len(prefetch),
                grid=grid,
                in_specs=[spec for _, spec in ins] + [pl.BlockSpec(memory_space=pl.ANY)] * len(extra),
                out_specs=[spec for _, _, spec, *_ in outs] + [pl.BlockSpec(token, lambda *_: (0, 0))],
                scratch_shapes=scratch,
            ),
            out_shape=[
                pltpu.HBM(shape, dtype) if far else jax.ShapeDtypeStruct(shape, dtype)
                for shape, dtype, _, *far in outs
            ]
            + [jax.ShapeDtypeStruct(token, F32)],
            input_output_aliases={} if alias is None else {count + len(extra) - 1: 0},
            compiler_params=pltpu.CompilerParams(vmem_limit_bytes=room),
            cost_estimate=pl.CostEstimate(
                flops=int(micros * 3e9), bytes_accessed=int(micros * 9e6), transcendentals=0
            ),
            name=name,
        )(*prefetch, *(value for value, _ in ins), *extra)
        self.last = [last]
        return results


def swap(value, level, k=1):
    name, size, shift = level
    count = lax.axis_size(name)
    return lax.ppermute(value, name, [(i, i ^ (k << shift)) for i in range(count)])


def swaps(values, level):
    return [swap(value, level, k) for k, value in enumerate(values, 1)]


ALL = slice(None)
BELOW = 16


def stage_body(layout, cuts, *refs):
    sums, position = [], 0
    for number in layout:
        sums.append(refs[position : position + number])
        position += number

    def piece(number, index, cols, rows=ALL):
        total = sums[number][0][index][rows, cols]
        for ref in sums[number][1:]:
            total = total.astype(F32) + ref[index][rows, cols].astype(F32)
        return total

    for out_ref, sources in zip(refs[position:], cuts):
        for target, parts in sources:
            for number, index, cols, row, col, *rows in parts:
                value = piece(number, index, cols, *rows).astype(out_ref.dtype)
                where = target + (slice(row, row + value.shape[0]), slice(col, col + value.shape[1]))
                out_ref[where] = value


def stage(line, sums, outs, steps=1):
    values = [value for kept, received in sums for value in [kept, *received]]

    def spec(shape):
        return pl.BlockSpec(memory_space=pltpu.VMEM)

    cuts = [
        [(target, source(target)) for target in np.ndindex(*lead)] for lead, _, _, _, source in outs
    ]
    shapes = [(lead + (rows, cols), dtype) for lead, rows, cols, dtype, _ in outs]
    held = [(value.shape, value.dtype) for value in values] + [(shape, jnp.dtype(dtype)) for shape, dtype in shapes]
    return line.run(
        functools.partial(stage_body, [1 + len(received) for _, received in sums], cuts),
        "exchange",
        0.5,
        (),
        [(value, spec(value.shape)) for value in values],
        [(shape, dtype, spec(shape)) for shape, dtype in shapes],
        room=2 * MIB + sum(math.prod(shape) * dtype.itemsize for shape, dtype in held),
    )


def split(number, value, axis, cols=ALL, width=None):
    lead = value.shape[:-2]
    rest = lead[:axis] + lead[axis + 1 :]
    outs = []
    for k in range(lead[axis]):

        def source(index, k=k):
            return [(number, index[:axis] + (k,) + index[axis:], cols, 0, 0)]

        outs.append((rest, value.shape[-2], width or value.shape[-1], F32 if k == 0 else BF16, source))
    return outs


def stacked(numbers, value, axis, rows=ALL):
    lead = value.shape[:-2]
    shape = lead[:axis] + (len(numbers),) + lead[axis:]

    def source(index):
        return [(numbers[index[axis]], index[:axis] + index[axis + 1 :], ALL, 0, 0)]

    return (shape, value.shape[-2], value.shape[-1], value.dtype, source)


def finish(line, sums, far, shape, dtype):
    whole = [(0, (), ALL, 0, 0)]
    for level in far:
        outs = [((), *shape, kind, lambda index: whole) for kind in (F32, BF16)]
        keep, send = stage(line, sums, outs)
        sums = [(keep, [swap(send, level, k) for k in range(1, level[1])])]
        yield
    yield stage(line, sums, [((), *shape, dtype, lambda index: whole)])[0]


def sum_halves(line, keep, send, levels, out, far=(), dtype=F32):
    received = swap(send, levels[0])
    yield
    rows, width = keep.shape[-2:]
    half = width // 2
    left, right = slice(0, half), slice(half, width)
    steps = 4 if rows % 64 == 0 else 1
    outs = split(0, keep, 0, left, half) + split(0, keep, 1, right, half)
    keep_a, send_a, keep_b, send_b = stage(line, [(keep, [received])], outs, steps)
    got_a, got_b = swap(send_a, levels[1]), swap(send_b, levels[2])
    yield
    outs = split(0, keep_a, 0) + split(1, keep_b, 0)
    sums = [(keep_a, [got_a]), (keep_b, [got_b])]
    keep_a, send_a, keep_b, send_b = stage(line, sums, outs, steps)
    sums = [(keep_a, [swap(send_a, levels[2])]), (keep_b, [swap(send_b, levels[1])])]
    yield
    for place, level in enumerate(levels[3:]):
        if place == 0:
            lead = keep_a.shape[1:-2]

            def source(index, k):
                return [(0, (k,) + index, ALL, 0, 0), (1, (k,) + index, ALL, 0, half)]

            outs = [
                (lead, rows, width, F32 if k == 0 else BF16, functools.partial(source, k=k))
                for k in range(level[1])
            ]
        else:
            outs = split(0, keep, 0)
        keep, *sends = stage(line, sums, outs)
        sums = [(keep, swaps(sends, level))]
        yield
    for value in finish(line, sums, far, (rows, width), dtype):
        if value is None:
            yield
    out.append(value)


def gather_halves(line, value, levels, out):
    rows, width = value.shape
    half = width // 2
    for place, level in reversed(list(enumerate(levels[3:]))):
        got = [swap(value, level, k) for k in range(1, level[1])]
        yield
        parts = [(part, []) for part in [value, *got]]
        numbers = list(range(level[1]))
        if place:
            value = stage(line, parts, [stacked(numbers, value, 0)])[0]
        else:
            lead = (level[1],) + value.shape[:-2]

            def source(index, cols):
                return [(index[0], index[1:], cols, 0, 0)]

            outs = [
                (lead, rows, half, BF16, functools.partial(source, cols=cols))
                for cols in (slice(0, half), slice(half, width))
            ]
            value_a, value_b = stage(line, parts, outs)
    got_a, got_b = swap(value_a, levels[2]), swap(value_b, levels[1])
    yield
    sums = [(part, []) for part in (value_a, got_a, value_b, got_b)]
    outs = [stacked([0, 1], value_a, 0), stacked([2, 3], value_b, 0)]
    value_a, value_b = stage(line, sums, outs)
    got_a, got_b = swap(value_a, levels[1]), swap(value_b, levels[2])
    yield
    sums = [(part, []) for part in (value_a, got_a, value_b, got_b)]
    lead = (2,) + value_a.shape[:-2]

    def joined(index):
        left, right = index[0], index[1]
        return [(left, index[1:], ALL, 0, 0), (2 + right, (left,) + index[2:], ALL, 0, half)]

    value = stage(line, sums, [(lead, rows, width, BF16, joined)])[0]
    out += [value, swap(value, levels[0])]
    yield


def all_sum(line, keep, send, near, far, out):
    mine = []
    yield from sum_halves(line, keep, send, near, mine, far, BF16)
    yield from gather_halves(line, mine[0], near, out)


def all_sum_two(line, keep_a, send_a, keep_b, send_b, extra, near, far, out):
    got_a, got_b = swap(send_a, near[0]), swap(send_b, near[0])
    yield
    rows = keep_a.shape[-2]
    outs = split(0, keep_a, 0) + split(1, keep_b, 1)
    keep_a, send_a, keep_b, send_b = stage(line, [(keep_a, [got_a]), (keep_b, [got_b])], outs)
    got_a, got_b = swap(send_a, near[1]), swap(send_b, near[2])
    yield
    outs = split(0, keep_a, 0) + split(1, keep_b, 0)
    keep_a, send_a, keep_b, send_b = stage(line, [(keep_a, [got_a]), (keep_b, [got_b])], outs)
    sums = [(keep_a, [swap(send_a, near[2])]), (keep_b, [swap(send_b, near[1])])]
    yield
    below = extra()
    added = below.shape[0]
    for place, level in enumerate(near[3:]):
        if place == 0:
            lead = keep_a.shape[1:-2]
            sums = sums + [(below, [])]

            def source(index, k):
                places = [(0, (k,) + index, 0), (1, (k,) + index, rows), (2, (), 2 * rows)]
                return [(number, where, ALL, row, 0) for number, where, row in places]

            outs = [
                (lead, 2 * rows + added, PANEL, F32 if k == 0 else BF16, functools.partial(source, k=k))
                for k in range(level[1])
            ]
        else:
            outs = split(0, keep, 0)
        keep, *sends = stage(line, sums, outs)
        sums = [(keep, swaps(sends, level))]
        yield
    for level in far:
        outs = [((), 2 * rows + added, PANEL, kind, lambda index: [(0, (), ALL, 0, 0)]) for kind in (F32, BF16)]
        keep, send = stage(line, sums, outs)
        sums = [(keep, [swap(send, level, k) for k in range(1, level[1])])]
        yield
    outs = [
        ((), size, PANEL, BF16, lambda index, part=part: [(0, (), ALL, 0, 0, part)])
        for size, part in ((2 * rows, slice(0, 2 * rows)), (added, slice(2 * rows, 2 * rows + added)))
    ]
    value, below = stage(line, sums, outs)
    for place, level in reversed(list(enumerate(near[3:]))):
        got = [swap(value, level, k) for k in range(1, level[1])]
        yield
        numbers = list(range(level[1]))
        parts = [(part, []) for part in [value, *got]]
        if place:
            value = stage(line, parts, [stacked(numbers, value, 0)])[0]
            continue
        lead = (level[1],) + value.shape[:-2]

        def first(index):
            return [(index[0], index[1:], ALL, 0, 0, slice(0, rows))]

        def second(index):
            number = int(np.ravel_multi_index(index, lead)) * BELOW % added
            return [
                (index[0], index[1:], ALL, 0, 0, slice(rows, 2 * rows)),
                (len(numbers), (), ALL, rows, 0, slice(number, number + BELOW)),
            ]

        outs = [(lead, rows, PANEL, BF16, first), (lead, rows + BELOW, PANEL, BF16, second)]
        value_a, value_b = stage(line, parts + [(below, [])], outs)
    got_a, got_b = swap(value_a, near[2]), swap(value_b, near[1])
    yield
    sums = [(part, []) for part in (value_a, got_a, value_b, got_b)]
    outs = [stacked([0, 1], value_a, 0), stacked([2, 3], value_b, 0)]
    value_a, value_b = stage(line, sums, outs)
    got_a, got_b = swap(value_a, near[1]), swap(value_b, near[2])
    yield
    sums = [(part, []) for part in (value_a, got_a, value_b, got_b)]
    outs = [stacked([0, 1], value_a, 0), stacked([2, 3], value_b, 1)]
    value_a, value_b = stage(line, sums, outs)
    out += [value_a, swap(value_a, near[0]), value_b, swap(value_b, near[0])]
    yield


def fixed(shape):
    return pl.BlockSpec(shape, lambda i, *_: (0,) * len(shape))


def rows_of(rows, width):
    return pl.BlockSpec((rows, width), lambda i, *_: (i, 0))


def selector(ids, base, rows):
    entry = lax.broadcasted_iota(jnp.int32, (rows, 1), 0).astype(jnp.int16)
    return jnp.where(entry == (ids - base).astype(jnp.int16), jnp.ones((), BF16), jnp.zeros((), BF16))


def nt(left, right):
    return lax.dot_general(left, right, (((1,), (1,)), ((), ())), preferred_element_type=F32)


def tn(left, right):
    return lax.dot_general(left, right, (((0,), (0,)), ((), ())), preferred_element_type=F32)


def mm(left, right):
    return jnp.dot(left, right, preferred_element_type=F32)


def scatter_body(first, ids_ref, grad_ref, proj_ref, table_ref, pooled_ref, flat_ref):
    @pl.when(pl.program_id(0) == 0)
    def _():
        flat_ref[...] = grad_ref[...].reshape(flat_ref.shape)

    rows = table_ref.shape[0]
    some = min(256, rows)
    parts = []
    for low in range(0, rows, some):
        base = first + pl.program_id(0) * rows + low
        picks = [selector(ids_ref[row : row + 1], base, some) for row in range(ids_ref.shape[0])]
        parts.append(nt(jnp.concatenate(picks, axis=1), flat_ref[...]))
    part = jnp.concatenate(parts, axis=0).astype(BF16)
    table_ref[...] = part
    pooled_ref[...] = nt(part, proj_ref[...]).astype(pooled_ref.dtype)


def scatter_rows(line, ids, grad, w_proj, first, count, dtype):
    features = grad.shape[0]
    width = w_proj.shape[0]
    rows = min(1024, count)
    return line.run(
        functools.partial(scatter_body, first),
        "scatter_rows",
        14,
        (count // rows,),
        [
            (ids, fixed(ids.shape)),
            (grad, pl.BlockSpec(memory_space=pltpu.VMEM)),
            (w_proj, fixed(w_proj.shape)),
        ],
        [
            ((count, features), BF16, rows_of(rows, features), FAR),
            ((count, width), dtype, rows_of(rows, width)),
        ],
        room=28 * MIB,
        scratch=[pltpu.VMEM((features, ids.size), BF16)],
    )


def table_body(steps, own_ref, other_ref, proj_ref, part_own_ref, part_other_ref, table_ref, grad_ref):
    step = pl.program_id(0)

    @pl.when(step == 0)
    def _():
        grad_ref[...] = jnp.zeros_like(grad_ref)

    def one(pooled_ref, part_ref):
        pooled = pooled_ref[...]
        cols = lax.dot_general(
            proj_ref[...], pooled, (((0,), (1,)), ((), ())), preferred_element_type=F32
        )
        table_ref[...] = cols.astype(BF16)
        grad_ref[...] += tn(pooled, part_ref[...])

    @pl.when(step < steps)
    def _():
        one(own_ref, part_own_ref)

    @pl.when(step >= steps)
    def _():
        one(other_ref, part_other_ref)


def table_and_grad(line, own, other, w_proj, part_own, part_other):
    count, width = own.shape
    features = w_proj.shape[1]
    rows = min(1024, count)
    steps = count // rows

    def first(cols):
        return pl.BlockSpec((rows, cols), lambda i, *_: (jnp.minimum(i, steps - 1), 0))

    def second(cols):
        return pl.BlockSpec((rows, cols), lambda i, *_: (jnp.maximum(i - steps, 0), 0))

    return line.run(
        functools.partial(table_body, steps),
        "table_and_grad",
        5,
        (2 * steps,),
        [
            (own, first(width)),
            (other, second(width)),
            (w_proj, fixed(w_proj.shape)),
            (part_own, first(features)),
            (part_other, second(features)),
        ],
        [
            ((features, 2 * count), BF16, pl.BlockSpec((features, rows), lambda i, *_: (0, i))),
            ((width, features), F32, fixed((width, features))),
        ],
    )


def lookup_body(chunk, ids_ref, *refs):
    table_refs, out_ref = refs[:-1], refs[-1]
    rows = ids_ref.shape[0]

    def find(base, table):
        picks = [selector(ids_ref[row : row + 1], base, chunk) for row in range(rows)]
        return mm(table, jnp.concatenate(picks, axis=1))

    total = None
    for index, table_ref in enumerate(table_refs):
        vocab = table_ref.shape[1]
        for inner in range(0, vocab, chunk):
            part = find(index * vocab + inner, table_ref[:, inner : inner + chunk])
            total = part if total is None else total + part
    out_ref[...] = total.astype(BF16).reshape(out_ref.shape)


def lookup(line, ids, tables, part, before=None):
    rows, text_len = ids.shape
    features, vocab = tables[0].shape
    block = text_len // 8
    first, last = part
    return line.run(
        functools.partial(lookup_body, min(vocab, 4096)),
        "lookup",
        3 * (last - first),
        (last - first,),
        [(ids, pl.BlockSpec((rows, block), lambda i, *_: (0, i + first)))]
        + [(table, fixed(table.shape)) for table in tables],
        [
            (
                (features, rows, text_len),
                BF16,
                pl.BlockSpec((features, rows, block), lambda i, *_: (0, 0, i + first)),
                FAR,
            )
        ],
        alias=before,
    )[0]


PANEL = 512


def store_slots(slots_ref, first, part, keep_ref, send_ref):
    half, rows, _ = keep_ref.shape
    for j in range(part.shape[0] // rows):
        slot = slots_ref[first + j]
        piece = part[j * rows : (j + 1) * rows]

        @pl.when(slot < half)
        def _():
            keep_ref[slot] = piece

        @pl.when(slot >= half)
        def _():
            send_ref[slot - half] = piece.astype(BF16)


def weight_body(slots_ref, left_ref, right_ref, keep_ref, send_ref):
    part = tn(left_ref[...], right_ref[...])
    store_slots(slots_ref, pl.program_id(0) * (part.shape[0] // keep_ref.shape[1]), part, keep_ref, send_ref)


def tall_body(steps, slots_ref, first_ref, second_ref, right_ref, keep_ref, send_ref):
    step = pl.program_id(0)
    each = PANEL // keep_ref.shape[1]

    @pl.when(step < steps)
    def _():
        store_slots(slots_ref, step * each, tn(first_ref[...], right_ref[...]), keep_ref, send_ref)

    @pl.when(step >= steps)
    def _():
        store_slots(slots_ref, step * each, tn(second_ref[...], right_ref[...]), keep_ref, send_ref)


def two_weights_body(last, slots_ref, left_ref, right_ref, left2_ref, right2_ref, keep_ref, send_ref):
    step = pl.program_id(0)
    each = left_ref.shape[1] // keep_ref.shape[1]

    @pl.when(step < last)
    def _():
        store_slots(slots_ref, step * each, tn(left_ref[...], right_ref[...]), keep_ref, send_ref)

    @pl.when(step == last)
    def _():
        store_slots(slots_ref, step * each, tn(left2_ref[...], right2_ref[...]), keep_ref, send_ref)


def slot_outs(count, rows):
    shape = (count // 2, rows, PANEL)
    return [(shape, F32, fixed(shape)), (shape, BF16, fixed(shape))]


def panel_of(depth):
    return pl.BlockSpec((depth, PANEL), lambda i, *_: (0, i))


def tall_weight(line, slots, lefts, right):
    depth, half = lefts[0].shape
    steps = half // PANEL
    return line.run(
        functools.partial(tall_body, steps),
        "tall_weight",
        3,
        (2 * steps,),
        [
            (lefts[0], pl.BlockSpec((depth, PANEL), lambda i, *_: (0, jnp.minimum(i, steps - 1)))),
            (lefts[1], pl.BlockSpec((depth, PANEL), lambda i, *_: (0, jnp.maximum(i - steps, 0)))),
            (right, fixed(right.shape)),
        ],
        slot_outs(slots.shape[0], 2 * half // slots.shape[0]),
        [slots],
    )


def wide_weight(line, slots, left, right):
    depth, cols = right.shape
    return line.run(
        weight_body,
        "wide_weight",
        8,
        (cols // PANEL,),
        [(left, fixed(left.shape)), (right, panel_of(depth))],
        slot_outs(slots.shape[0], cols // PANEL * left.shape[1] // slots.shape[0]),
        [slots],
    )


def two_weights(line, slots, left, right, left2, right2):
    depth, cols = right.shape
    last = cols // PANEL
    return line.run(
        functools.partial(two_weights_body, last),
        "two_weights",
        5,
        (last + 1,),
        [
            (left, fixed(left.shape)),
            (right, pl.BlockSpec((depth, PANEL), lambda i, *_: (0, jnp.minimum(i, last - 1)))),
            (left2, fixed(left2.shape)),
            (right2, fixed(right2.shape)),
        ],
        slot_outs(slots.shape[0], (last + 1) * left.shape[1] // slots.shape[0]),
        [slots],
    )


def load_slots(slots_ref, first, own_ref, other_ref, out_ref, rows):
    half = own_ref.shape[0]
    for j in range(out_ref.shape[0] // rows):
        slot = slots_ref[first + j]

        @pl.when(slot < half)
        def _():
            out_ref[j * rows : (j + 1) * rows] = own_ref[slot, :rows].astype(F32)

        @pl.when(slot >= half)
        def _():
            out_ref[j * rows : (j + 1) * rows] = other_ref[slot - half, :rows].astype(F32)


def unpack_body(slots_ref, own_ref, other_ref, out_ref):
    rows = own_ref.shape[1]
    each = out_ref.shape[0] // rows
    load_slots(slots_ref, pl.program_id(0) * each, own_ref, other_ref, out_ref, rows)


def unpack(line, slots, own, other, height):
    tile = min(512, height)
    return line.run(
        unpack_body,
        "unpack",
        5,
        (height // tile,),
        [(own, fixed(own.shape)), (other, fixed(other.shape))],
        [((height, PANEL), F32, pl.BlockSpec((tile, PANEL), lambda i, *_: (i, 0)), FAR)],
        [slots],
    )[0]


def unpack_extra_body(rows, inner, slots_ref, own_ref, other_ref, out_ref, *extra_refs):
    each = out_ref.shape[0] // rows
    load_slots(slots_ref, pl.program_id(0) * each, own_ref, other_ref, out_ref, rows)

    @pl.when(pl.program_id(0) == 0)
    def _():
        needed = sum(ref.shape[0] for ref in extra_refs)
        sums = []
        for place in range((needed + BELOW - 1) // BELOW):
            total = jnp.zeros((BELOW, PANEL), F32)
            for ref in (own_ref, other_ref):
                for slot in range(place, ref.shape[0], inner):
                    total += ref[slot, rows:].astype(F32)
            sums.append(total)
        total = jnp.concatenate(sums, axis=0)
        first = 0
        for ref in extra_refs:
            ref[...] = total[first : first + ref.shape[0]]
            first += ref.shape[0]


def unpack_extra(line, slots, own, other, height, cols, extra, inner):
    return line.run(
        functools.partial(unpack_extra_body, height * cols // PANEL // slots.shape[0], inner),
        "unpack",
        5,
        (cols // PANEL,),
        [(own, fixed(own.shape)), (other, fixed(other.shape))],
        [((height, cols), F32, pl.BlockSpec((height, PANEL), lambda i, *_: (0, i)), FAR)]
        + [((rows, PANEL), F32, fixed((rows, PANEL))) for rows in extra],
        [slots],
    )


def unpack_two_body(last, slots_ref, own_ref, other_ref, out_ref, out2_ref):
    step = pl.program_id(0)
    rows = own_ref.shape[1]
    each = out_ref.shape[0] // rows

    @pl.when(step < last)
    def _():
        load_slots(slots_ref, step * each, own_ref, other_ref, out_ref, rows)

    @pl.when(step == last)
    def _():
        load_slots(slots_ref, step * each, own_ref, other_ref, out2_ref, rows)


def unpack_two(line, slots, own, other, height, cols):
    last = cols // PANEL
    return line.run(
        functools.partial(unpack_two_body, last),
        "unpack_two",
        5,
        (last + 1,),
        [(own, fixed(own.shape)), (other, fixed(other.shape))],
        [
            (
                (height, cols),
                F32,
                pl.BlockSpec((height, PANEL), lambda i, *_: (0, jnp.minimum(i, last - 1))),
                FAR,
            ),
            ((height, PANEL), F32, fixed((height, PANEL)), FAR),
        ],
        [slots],
    )


GROUP = 128
PAIR = 2 * HEAD_DIM
GELU_SCALE = 0.7978845608028654
GELU_CUBE = 0.044715


def center(values):
    centered = values - jnp.mean(values, axis=-1, keepdims=True)
    spread = jnp.mean(centered * centered, axis=-1, keepdims=True)
    rate = lax.rsqrt(spread + 1e-05)
    return centered * rate, rate


def center_back(grad, gain, unit, rate):
    gain_grad = jnp.sum(grad * unit, axis=0, keepdims=True)
    grad = grad * gain
    mean_grad = jnp.mean(grad, axis=-1, keepdims=True)
    mean_unit = jnp.mean(grad * unit, axis=-1, keepdims=True)
    return rate * (grad - mean_grad - unit * mean_unit), gain_grad


def start_of(pieces_ref, scripts_ref, script_table_ref):
    entries, slots, width = pieces_ref.shape
    groups = script_table_ref.shape[0]
    pieces = pieces_ref[...].astype(F32).reshape(entries * slots, width)
    onehot = (scripts_ref[...] == lax.broadcasted_iota(jnp.int32, (1, groups), 1)).astype(F32)
    return pieces + jnp.dot(onehot, script_table_ref[...], precision=highest), onehot


def slot_weights(lengths, slots):
    rows = lengths.shape[0]
    slot = lax.broadcasted_iota(jnp.int32, (rows, 1), 0) % slots
    return jnp.where(slot <= lengths, 1.0 / (lengths + 1).astype(F32), 0.0)


def split_heads(pair):
    first = lax.broadcasted_iota(jnp.int32, pair.shape, 1) < HEAD_DIM
    zero = jnp.zeros_like(pair)
    return jnp.concatenate([jnp.where(first, pair, zero), jnp.where(first, zero, pair)], axis=0)


def join_heads(stacked):
    first = lax.broadcasted_iota(jnp.int32, (GROUP, PAIR), 1) < HEAD_DIM
    return jnp.where(first, stacked[:GROUP], stacked[GROUP:])


def attn_body(
    slots,
    pieces_ref,
    scripts_ref,
    lengths_ref,
    script_table_ref,
    gain_attn_ref,
    gain_ffn_ref,
    w_qkv_ref,
    w_out_ref,
    normed_ref,
    mixed_ref,
    context_ref,
    middle_ref,
    normed_ffn_ref,
):
    start, _ = start_of(pieces_ref, scripts_ref, script_table_ref)
    rows, width = start.shape
    lengths = lengths_ref[...]
    normed = (center(start)[0] * gain_attn_ref[...]).astype(BF16)
    normed_ref[...] = normed
    mixed = mm(normed, w_qkv_ref[...]).astype(BF16)
    mixed_ref[...] = mixed
    row = lax.broadcasted_iota(jnp.int32, (GROUP, GROUP), 0)
    col = lax.broadcasted_iota(jnp.int32, (GROUP, GROUP), 1)
    groups = []
    for base in range(0, rows, GROUP):
        part = mixed[base : base + GROUP]
        valid = (row // slots == col // slots) & (col % slots <= lengths[base : base + GROUP])
        lows = range(0, width, PAIR)
        raws = [
            nt(part[:, low : low + PAIR], split_heads(part[:, width + low : width + low + PAIR]))
            for low in lows
        ]
        heads = [raw[:, side : side + GROUP] for raw in raws for side in (0, GROUP)]
        heads = [jnp.where(valid, head * HEAD_DIM ** (-0.5), -1000000000.0) for head in heads]
        heads = [jnp.exp(head - jnp.max(head, axis=1, keepdims=True)) for head in heads]
        heads = [(head * (1.0 / jnp.sum(head, axis=1, keepdims=True))).astype(BF16) for head in heads]
        pairs = [
            mm(
                jnp.concatenate(heads[2 * j : 2 * j + 2], axis=1),
                split_heads(part[:, 2 * width + low : 2 * width + low + PAIR]),
            )
            for j, low in enumerate(lows)
        ]
        groups.append(jnp.concatenate(pairs, axis=1).astype(BF16))
    context = jnp.concatenate(groups, axis=0)
    context_ref[...] = context
    middle = start + mm(context, w_out_ref[...])
    middle_ref[...] = middle
    normed_ffn_ref[...] = (center(middle)[0] * gain_ffn_ref[...]).astype(BF16)


def attn_forward(
    line, pieces, scripts, lengths, script_table, gain_attn, gain_ffn, w_qkv, w_out
):
    entries, slots, width = pieces.shape
    total = entries * slots
    rows = math.gcd(total, 256)
    some = rows // slots
    whole = (script_table, gain_attn, gain_ffn, w_qkv, w_out)
    return line.run(
        functools.partial(attn_body, slots),
        "attn_forward",
        12,
        (total // rows,),
        [
            (pieces, pl.BlockSpec((some, slots, width), lambda i, *_: (i, 0, 0))),
            (scripts, rows_of(rows, 1)),
            (lengths, rows_of(rows, 1)),
        ]
        + [(value, fixed(value.shape)) for value in whole],
        [
            ((total, width), BF16, rows_of(rows, width)),
            ((total, 3 * width), BF16, rows_of(rows, 3 * width), FAR),
            ((total, width), BF16, rows_of(rows, width)),
            ((total, width), F32, rows_of(rows, width)),
            ((total, width), BF16, rows_of(rows, width)),
        ],
    )


def ffn_body(
    slots,
    last,
    length_rows_ref,
    lengths_ref,
    before_ref,
    normed_ref,
    w_up_ref,
    w_down_ref,
    slope_ref,
    hidden_ref,
    pooled_ref,
):
    rows, width = normed_ref.shape
    some = rows // slots
    row = lax.broadcasted_iota(jnp.int32, (some, rows), 1)
    entry = lax.broadcasted_iota(jnp.int32, (some, rows), 0)
    lengths = lengths_ref[...]
    valid = (row // slots == entry) & (row % slots <= lengths)
    valid = jnp.where(valid, 1.0, 0.0).astype(BF16)
    scale = 1.0 / (lengths + 1).astype(F32)
    pooled = before_ref[...]
    if not last:
        weights = slot_weights(length_rows_ref[...], slots)
        pooled = jnp.sum((pooled * weights).reshape(some, slots, width), axis=1)
    ff = w_up_ref.shape[1]
    step = ff // 2
    for low in range(0, ff, step):
        up = mm(normed_ref[...], w_up_ref[:, low : low + step])
        square = up * up
        tanh = jnp.tanh(up * (GELU_SCALE + GELU_SCALE * GELU_CUBE * square))
        half_up = 0.5 * up
        hidden = (half_up + half_up * tanh).astype(BF16)
        slope_ref[:, low : low + step] = (0.5 + 0.5 * tanh) + half_up * (1.0 - tanh * tanh) * (
            GELU_SCALE + 3.0 * GELU_SCALE * GELU_CUBE * square
        )
        mean_hidden = mm(valid, hidden) * scale
        high = mean_hidden.astype(BF16)
        rest = (mean_hidden - high.astype(F32)).astype(BF16)
        hidden_ref[:, low : low + step] = high
        w_down = w_down_ref[low : low + step]
        pooled += mm(high, w_down) + mm(rest, w_down)
    pooled_ref[...] = pooled.astype(pooled_ref.dtype)


def ffn_forward(line, length_rows, lengths, before, normed, w_up, w_down, last):
    total, width = normed.shape
    entries = lengths.shape[0]
    slots = total // entries
    rows = math.gcd(total, 256)
    some = rows // slots
    ff = w_up.shape[1] // 2
    return line.run(
        functools.partial(ffn_body, slots, last),
        "ffn_forward",
        7,
        (total // rows,),
        [
            (length_rows, rows_of(rows, 1)),
            (lengths, rows_of(some, 1)),
            (before, rows_of(some if last else rows, width)),
            (normed, rows_of(rows, width)),
            (w_up, pl.BlockSpec((width, ff), lambda i, *_: (0, int(last)))),
            (w_down, pl.BlockSpec((ff, width), lambda i, *_: (int(last), 0))),
        ],
        [
            ((total, ff), F32, rows_of(rows, ff), FAR),
            ((entries, ff), BF16, rows_of(some, ff)),
            ((entries, width), BF16 if last else F32, rows_of(some, width)),
        ],
    )


def ffn_back_body(
    slots,
    pooled_grad_ref,
    lengths_ref,
    slope_a_ref,
    slope_b_ref,
    middle_ref,
    gain_ffn_ref,
    w_up_ref,
    w_down_ref,
    grad_up_ref,
    grad_middle_ref,
    grad_branch_ref,
    gain_grad_ref,
):
    pooled_grad = pooled_grad_ref[...]
    rows, width = middle_ref.shape
    some = rows // slots
    wide = jnp.broadcast_to(pooled_grad[:, None, :], (some, slots, width)).reshape(rows, width)
    grad_final = wide * slot_weights(lengths_ref[...], slots)
    grad_ffn = grad_final.astype(BF16)
    ff = w_up_ref.shape[1]
    step = ff // 4
    grad_normed = jnp.zeros((rows, width), F32)
    for low in range(0, ff, step):
        grad_hidden = nt(grad_ffn, w_down_ref[low : low + step])
        slope_ref, inner = (slope_a_ref, low) if low < ff // 2 else (slope_b_ref, low - ff // 2)
        grad_up = (slope_ref[:, inner : inner + step] * grad_hidden).astype(BF16)
        grad_up_ref[:, low : low + step] = grad_up
        grad_normed += nt(grad_up, w_up_ref[:, low : low + step])
    unit, rate = center(middle_ref[...])
    grad, gain_grad = center_back(grad_normed, gain_ffn_ref[...], unit, rate)
    grad_middle = grad_final + grad
    grad_middle_ref[...] = grad_middle
    grad_branch_ref[...] = grad_middle.astype(BF16)

    @pl.when(pl.program_id(0) == 0)
    def _():
        gain_grad_ref[...] = jnp.zeros_like(gain_grad_ref)

    gain_grad_ref[...] += gain_grad


def ffn_back(line, pooled_grad, lengths, slopes, middle, gain_ffn, w_up, w_down):
    total, width = middle.shape
    entries = pooled_grad.shape[0]
    slots = total // entries
    rows = math.gcd(total, 256)
    some = rows // slots
    ff = w_up.shape[1]
    return line.run(
        functools.partial(ffn_back_body, slots),
        "ffn_back",
        15,
        (total // rows,),
        [
            (pooled_grad, rows_of(some, width)),
            (lengths, rows_of(rows, 1)),
            *((slope, rows_of(rows, ff // 2)) for slope in slopes),
            (middle, rows_of(rows, width)),
            (gain_ffn, fixed(gain_ffn.shape)),
            (w_up, fixed(w_up.shape)),
            (w_down, fixed(w_down.shape)),
        ],
        [
            ((total, ff), BF16, rows_of(rows, ff)),
            ((total, width), F32, rows_of(rows, width)),
            ((total, width), BF16, rows_of(rows, width)),
            ((1, width), F32, fixed((1, width))),
        ],
    )


def heads_back_body(slots, lengths_ref, w_out_ref, mixed_ref, grad_branch_ref, grad_mixed_ref):
    rows, width = grad_branch_ref.shape
    lengths = lengths_ref[...]
    grad_ctx = nt(grad_branch_ref[...], w_out_ref[...]).astype(BF16)
    row = lax.broadcasted_iota(jnp.int32, (GROUP, GROUP), 0)
    col = lax.broadcasted_iota(jnp.int32, (GROUP, GROUP), 1)
    same = row // slots == col // slots
    lows = range(0, width, PAIR)
    for base in range(0, rows, GROUP):
        span = slice(base, base + GROUP)
        valid = same & (row % slots <= lengths[span])
        queries = [mixed_ref[span, low : low + PAIR] for low in lows]
        keys = [split_heads(mixed_ref[span, width + low : width + low + PAIR]) for low in lows]
        values = [split_heads(mixed_ref[span, 2 * width + low : 2 * width + low + PAIR]) for low in lows]
        grad_pairs = [grad_ctx[span, low : low + PAIR] for low in lows]
        raws = [nt(key, query) for key, query in zip(keys, queries)]
        grad_raws = [nt(value, grad_pair) for value, grad_pair in zip(values, grad_pairs)]
        sides = (slice(0, GROUP), slice(GROUP, 2 * GROUP))
        heads = [raw[side] for raw in raws for side in sides]
        heads = [jnp.where(valid, head * HEAD_DIM ** (-0.5), -1000000000.0) for head in heads]
        heads = [jnp.exp(head - jnp.max(head, axis=0, keepdims=True)) for head in heads]
        probs = [head * (1.0 / jnp.sum(head, axis=0, keepdims=True)) for head in heads]
        grads = [grad_raw[side] for grad_raw in grad_raws for side in sides]
        grads = [
            prob * (grad - jnp.sum(grad * prob, axis=0, keepdims=True)) for prob, grad in zip(probs, grads)
        ]
        probs = [prob.astype(BF16) for prob in probs]
        grads = [(grad * HEAD_DIM ** (-0.5)).astype(BF16) for grad in grads]
        for j, low in enumerate(lows):
            scores_grad = jnp.concatenate(grads[2 * j : 2 * j + 2], axis=0)
            prob = jnp.concatenate(probs[2 * j : 2 * j + 2], axis=0)
            grad_mixed_ref[span, low : low + PAIR] = tn(scores_grad, keys[j]).astype(BF16)
            grad_keys = join_heads(mm(scores_grad, queries[j]))
            grad_mixed_ref[span, width + low : width + low + PAIR] = grad_keys.astype(BF16)
            grad_values = join_heads(mm(prob, grad_pairs[j]))
            grad_mixed_ref[span, 2 * width + low : 2 * width + low + PAIR] = grad_values.astype(BF16)


def heads_back(line, lengths, w_out, mixed, grad_branch, slots):
    total, width = grad_branch.shape
    rows = math.gcd(total, 256)
    return line.run(
        functools.partial(heads_back_body, slots),
        "heads_back",
        13,
        (total // rows,),
        [
            (lengths, rows_of(rows, 1)),
            (w_out, fixed(w_out.shape)),
            (mixed, rows_of(rows, 3 * width)),
            (grad_branch, rows_of(rows, width)),
        ],
        [((total, 3 * width), BF16, rows_of(rows, 3 * width))],
    )[0]


def attn_back_body(
    pieces_ref,
    scripts_ref,
    script_table_ref,
    gain_attn_ref,
    w_qkv_ref,
    grad_mixed_ref,
    grad_middle_ref,
    gain_ffn_grad_ref,
    grad_pieces_ref,
    small_ref,
):
    start, onehot = start_of(pieces_ref, scripts_ref, script_table_ref)
    grad_normed = nt(grad_mixed_ref[...], w_qkv_ref[...])
    unit, rate = center(start)
    grad, gain_grad = center_back(grad_normed, gain_attn_ref[...], unit, rate)
    grad_pieces = grad_middle_ref[...] + grad
    grad_pieces_ref[...] = grad_pieces.reshape(grad_pieces_ref.shape)

    groups = onehot.shape[1]

    @pl.when(pl.program_id(0) == 0)
    def _():
        small_ref[...] = jnp.zeros_like(small_ref)
        small_ref[groups + 1 : groups + 2] = gain_ffn_grad_ref[...]

    small_ref[groups : groups + 1] += gain_grad
    small_ref[:groups] += lax.dot_general(
        onehot, grad_pieces, (((0,), (0,)), ((), ())), precision=highest
    )


def attn_back(
    line, pieces, scripts, script_table, gain_attn, w_qkv, grad_mixed, grad_middle, gain_ffn_grad
):
    entries, slots, width = pieces.shape
    total = entries * slots
    rows = math.gcd(total, 256)
    some = rows // slots
    small = ((script_table.shape[0] + 2 + 15) // 16 * 16, width)
    return line.run(
        attn_back_body,
        "attn_back",
        9,
        (total // rows,),
        [
            (pieces, pl.BlockSpec((some, slots, width), lambda i, *_: (i, 0, 0))),
            (scripts, rows_of(rows, 1)),
            (script_table, fixed(script_table.shape)),
            (gain_attn, fixed(gain_attn.shape)),
            (w_qkv, fixed(w_qkv.shape)),
            (grad_mixed, rows_of(rows, 3 * width)),
            (grad_middle, rows_of(rows, width)),
            (gain_ffn_grad, fixed(gain_ffn_grad.shape)),
        ],
        [
            ((entries, slots, width), F32, pl.BlockSpec((some, slots, width), lambda i, *_: (i, 0, 0)), FAR),
            (small, F32, fixed(small)),
        ],
    )


PLAN = ("f t T f", "03 t f", "36 t f", "68 t f t", "w t E F", "Q")


def per_device(
    pieces,
    lengths,
    scripts,
    script_table,
    gain_attn,
    gain_ffn,
    w_qkv,
    w_out,
    w_up,
    w_down,
    w_proj,
    token_ids,
    out_grad,
):
    entries, slots, width = pieces.shape
    ent_count = lax.axis_size("ent")
    rep_count = lax.axis_size("rep")
    devices = ent_count * rep_count
    features = w_proj.shape[1]
    vocab = entries * devices
    rows_dev, text_len = token_ids.shape
    tokens = rows_dev * text_len
    levels = make_levels(ent_count, rep_count)
    sizes = tuple(size for _, size, _ in levels)
    me = lax.axis_index("ent") * rep_count + lax.axis_index("rep")
    chunks = 1 if devices <= 32 else 8
    each = entries // chunks
    span = vocab // chunks
    slot = slot_of(token_ids // entries ^ me, levels)
    within = token_ids % entries
    slot_ids = within // each * span + slot * each + within % each
    script_rows = jnp.repeat(scripts, slots)[:, None]
    length_rows = jnp.repeat(lengths, slots)[:, None]
    gain_attn, gain_ffn = gain_attn[None], gain_ffn[None]

    cut = len(levels)
    while math.prod(sizes[:cut]) * 16 > w_down.shape[0]:
        cut -= 1
    near, far = levels[:cut], levels[cut:]
    count = math.prod(sizes[:cut])
    slot_index = jnp.arange(count, dtype=jnp.int32) ^ slot_of(me, near)
    line = Line()

    def cut_up(keep, send, some):
        shape = tuple(size for _, size, _ in some[1:]) + keep.shape[-2:]
        return keep.reshape(shape), send.reshape(shape)

    parts, pooled_grads = [], []
    for chunk in range(chunks):
        first = chunk * span
        part_send, send = scatter_rows(
            line, slot_ids, out_grad, w_proj, first + span // 2, span // 2, BF16
        )
        part_keep, keep = scatter_rows(line, slot_ids, out_grad, w_proj, first, span // 2, F32)
        parts.append((part_keep, part_send))
        shape = sizes[1:] + (each, width)
        pooling = sum_halves(line, keep.reshape(shape), send.reshape(shape), levels, pooled_grads)
        if chunks > 1:
            for _ in pooling:
                pass
    next(pooling, None)
    next(pooling, None)
    normed, mixed, context, middle, normed_ffn = attn_forward(
        line, pieces, script_rows, length_rows, script_table, gain_attn, gain_ffn, w_qkv, w_out
    )
    next(pooling, None)
    length_cols = lengths[:, None]
    slope_a, hidden_a, pooled = ffn_forward(
        line, length_rows, length_cols, middle, normed_ffn, w_up, w_down, False
    )
    next(pooling, None)
    slope_b, hidden_b, pooled = ffn_forward(
        line, length_rows, length_cols, pooled, normed_ffn, w_up, w_down, True
    )
    for _ in pooling:
        pass
    grad_pooled = jnp.concatenate(pooled_grads, axis=0) if chunks > 1 else pooled_grads[0]

    held = [((), each, width, BF16, lambda index: [(0, (), ALL, 0, 0)])]
    halves = [[] for _ in range(chunks)]
    spreads = [
        gather_halves(
            line, stage(line, [(pooled[chunk * each :][:each], [])], held)[0], levels, halves[chunk]
        )
        for chunk in range(chunks)
    ]

    def spread_on():
        if chunks == 1:
            next(spreads[0])

    spread_on()
    down = tall_weight(line, slot_index, (hidden_a, hidden_b), grad_pooled.astype(BF16))
    grad_up, grad_middle, grad_branch, part_gain_ffn = ffn_back(
        line, grad_pooled, length_rows, (slope_a, slope_b), middle, gain_ffn, w_up, w_down
    )
    spread_on()
    up = wide_weight(line, slot_index, normed_ffn, grad_up)
    small, ffn_all, two_all = [], [], []
    ffn_sum = all_sum_two(
        line, *cut_up(*down, near), *cut_up(*up, near), lambda: small[0], near, far, ffn_all
    )
    next(ffn_sum)
    spread_on()
    grad_mixed = heads_back(line, length_rows, w_out, mixed, grad_branch, slots)
    next(ffn_sum)
    two = two_weights(line, slot_index, normed, grad_mixed, context, grad_branch)
    two_sum = all_sum(line, *cut_up(*two, near), near, far, two_all)
    next(two_sum)
    spread_on()
    grad_pieces, part_small = attn_back(
        line,
        pieces,
        script_rows,
        script_table,
        gain_attn,
        w_qkv,
        grad_mixed,
        grad_middle,
        part_gain_ffn,
    )
    small.append(part_small)
    results = {}

    def make_table():
        tables, total = [], None
        for chunk in range(chunks):
            for _ in spreads[chunk]:
                pass
            own, other = (value.reshape(span // 2, width) for value in halves[chunk])
            table, part = table_and_grad(line, own, other, w_proj, *parts[chunk])
            tables.append(table)
            total = part if total is None else total + part
        results["tables"] = tables
        results["proj"] = total, swap(total, levels[0])

    def look_up(first, last):
        before = results.get("looked_up")
        results["looked_up"] = lookup(line, slot_ids, results["tables"], (first, last), before)

    def add_proj():
        total, other = results["proj"]
        whole = [((), width, features, F32, lambda index: [(0, (), ALL, 0, 0)])]
        results["w_proj"] = stage(line, [(total, [other])], whole)[0]

    def end_ffn():
        results["w_down"] = unpack(line, slot_index, *map(merge, ffn_all[:2]), w_down.shape[0])
        results["w_up"], *results["small"] = unpack_extra(
            line,
            slot_index,
            *map(merge, ffn_all[2:]),
            *w_up.shape,
            (script_table.shape[0], 1, 1),
            math.prod(sizes[3:cut]),
        )

    def end_two():
        for _ in two_sum:
            pass
        results["w_qkv"], results["w_out"] = unpack_two(
            line, slot_index, *map(merge, two_all), *w_qkv.shape
        )

    acts = {
        "f": lambda: next(ffn_sum, 0),
        "t": lambda: next(two_sum, 0),
        "T": make_table,
        "w": add_proj,
        "E": lambda: list(ffn_sum),
        "F": end_ffn,
        "Q": end_two,
    }
    for act in (act for part in PLAN for act in part.split()):
        if act.isdigit():
            look_up(int(act[0]), int(act[1]))
        else:
            acts[act]()
    looked_up, grad_w_proj = results["looked_up"], results["w_proj"]
    grad_w_down, grad_w_up = results["w_down"], results["w_up"]
    grad_w_qkv, grad_w_out = results["w_qkv"], results["w_out"]
    grad_script, grad_gain_attn, grad_gain_ffn = results["small"]
    return (
        looked_up,
        grad_pieces,
        grad_script,
        grad_gain_attn.reshape(width),
        grad_gain_ffn.reshape(width),
        grad_w_qkv,
        grad_w_out,
        grad_w_up,
        grad_w_down,
        grad_w_proj,
    )


def solution(mesh):
    in_specs = (
        P(("ent", "rep"), None, None),
        P(("ent", "rep")),
        P(("ent", "rep")),
        P(),
        P(),
        P(),
        P(),
        P(),
        P(),
        P(),
        P(None, "ent"),
        P("rep", None),
        P("ent", "rep", None),
    )
    out_specs = (
        P("ent", "rep", None),
        P(("ent", "rep"), None, None),
        P(),
        P(),
        P(),
        P(),
        P(),
        P(),
        P(),
        P(None, "ent"),
    )
    return jax.shard_map(
        per_device, mesh=mesh, in_specs=in_specs, out_specs=out_specs, check_vma=False
    )
```

```python
import functools
import math

import jax
import jax.numpy as jnp
import numpy as np
from jax import lax
from jax.experimental import pallas as pl
from jax.experimental.pallas import tpu as pltpu
from jax.sharding import PartitionSpec as P

HEADS = 8
HEAD_DIM = 64
F32 = jnp.float32
BF16 = jnp.bfloat16
highest = lax.Precision.HIGHEST
MIB = 1024 * 1024


def make_levels(ent_count, rep_count):
    levels = [("rep", rep_count, 0)]
    bit, total = 0, ent_count.bit_length() - 1
    while bit < total:
        width = 1 if bit < 2 else min(2, total - bit)
        levels.append(("ent", 1 << width, bit))
        bit += width
    return levels


def slot_of(number, levels):
    rep_count = levels[0][1]
    slot = number % rep_count
    ent = number // rep_count
    for _, size, shift in levels[1:]:
        slot = slot * size + (ent >> shift) % size
    return slot


def swap(value, level, k):
    name, size, shift = level
    count = lax.axis_size(name)
    return lax.ppermute(value, name, [(i, i ^ (k << shift)) for i in range(count)])


def merge(value):
    return value.reshape((-1,) + value.shape[-2:])


FAR = True


class Line:
    def __init__(self):
        self.last = []

    def run(self, body, name, micros, grid, ins, outs, prefetch=(), alias=None, room=24 * MIB, scratch=()):
        count = len(prefetch) + len(ins)
        extra = self.last + ([] if alias is None else [alias])
        token = (8, 128)

        def wrapped(*refs):
            held = len(refs) - len(scratch)
            refs[held - 1][...] = jnp.zeros(token, F32)
            body(*refs[:count], *refs[count + len(extra) : held - 1], *refs[held:])

        *results, last = pl.pallas_call(
            wrapped,
            grid_spec=pltpu.PrefetchScalarGridSpec(
                num_scalar_prefetch=len(prefetch),
                grid=grid,
                in_specs=[spec for _, spec in ins] + [pl.BlockSpec(memory_space=pl.ANY)] * len(extra),
                out_specs=[spec for _, _, spec, *_ in outs] + [pl.BlockSpec(token, lambda *_: (0, 0))],
                scratch_shapes=scratch,
            ),
            out_shape=[
                pltpu.HBM(shape, dtype) if far else jax.ShapeDtypeStruct(shape, dtype)
                for shape, dtype, _, *far in outs
            ]
            + [jax.ShapeDtypeStruct(token, F32)],
            input_output_aliases={} if alias is None else {count + len(extra) - 1: 0},
            compiler_params=pltpu.CompilerParams(vmem_limit_bytes=room),
            cost_estimate=pl.CostEstimate(
                flops=int(micros * 3e9), bytes_accessed=int(micros * 9e6), transcendentals=0
            ),
            name=name,
        )(*prefetch, *(value for value, _ in ins), *extra)
        self.last = [last]
        return results


def swap(value, level, k=1):
    name, size, shift = level
    count = lax.axis_size(name)
    return lax.ppermute(value, name, [(i, i ^ (k << shift)) for i in range(count)])


def swaps(values, level):
    return [swap(value, level, k) for k, value in enumerate(values, 1)]


ALL = slice(None)
BELOW = 16


def stage_body(layout, cuts, *refs):
    sums, position = [], 0
    for number in layout:
        sums.append(refs[position : position + number])
        position += number

    def piece(number, index, cols, rows=ALL):
        total = sums[number][0][index][rows, cols]
        for ref in sums[number][1:]:
            total = total.astype(F32) + ref[index][rows, cols].astype(F32)
        return total

    for out_ref, sources in zip(refs[position:], cuts):
        for target, parts in sources:
            for number, index, cols, row, col, *rows in parts:
                value = piece(number, index, cols, *rows).astype(out_ref.dtype)
                where = target + (slice(row, row + value.shape[0]), slice(col, col + value.shape[1]))
                out_ref[where] = value


def stage(line, sums, outs, steps=1):
    values = [value for kept, received in sums for value in [kept, *received]]

    def spec(shape):
        return pl.BlockSpec(memory_space=pltpu.VMEM)

    cuts = [
        [(target, source(target)) for target in np.ndindex(*lead)] for lead, _, _, _, source in outs
    ]
    shapes = [(lead + (rows, cols), dtype) for lead, rows, cols, dtype, _ in outs]
    held = [(value.shape, value.dtype) for value in values] + [(shape, jnp.dtype(dtype)) for shape, dtype in shapes]
    return line.run(
        functools.partial(stage_body, [1 + len(received) for _, received in sums], cuts),
        "exchange",
        0.5,
        (),
        [(value, spec(value.shape)) for value in values],
        [(shape, dtype, spec(shape)) for shape, dtype in shapes],
        room=2 * MIB + sum(math.prod(shape) * dtype.itemsize for shape, dtype in held),
    )


def split(number, value, axis, cols=ALL, width=None):
    lead = value.shape[:-2]
    rest = lead[:axis] + lead[axis + 1 :]
    outs = []
    for k in range(lead[axis]):

        def source(index, k=k):
            return [(number, index[:axis] + (k,) + index[axis:], cols, 0, 0)]

        outs.append((rest, value.shape[-2], width or value.shape[-1], F32 if k == 0 else BF16, source))
    return outs


def stacked(numbers, value, axis, rows=ALL):
    lead = value.shape[:-2]
    shape = lead[:axis] + (len(numbers),) + lead[axis:]

    def source(index):
        return [(numbers[index[axis]], index[:axis] + index[axis + 1 :], ALL, 0, 0)]

    return (shape, value.shape[-2], value.shape[-1], value.dtype, source)


def finish(line, sums, far, shape, dtype):
    whole = [(0, (), ALL, 0, 0)]
    for level in far:
        outs = [((), *shape, kind, lambda index: whole) for kind in (F32, BF16)]
        keep, send = stage(line, sums, outs)
        sums = [(keep, [swap(send, level, k) for k in range(1, level[1])])]
        yield
    yield stage(line, sums, [((), *shape, dtype, lambda index: whole)])[0]


def sum_halves(line, keep, send, levels, out, far=(), dtype=F32):
    received = swap(send, levels[0])
    yield
    rows, width = keep.shape[-2:]
    half = width // 2
    left, right = slice(0, half), slice(half, width)
    steps = 4 if rows % 64 == 0 else 1
    outs = split(0, keep, 0, left, half) + split(0, keep, 1, right, half)
    keep_a, send_a, keep_b, send_b = stage(line, [(keep, [received])], outs, steps)
    got_a, got_b = swap(send_a, levels[1]), swap(send_b, levels[2])
    yield
    outs = split(0, keep_a, 0) + split(1, keep_b, 0)
    sums = [(keep_a, [got_a]), (keep_b, [got_b])]
    keep_a, send_a, keep_b, send_b = stage(line, sums, outs, steps)
    sums = [(keep_a, [swap(send_a, levels[2])]), (keep_b, [swap(send_b, levels[1])])]
    yield
    for place, level in enumerate(levels[3:]):
        if place == 0:
            lead = keep_a.shape[1:-2]

            def source(index, k):
                return [(0, (k,) + index, ALL, 0, 0), (1, (k,) + index, ALL, 0, half)]

            outs = [
                (lead, rows, width, F32 if k == 0 else BF16, functools.partial(source, k=k))
                for k in range(level[1])
            ]
        else:
            outs = split(0, keep, 0)
        keep, *sends = stage(line, sums, outs)
        sums = [(keep, swaps(sends, level))]
        yield
    for value in finish(line, sums, far, (rows, width), dtype):
        if value is None:
            yield
    out.append(value)


def gather_halves(line, value, levels, out):
    rows, width = value.shape
    half = width // 2
    for place, level in reversed(list(enumerate(levels[3:]))):
        got = [swap(value, level, k) for k in range(1, level[1])]
        yield
        parts = [(part, []) for part in [value, *got]]
        numbers = list(range(level[1]))
        if place:
            value = stage(line, parts, [stacked(numbers, value, 0)])[0]
        else:
            lead = (level[1],) + value.shape[:-2]

            def source(index, cols):
                return [(index[0], index[1:], cols, 0, 0)]

            outs = [
                (lead, rows, half, BF16, functools.partial(source, cols=cols))
                for cols in (slice(0, half), slice(half, width))
            ]
            value_a, value_b = stage(line, parts, outs)
    got_a, got_b = swap(value_a, levels[2]), swap(value_b, levels[1])
    yield
    sums = [(part, []) for part in (value_a, got_a, value_b, got_b)]
    outs = [stacked([0, 1], value_a, 0), stacked([2, 3], value_b, 0)]
    value_a, value_b = stage(line, sums, outs)
    got_a, got_b = swap(value_a, levels[1]), swap(value_b, levels[2])
    yield
    sums = [(part, []) for part in (value_a, got_a, value_b, got_b)]
    lead = (2,) + value_a.shape[:-2]

    def joined(index):
        left, right = index[0], index[1]
        return [(left, index[1:], ALL, 0, 0), (2 + right, (left,) + index[2:], ALL, 0, half)]

    value = stage(line, sums, [(lead, rows, width, BF16, joined)])[0]
    out += [value, swap(value, levels[0])]
    yield


def all_sum(line, keep, send, near, far, out):
    mine = []
    yield from sum_halves(line, keep, send, near, mine, far, BF16)
    yield from gather_halves(line, mine[0], near, out)


def all_sum_two(line, keep_a, send_a, keep_b, send_b, extra, near, far, out):
    got_a, got_b = swap(send_a, near[0]), swap(send_b, near[0])
    yield
    rows = keep_a.shape[-2]
    outs = split(0, keep_a, 0) + split(1, keep_b, 1)
    keep_a, send_a, keep_b, send_b = stage(line, [(keep_a, [got_a]), (keep_b, [got_b])], outs)
    got_a, got_b = swap(send_a, near[1]), swap(send_b, near[2])
    yield
    outs = split(0, keep_a, 0) + split(1, keep_b, 0)
    keep_a, send_a, keep_b, send_b = stage(line, [(keep_a, [got_a]), (keep_b, [got_b])], outs)
    sums = [(keep_a, [swap(send_a, near[2])]), (keep_b, [swap(send_b, near[1])])]
    yield
    below = extra()
    added = below.shape[0]
    for place, level in enumerate(near[3:]):
        if place == 0:
            lead = keep_a.shape[1:-2]
            sums = sums + [(below, [])]

            def source(index, k):
                places = [(0, (k,) + index, 0), (1, (k,) + index, rows), (2, (), 2 * rows)]
                return [(number, where, ALL, row, 0) for number, where, row in places]

            outs = [
                (lead, 2 * rows + added, PANEL, F32 if k == 0 else BF16, functools.partial(source, k=k))
                for k in range(level[1])
            ]
        else:
            outs = split(0, keep, 0)
        keep, *sends = stage(line, sums, outs)
        sums = [(keep, swaps(sends, level))]
        yield
    for level in far:
        outs = [((), 2 * rows + added, PANEL, kind, lambda index: [(0, (), ALL, 0, 0)]) for kind in (F32, BF16)]
        keep, send = stage(line, sums, outs)
        sums = [(keep, [swap(send, level, k) for k in range(1, level[1])])]
        yield
    outs = [
        ((), size, PANEL, BF16, lambda index, part=part: [(0, (), ALL, 0, 0, part)])
        for size, part in ((2 * rows, slice(0, 2 * rows)), (added, slice(2 * rows, 2 * rows + added)))
    ]
    value, below = stage(line, sums, outs)
    for place, level in reversed(list(enumerate(near[3:]))):
        got = [swap(value, level, k) for k in range(1, level[1])]
        yield
        numbers = list(range(level[1]))
        parts = [(part, []) for part in [value, *got]]
        if place:
            value = stage(line, parts, [stacked(numbers, value, 0)])[0]
            continue
        lead = (level[1],) + value.shape[:-2]

        def first(index):
            return [(index[0], index[1:], ALL, 0, 0, slice(0, rows))]

        def second(index):
            number = int(np.ravel_multi_index(index, lead)) * BELOW % added
            return [
                (index[0], index[1:], ALL, 0, 0, slice(rows, 2 * rows)),
                (len(numbers), (), ALL, rows, 0, slice(number, number + BELOW)),
            ]

        outs = [(lead, rows, PANEL, BF16, first), (lead, rows + BELOW, PANEL, BF16, second)]
        value_a, value_b = stage(line, parts + [(below, [])], outs)
    got_a, got_b = swap(value_a, near[2]), swap(value_b, near[1])
    yield
    sums = [(part, []) for part in (value_a, got_a, value_b, got_b)]
    outs = [stacked([0, 1], value_a, 0), stacked([2, 3], value_b, 0)]
    value_a, value_b = stage(line, sums, outs)
    got_a, got_b = swap(value_a, near[1]), swap(value_b, near[2])
    yield
    sums = [(part, []) for part in (value_a, got_a, value_b, got_b)]
    outs = [stacked([0, 1], value_a, 0), stacked([2, 3], value_b, 1)]
    value_a, value_b = stage(line, sums, outs)
    out += [value_a, swap(value_a, near[0]), value_b, swap(value_b, near[0])]
    yield


def fixed(shape):
    return pl.BlockSpec(shape, lambda i, *_: (0,) * len(shape))


def rows_of(rows, width):
    return pl.BlockSpec((rows, width), lambda i, *_: (i, 0))


def selector(ids, base, rows):
    entry = lax.broadcasted_iota(jnp.int32, (rows, 1), 0).astype(jnp.int16)
    return jnp.where(entry == (ids - base).astype(jnp.int16), jnp.ones((), BF16), jnp.zeros((), BF16))


def nt(left, right):
    return lax.dot_general(left, right, (((1,), (1,)), ((), ())), preferred_element_type=F32)


def tn(left, right):
    return lax.dot_general(left, right, (((0,), (0,)), ((), ())), preferred_element_type=F32)


def mm(left, right):
    return jnp.dot(left, right, preferred_element_type=F32)


def scatter_body(first, ids_ref, grad_ref, proj_ref, table_ref, pooled_ref, flat_ref):
    @pl.when(pl.program_id(0) == 0)
    def _():
        flat_ref[...] = grad_ref[...].reshape(flat_ref.shape)

    rows = table_ref.shape[0]
    some = min(256, rows)
    parts = []
    for low in range(0, rows, some):
        base = first + pl.program_id(0) * rows + low
        picks = [selector(ids_ref[row : row + 1], base, some) for row in range(ids_ref.shape[0])]
        parts.append(nt(jnp.concatenate(picks, axis=1), flat_ref[...]))
    part = jnp.concatenate(parts, axis=0).astype(BF16)
    table_ref[...] = part
    pooled_ref[...] = nt(part, proj_ref[...]).astype(pooled_ref.dtype)


def scatter_rows(line, ids, grad, w_proj, first, count, dtype):
    features = grad.shape[0]
    width = w_proj.shape[0]
    rows = min(1024, count)
    return line.run(
        functools.partial(scatter_body, first),
        "scatter_rows",
        14,
        (count // rows,),
        [
            (ids, fixed(ids.shape)),
            (grad, pl.BlockSpec(memory_space=pltpu.VMEM)),
            (w_proj, fixed(w_proj.shape)),
        ],
        [
            ((count, features), BF16, rows_of(rows, features), FAR),
            ((count, width), dtype, rows_of(rows, width)),
        ],
        room=28 * MIB,
        scratch=[pltpu.VMEM((features, ids.size), BF16)],
    )


def table_body(steps, own_ref, other_ref, proj_ref, part_own_ref, part_other_ref, table_ref, grad_ref):
    step = pl.program_id(0)

    @pl.when(step == 0)
    def _():
        grad_ref[...] = jnp.zeros_like(grad_ref)

    def one(pooled_ref, part_ref):
        pooled = pooled_ref[...]
        cols = lax.dot_general(
            proj_ref[...], pooled, (((0,), (1,)), ((), ())), preferred_element_type=F32
        )
        table_ref[...] = cols.astype(BF16)
        grad_ref[...] += tn(pooled, part_ref[...])

    @pl.when(step < steps)
    def _():
        one(own_ref, part_own_ref)

    @pl.when(step >= steps)
    def _():
        one(other_ref, part_other_ref)


def table_and_grad(line, own, other, w_proj, part_own, part_other):
    count, width = own.shape
    features = w_proj.shape[1]
    rows = min(1024, count)
    steps = count // rows

    def first(cols):
        return pl.BlockSpec((rows, cols), lambda i, *_: (jnp.minimum(i, steps - 1), 0))

    def second(cols):
        return pl.BlockSpec((rows, cols), lambda i, *_: (jnp.maximum(i - steps, 0), 0))

    return line.run(
        functools.partial(table_body, steps),
        "table_and_grad",
        5,
        (2 * steps,),
        [
            (own, first(width)),
            (other, second(width)),
            (w_proj, fixed(w_proj.shape)),
            (part_own, first(features)),
            (part_other, second(features)),
        ],
        [
            ((features, 2 * count), BF16, pl.BlockSpec((features, rows), lambda i, *_: (0, i))),
            ((width, features), F32, fixed((width, features))),
        ],
    )


def lookup_body(chunk, ids_ref, *refs):
    table_refs, out_ref = refs[:-1], refs[-1]
    rows = ids_ref.shape[0]

    def find(base, table):
        picks = [selector(ids_ref[row : row + 1], base, chunk) for row in range(rows)]
        return mm(table, jnp.concatenate(picks, axis=1))

    total = None
    for index, table_ref in enumerate(table_refs):
        vocab = table_ref.shape[1]
        for inner in range(0, vocab, chunk):
            part = find(index * vocab + inner, table_ref[:, inner : inner + chunk])
            total = part if total is None else total + part
    out_ref[...] = total.astype(BF16).reshape(out_ref.shape)


def lookup(line, ids, tables, part, before=None):
    rows, text_len = ids.shape
    features, vocab = tables[0].shape
    block = text_len // 8
    first, last = part
    return line.run(
        functools.partial(lookup_body, min(vocab, 4096)),
        "lookup",
        3 * (last - first),
        (last - first,),
        [(ids, pl.BlockSpec((rows, block), lambda i, *_: (0, i + first)))]
        + [(table, fixed(table.shape)) for table in tables],
        [
            (
                (features, rows, text_len),
                BF16,
                pl.BlockSpec((features, rows, block), lambda i, *_: (0, 0, i + first)),
                FAR,
            )
        ],
        alias=before,
    )[0]


PANEL = 512


def store_slots(slots_ref, first, part, keep_ref, send_ref):
    half, rows, _ = keep_ref.shape
    for j in range(part.shape[0] // rows):
        slot = slots_ref[first + j]
        piece = part[j * rows : (j + 1) * rows]

        @pl.when(slot < half)
        def _():
            keep_ref[slot] = piece

        @pl.when(slot >= half)
        def _():
            send_ref[slot - half] = piece.astype(BF16)


def weight_body(slots_ref, left_ref, right_ref, keep_ref, send_ref):
    part = tn(left_ref[...], right_ref[...])
    store_slots(slots_ref, pl.program_id(0) * (part.shape[0] // keep_ref.shape[1]), part, keep_ref, send_ref)


def tall_body(steps, slots_ref, first_ref, second_ref, right_ref, keep_ref, send_ref):
    step = pl.program_id(0)
    each = PANEL // keep_ref.shape[1]

    @pl.when(step < steps)
    def _():
        store_slots(slots_ref, step * each, tn(first_ref[...], right_ref[...]), keep_ref, send_ref)

    @pl.when(step >= steps)
    def _():
        store_slots(slots_ref, step * each, tn(second_ref[...], right_ref[...]), keep_ref, send_ref)


def two_weights_body(last, slots_ref, left_ref, right_ref, left2_ref, right2_ref, keep_ref, send_ref):
    step = pl.program_id(0)
    each = left_ref.shape[1] // keep_ref.shape[1]

    @pl.when(step < last)
    def _():
        store_slots(slots_ref, step * each, tn(left_ref[...], right_ref[...]), keep_ref, send_ref)

    @pl.when(step == last)
    def _():
        store_slots(slots_ref, step * each, tn(left2_ref[...], right2_ref[...]), keep_ref, send_ref)


def slot_outs(count, rows):
    shape = (count // 2, rows, PANEL)
    return [(shape, F32, fixed(shape)), (shape, BF16, fixed(shape))]


def panel_of(depth):
    return pl.BlockSpec((depth, PANEL), lambda i, *_: (0, i))


def tall_weight(line, slots, lefts, right):
    depth, half = lefts[0].shape
    steps = half // PANEL
    return line.run(
        functools.partial(tall_body, steps),
        "tall_weight",
        3,
        (2 * steps,),
        [
            (lefts[0], pl.BlockSpec((depth, PANEL), lambda i, *_: (0, jnp.minimum(i, steps - 1)))),
            (lefts[1], pl.BlockSpec((depth, PANEL), lambda i, *_: (0, jnp.maximum(i - steps, 0)))),
            (right, fixed(right.shape)),
        ],
        slot_outs(slots.shape[0], 2 * half // slots.shape[0]),
        [slots],
    )


def wide_weight(line, slots, left, right):
    depth, cols = right.shape
    return line.run(
        weight_body,
        "wide_weight",
        8,
        (cols // PANEL,),
        [(left, fixed(left.shape)), (right, panel_of(depth))],
        slot_outs(slots.shape[0], cols // PANEL * left.shape[1] // slots.shape[0]),
        [slots],
    )


def two_weights(line, slots, left, right, left2, right2):
    depth, cols = right.shape
    last = cols // PANEL
    return line.run(
        functools.partial(two_weights_body, last),
        "two_weights",
        5,
        (last + 1,),
        [
            (left, fixed(left.shape)),
            (right, pl.BlockSpec((depth, PANEL), lambda i, *_: (0, jnp.minimum(i, last - 1)))),
            (left2, fixed(left2.shape)),
            (right2, fixed(right2.shape)),
        ],
        slot_outs(slots.shape[0], (last + 1) * left.shape[1] // slots.shape[0]),
        [slots],
    )


def load_slots(slots_ref, first, own_ref, other_ref, out_ref, rows):
    half = own_ref.shape[0]
    for j in range(out_ref.shape[0] // rows):
        slot = slots_ref[first + j]

        @pl.when(slot < half)
        def _():
            out_ref[j * rows : (j + 1) * rows] = own_ref[slot, :rows].astype(F32)

        @pl.when(slot >= half)
        def _():
            out_ref[j * rows : (j + 1) * rows] = other_ref[slot - half, :rows].astype(F32)


def unpack_body(slots_ref, own_ref, other_ref, out_ref):
    rows = own_ref.shape[1]
    each = out_ref.shape[0] // rows
    load_slots(slots_ref, pl.program_id(0) * each, own_ref, other_ref, out_ref, rows)


def unpack(line, slots, own, other, height):
    tile = min(512, height)
    return line.run(
        unpack_body,
        "unpack",
        5,
        (height // tile,),
        [(own, fixed(own.shape)), (other, fixed(other.shape))],
        [((height, PANEL), F32, pl.BlockSpec((tile, PANEL), lambda i, *_: (i, 0)), FAR)],
        [slots],
    )[0]


def unpack_extra_body(rows, inner, slots_ref, own_ref, other_ref, out_ref, *extra_refs):
    each = out_ref.shape[0] // rows
    load_slots(slots_ref, pl.program_id(0) * each, own_ref, other_ref, out_ref, rows)

    @pl.when(pl.program_id(0) == 0)
    def _():
        needed = sum(ref.shape[0] for ref in extra_refs)
        sums = []
        for place in range((needed + BELOW - 1) // BELOW):
            total = jnp.zeros((BELOW, PANEL), F32)
            for ref in (own_ref, other_ref):
                for slot in range(place, ref.shape[0], inner):
                    total += ref[slot, rows:].astype(F32)
            sums.append(total)
        total = jnp.concatenate(sums, axis=0)
        first = 0
        for ref in extra_refs:
            ref[...] = total[first : first + ref.shape[0]]
            first += ref.shape[0]


def unpack_extra(line, slots, own, other, height, cols, extra, inner):
    return line.run(
        functools.partial(unpack_extra_body, height * cols // PANEL // slots.shape[0], inner),
        "unpack",
        5,
        (cols // PANEL,),
        [(own, fixed(own.shape)), (other, fixed(other.shape))],
        [((height, cols), F32, pl.BlockSpec((height, PANEL), lambda i, *_: (0, i)), FAR)]
        + [((rows, PANEL), F32, fixed((rows, PANEL))) for rows in extra],
        [slots],
    )


def unpack_two_body(last, slots_ref, own_ref, other_ref, out_ref, out2_ref):
    step = pl.program_id(0)
    rows = own_ref.shape[1]
    each = out_ref.shape[0] // rows

    @pl.when(step < last)
    def _():
        load_slots(slots_ref, step * each, own_ref, other_ref, out_ref, rows)

    @pl.when(step == last)
    def _():
        load_slots(slots_ref, step * each, own_ref, other_ref, out2_ref, rows)


def unpack_two(line, slots, own, other, height, cols):
    last = cols // PANEL
    return line.run(
        functools.partial(unpack_two_body, last),
        "unpack_two",
        5,
        (last + 1,),
        [(own, fixed(own.shape)), (other, fixed(other.shape))],
        [
            (
                (height, cols),
                F32,
                pl.BlockSpec((height, PANEL), lambda i, *_: (0, jnp.minimum(i, last - 1))),
                FAR,
            ),
            ((height, PANEL), F32, fixed((height, PANEL)), FAR),
        ],
        [slots],
    )


GROUP = 128
PAIR = 2 * HEAD_DIM
GELU_SCALE = 0.7978845608028654
GELU_CUBE = 0.044715


def center(values):
    centered = values - jnp.mean(values, axis=-1, keepdims=True)
    spread = jnp.mean(centered * centered, axis=-1, keepdims=True)
    rate = lax.rsqrt(spread + 1e-05)
    return centered * rate, rate


def center_back(grad, gain, unit, rate):
    gain_grad = jnp.sum(grad * unit, axis=0, keepdims=True)
    grad = grad * gain
    mean_grad = jnp.mean(grad, axis=-1, keepdims=True)
    mean_unit = jnp.mean(grad * unit, axis=-1, keepdims=True)
    return rate * (grad - mean_grad - unit * mean_unit), gain_grad


def start_of(pieces_ref, scripts_ref, script_table_ref):
    entries, slots, width = pieces_ref.shape
    groups = script_table_ref.shape[0]
    pieces = pieces_ref[...].astype(F32).reshape(entries * slots, width)
    onehot = (scripts_ref[...] == lax.broadcasted_iota(jnp.int32, (1, groups), 1)).astype(F32)
    return pieces + jnp.dot(onehot, script_table_ref[...], precision=highest), onehot


def slot_weights(lengths, slots):
    rows = lengths.shape[0]
    slot = lax.broadcasted_iota(jnp.int32, (rows, 1), 0) % slots
    return jnp.where(slot <= lengths, 1.0 / (lengths + 1).astype(F32), 0.0)


def split_heads(pair):
    first = lax.broadcasted_iota(jnp.int32, pair.shape, 1) < HEAD_DIM
    zero = jnp.zeros_like(pair)
    return jnp.concatenate([jnp.where(first, pair, zero), jnp.where(first, zero, pair)], axis=0)


def join_heads(stacked):
    first = lax.broadcasted_iota(jnp.int32, (GROUP, PAIR), 1) < HEAD_DIM
    return jnp.where(first, stacked[:GROUP], stacked[GROUP:])


def attn_body(
    slots,
    pieces_ref,
    scripts_ref,
    lengths_ref,
    script_table_ref,
    gain_attn_ref,
    gain_ffn_ref,
    w_qkv_ref,
    w_out_ref,
    normed_ref,
    mixed_ref,
    context_ref,
    middle_ref,
    normed_ffn_ref,
):
    start, _ = start_of(pieces_ref, scripts_ref, script_table_ref)
    rows, width = start.shape
    lengths = lengths_ref[...]
    normed = (center(start)[0] * gain_attn_ref[...]).astype(BF16)
    normed_ref[...] = normed
    mixed = mm(normed, w_qkv_ref[...]).astype(BF16)
    mixed_ref[...] = mixed
    row = lax.broadcasted_iota(jnp.int32, (GROUP, GROUP), 0)
    col = lax.broadcasted_iota(jnp.int32, (GROUP, GROUP), 1)
    groups = []
    for base in range(0, rows, GROUP):
        part = mixed[base : base + GROUP]
        valid = (row // slots == col // slots) & (col % slots <= lengths[base : base + GROUP])
        lows = range(0, width, PAIR)
        raws = [
            nt(part[:, low : low + PAIR], split_heads(part[:, width + low : width + low + PAIR]))
            for low in lows
        ]
        heads = [raw[:, side : side + GROUP] for raw in raws for side in (0, GROUP)]
        heads = [jnp.where(valid, head * HEAD_DIM ** (-0.5), -1000000000.0) for head in heads]
        heads = [jnp.exp(head - jnp.max(head, axis=1, keepdims=True)) for head in heads]
        heads = [(head * (1.0 / jnp.sum(head, axis=1, keepdims=True))).astype(BF16) for head in heads]
        pairs = [
            mm(
                jnp.concatenate(heads[2 * j : 2 * j + 2], axis=1),
                split_heads(part[:, 2 * width + low : 2 * width + low + PAIR]),
            )
            for j, low in enumerate(lows)
        ]
        groups.append(jnp.concatenate(pairs, axis=1).astype(BF16))
    context = jnp.concatenate(groups, axis=0)
    context_ref[...] = context
    middle = start + mm(context, w_out_ref[...])
    middle_ref[...] = middle
    normed_ffn_ref[...] = (center(middle)[0] * gain_ffn_ref[...]).astype(BF16)


def attn_forward(
    line, pieces, scripts, lengths, script_table, gain_attn, gain_ffn, w_qkv, w_out
):
    entries, slots, width = pieces.shape
    total = entries * slots
    rows = math.gcd(total, 256)
    some = rows // slots
    whole = (script_table, gain_attn, gain_ffn, w_qkv, w_out)
    return line.run(
        functools.partial(attn_body, slots),
        "attn_forward",
        12,
        (total // rows,),
        [
            (pieces, pl.BlockSpec((some, slots, width), lambda i, *_: (i, 0, 0))),
            (scripts, rows_of(rows, 1)),
            (lengths, rows_of(rows, 1)),
        ]
        + [(value, fixed(value.shape)) for value in whole],
        [
            ((total, width), BF16, rows_of(rows, width)),
            ((total, 3 * width), BF16, rows_of(rows, 3 * width), FAR),
            ((total, width), BF16, rows_of(rows, width)),
            ((total, width), F32, rows_of(rows, width)),
            ((total, width), BF16, rows_of(rows, width)),
        ],
    )


def ffn_body(
    slots,
    last,
    length_rows_ref,
    lengths_ref,
    before_ref,
    normed_ref,
    w_up_ref,
    w_down_ref,
    slope_ref,
    hidden_ref,
    pooled_ref,
):
    rows, width = normed_ref.shape
    some = rows // slots
    row = lax.broadcasted_iota(jnp.int32, (some, rows), 1)
    entry = lax.broadcasted_iota(jnp.int32, (some, rows), 0)
    lengths = lengths_ref[...]
    valid = (row // slots == entry) & (row % slots <= lengths)
    valid = jnp.where(valid, 1.0, 0.0).astype(BF16)
    scale = 1.0 / (lengths + 1).astype(F32)
    pooled = before_ref[...]
    if not last:
        weights = slot_weights(length_rows_ref[...], slots)
        pooled = jnp.sum((pooled * weights).reshape(some, slots, width), axis=1)
    ff = w_up_ref.shape[1]
    step = ff // 2
    for low in range(0, ff, step):
        up = mm(normed_ref[...], w_up_ref[:, low : low + step])
        square = up * up
        tanh = jnp.tanh(up * (GELU_SCALE + GELU_SCALE * GELU_CUBE * square))
        half_up = 0.5 * up
        hidden = (half_up + half_up * tanh).astype(BF16)
        slope_ref[:, low : low + step] = (0.5 + 0.5 * tanh) + half_up * (1.0 - tanh * tanh) * (
            GELU_SCALE + 3.0 * GELU_SCALE * GELU_CUBE * square
        )
        mean_hidden = mm(valid, hidden) * scale
        high = mean_hidden.astype(BF16)
        rest = (mean_hidden - high.astype(F32)).astype(BF16)
        hidden_ref[:, low : low + step] = high
        w_down = w_down_ref[low : low + step]
        pooled += mm(high, w_down) + mm(rest, w_down)
    pooled_ref[...] = pooled.astype(pooled_ref.dtype)


def ffn_forward(line, length_rows, lengths, before, normed, w_up, w_down, last):
    total, width = normed.shape
    entries = lengths.shape[0]
    slots = total // entries
    rows = math.gcd(total, 256)
    some = rows // slots
    ff = w_up.shape[1] // 2
    return line.run(
        functools.partial(ffn_body, slots, last),
        "ffn_forward",
        7,
        (total // rows,),
        [
            (length_rows, rows_of(rows, 1)),
            (lengths, rows_of(some, 1)),
            (before, rows_of(some if last else rows, width)),
            (normed, rows_of(rows, width)),
            (w_up, pl.BlockSpec((width, ff), lambda i, *_: (0, int(last)))),
            (w_down, pl.BlockSpec((ff, width), lambda i, *_: (int(last), 0))),
        ],
        [
            ((total, ff), F32, rows_of(rows, ff), FAR),
            ((entries, ff), BF16, rows_of(some, ff)),
            ((entries, width), BF16 if last else F32, rows_of(some, width)),
        ],
    )


def ffn_back_body(
    slots,
    pooled_grad_ref,
    lengths_ref,
    slope_a_ref,
    slope_b_ref,
    middle_ref,
    gain_ffn_ref,
    w_up_ref,
    w_down_ref,
    grad_up_ref,
    grad_middle_ref,
    grad_branch_ref,
    gain_grad_ref,
):
    pooled_grad = pooled_grad_ref[...]
    rows, width = middle_ref.shape
    some = rows // slots
    wide = jnp.broadcast_to(pooled_grad[:, None, :], (some, slots, width)).reshape(rows, width)
    grad_final = wide * slot_weights(lengths_ref[...], slots)
    grad_ffn = grad_final.astype(BF16)
    ff = w_up_ref.shape[1]
    step = ff // 4
    grad_normed = jnp.zeros((rows, width), F32)
    for low in range(0, ff, step):
        grad_hidden = nt(grad_ffn, w_down_ref[low : low + step])
        slope_ref, inner = (slope_a_ref, low) if low < ff // 2 else (slope_b_ref, low - ff // 2)
        grad_up = (slope_ref[:, inner : inner + step] * grad_hidden).astype(BF16)
        grad_up_ref[:, low : low + step] = grad_up
        grad_normed += nt(grad_up, w_up_ref[:, low : low + step])
    unit, rate = center(middle_ref[...])
    grad, gain_grad = center_back(grad_normed, gain_ffn_ref[...], unit, rate)
    grad_middle = grad_final + grad
    grad_middle_ref[...] = grad_middle
    grad_branch_ref[...] = grad_middle.astype(BF16)

    @pl.when(pl.program_id(0) == 0)
    def _():
        gain_grad_ref[...] = jnp.zeros_like(gain_grad_ref)

    gain_grad_ref[...] += gain_grad


def ffn_back(line, pooled_grad, lengths, slopes, middle, gain_ffn, w_up, w_down):
    total, width = middle.shape
    entries = pooled_grad.shape[0]
    slots = total // entries
    rows = math.gcd(total, 256)
    some = rows // slots
    ff = w_up.shape[1]
    return line.run(
        functools.partial(ffn_back_body, slots),
        "ffn_back",
        15,
        (total // rows,),
        [
            (pooled_grad, rows_of(some, width)),
            (lengths, rows_of(rows, 1)),
            *((slope, rows_of(rows, ff // 2)) for slope in slopes),
            (middle, rows_of(rows, width)),
            (gain_ffn, fixed(gain_ffn.shape)),
            (w_up, fixed(w_up.shape)),
            (w_down, fixed(w_down.shape)),
        ],
        [
            ((total, ff), BF16, rows_of(rows, ff)),
            ((total, width), F32, rows_of(rows, width)),
            ((total, width), BF16, rows_of(rows, width)),
            ((1, width), F32, fixed((1, width))),
        ],
    )


def heads_back_body(slots, lengths_ref, w_out_ref, mixed_ref, grad_branch_ref, grad_mixed_ref):
    rows, width = grad_branch_ref.shape
    lengths = lengths_ref[...]
    grad_ctx = nt(grad_branch_ref[...], w_out_ref[...]).astype(BF16)
    row = lax.broadcasted_iota(jnp.int32, (GROUP, GROUP), 0)
    col = lax.broadcasted_iota(jnp.int32, (GROUP, GROUP), 1)
    same = row // slots == col // slots
    lows = range(0, width, PAIR)
    for base in range(0, rows, GROUP):
        span = slice(base, base + GROUP)
        valid = same & (row % slots <= lengths[span])
        queries = [mixed_ref[span, low : low + PAIR] for low in lows]
        keys = [split_heads(mixed_ref[span, width + low : width + low + PAIR]) for low in lows]
        values = [split_heads(mixed_ref[span, 2 * width + low : 2 * width + low + PAIR]) for low in lows]
        grad_pairs = [grad_ctx[span, low : low + PAIR] for low in lows]
        raws = [nt(key, query) for key, query in zip(keys, queries)]
        grad_raws = [nt(value, grad_pair) for value, grad_pair in zip(values, grad_pairs)]
        sides = (slice(0, GROUP), slice(GROUP, 2 * GROUP))
        heads = [raw[side] for raw in raws for side in sides]
        heads = [jnp.where(valid, head * HEAD_DIM ** (-0.5), -1000000000.0) for head in heads]
        heads = [jnp.exp(head - jnp.max(head, axis=0, keepdims=True)) for head in heads]
        probs = [head * (1.0 / jnp.sum(head, axis=0, keepdims=True)) for head in heads]
        grads = [grad_raw[side] for grad_raw in grad_raws for side in sides]
        grads = [
            prob * (grad - jnp.sum(grad * prob, axis=0, keepdims=True)) for prob, grad in zip(probs, grads)
        ]
        probs = [prob.astype(BF16) for prob in probs]
        grads = [(grad * HEAD_DIM ** (-0.5)).astype(BF16) for grad in grads]
        for j, low in enumerate(lows):
            scores_grad = jnp.concatenate(grads[2 * j : 2 * j + 2], axis=0)
            prob = jnp.concatenate(probs[2 * j : 2 * j + 2], axis=0)
            grad_mixed_ref[span, low : low + PAIR] = tn(scores_grad, keys[j]).astype(BF16)
            grad_keys = join_heads(mm(scores_grad, queries[j]))
            grad_mixed_ref[span, width + low : width + low + PAIR] = grad_keys.astype(BF16)
            grad_values = join_heads(mm(prob, grad_pairs[j]))
            grad_mixed_ref[span, 2 * width + low : 2 * width + low + PAIR] = grad_values.astype(BF16)


def heads_back(line, lengths, w_out, mixed, grad_branch, slots):
    total, width = grad_branch.shape
    rows = math.gcd(total, 256)
    return line.run(
        functools.partial(heads_back_body, slots),
        "heads_back",
        13,
        (total // rows,),
        [
            (lengths, rows_of(rows, 1)),
            (w_out, fixed(w_out.shape)),
            (mixed, rows_of(rows, 3 * width)),
            (grad_branch, rows_of(rows, width)),
        ],
        [((total, 3 * width), BF16, rows_of(rows, 3 * width))],
    )[0]


def attn_back_body(
    pieces_ref,
    scripts_ref,
    script_table_ref,
    gain_attn_ref,
    w_qkv_ref,
    grad_mixed_ref,
    grad_middle_ref,
    gain_ffn_grad_ref,
    grad_pieces_ref,
    small_ref,
):
    start, onehot = start_of(pieces_ref, scripts_ref, script_table_ref)
    grad_normed = nt(grad_mixed_ref[...], w_qkv_ref[...])
    unit, rate = center(start)
    grad, gain_grad = center_back(grad_normed, gain_attn_ref[...], unit, rate)
    grad_pieces = grad_middle_ref[...] + grad
    grad_pieces_ref[...] = grad_pieces.reshape(grad_pieces_ref.shape)

    groups = onehot.shape[1]

    @pl.when(pl.program_id(0) == 0)
    def _():
        small_ref[...] = jnp.zeros_like(small_ref)
        small_ref[groups + 1 : groups + 2] = gain_ffn_grad_ref[...]

    small_ref[groups : groups + 1] += gain_grad
    small_ref[:groups] += lax.dot_general(
        onehot, grad_pieces, (((0,), (0,)), ((), ())), precision=highest
    )


def attn_back(
    line, pieces, scripts, script_table, gain_attn, w_qkv, grad_mixed, grad_middle, gain_ffn_grad
):
    entries, slots, width = pieces.shape
    total = entries * slots
    rows = math.gcd(total, 256)
    some = rows // slots
    small = ((script_table.shape[0] + 2 + 15) // 16 * 16, width)
    return line.run(
        attn_back_body,
        "attn_back",
        9,
        (total // rows,),
        [
            (pieces, pl.BlockSpec((some, slots, width), lambda i, *_: (i, 0, 0))),
            (scripts, rows_of(rows, 1)),
            (script_table, fixed(script_table.shape)),
            (gain_attn, fixed(gain_attn.shape)),
            (w_qkv, fixed(w_qkv.shape)),
            (grad_mixed, rows_of(rows, 3 * width)),
            (grad_middle, rows_of(rows, width)),
            (gain_ffn_grad, fixed(gain_ffn_grad.shape)),
        ],
        [
            ((entries, slots, width), F32, pl.BlockSpec((some, slots, width), lambda i, *_: (i, 0, 0)), FAR),
            (small, F32, fixed(small)),
        ],
    )


PLAN = ("f T t f", "04 t f", "46 t f", "68 t f t", "w t E F", "Q")


def per_device(
    pieces,
    lengths,
    scripts,
    script_table,
    gain_attn,
    gain_ffn,
    w_qkv,
    w_out,
    w_up,
    w_down,
    w_proj,
    token_ids,
    out_grad,
):
    entries, slots, width = pieces.shape
    ent_count = lax.axis_size("ent")
    rep_count = lax.axis_size("rep")
    devices = ent_count * rep_count
    features = w_proj.shape[1]
    vocab = entries * devices
    rows_dev, text_len = token_ids.shape
    tokens = rows_dev * text_len
    levels = make_levels(ent_count, rep_count)
    sizes = tuple(size for _, size, _ in levels)
    me = lax.axis_index("ent") * rep_count + lax.axis_index("rep")
    chunks = 1 if devices <= 32 else 8
    each = entries // chunks
    span = vocab // chunks
    slot = slot_of(token_ids // entries ^ me, levels)
    within = token_ids % entries
    slot_ids = within // each * span + slot * each + within % each
    script_rows = jnp.repeat(scripts, slots)[:, None]
    length_rows = jnp.repeat(lengths, slots)[:, None]
    gain_attn, gain_ffn = gain_attn[None], gain_ffn[None]

    cut = len(levels)
    while math.prod(sizes[:cut]) * 16 > w_down.shape[0]:
        cut -= 1
    near, far = levels[:cut], levels[cut:]
    count = math.prod(sizes[:cut])
    slot_index = jnp.arange(count, dtype=jnp.int32) ^ slot_of(me, near)
    line = Line()

    def cut_up(keep, send, some):
        shape = tuple(size for _, size, _ in some[1:]) + keep.shape[-2:]
        return keep.reshape(shape), send.reshape(shape)

    parts, pooled_grads = [], []
    for chunk in range(chunks):
        first = chunk * span
        part_send, send = scatter_rows(
            line, slot_ids, out_grad, w_proj, first + span // 2, span // 2, BF16
        )
        part_keep, keep = scatter_rows(line, slot_ids, out_grad, w_proj, first, span // 2, F32)
        parts.append((part_keep, part_send))
        shape = sizes[1:] + (each, width)
        pooling = sum_halves(line, keep.reshape(shape), send.reshape(shape), levels, pooled_grads)
        if chunks > 1:
            for _ in pooling:
                pass
    next(pooling, None)
    next(pooling, None)
    normed, mixed, context, middle, normed_ffn = attn_forward(
        line, pieces, script_rows, length_rows, script_table, gain_attn, gain_ffn, w_qkv, w_out
    )
    next(pooling, None)
    length_cols = lengths[:, None]
    slope_a, hidden_a, pooled = ffn_forward(
        line, length_rows, length_cols, middle, normed_ffn, w_up, w_down, False
    )
    next(pooling, None)
    slope_b, hidden_b, pooled = ffn_forward(
        line, length_rows, length_cols, pooled, normed_ffn, w_up, w_down, True
    )
    for _ in pooling:
        pass
    grad_pooled = jnp.concatenate(pooled_grads, axis=0) if chunks > 1 else pooled_grads[0]

    held = [((), each, width, BF16, lambda index: [(0, (), ALL, 0, 0)])]
    halves = [[] for _ in range(chunks)]
    spreads = [
        gather_halves(
            line, stage(line, [(pooled[chunk * each :][:each], [])], held)[0], levels, halves[chunk]
        )
        for chunk in range(chunks)
    ]

    def spread_on():
        if chunks == 1:
            next(spreads[0])

    spread_on()
    down = tall_weight(line, slot_index, (hidden_a, hidden_b), grad_pooled.astype(BF16))
    grad_up, grad_middle, grad_branch, part_gain_ffn = ffn_back(
        line, grad_pooled, length_rows, (slope_a, slope_b), middle, gain_ffn, w_up, w_down
    )
    spread_on()
    up = wide_weight(line, slot_index, normed_ffn, grad_up)
    small, ffn_all, two_all = [], [], []
    ffn_sum = all_sum_two(
        line, *cut_up(*down, near), *cut_up(*up, near), lambda: small[0], near, far, ffn_all
    )
    next(ffn_sum)
    spread_on()
    grad_mixed = heads_back(line, length_rows, w_out, mixed, grad_branch, slots)
    next(ffn_sum)
    two = two_weights(line, slot_index, normed, grad_mixed, context, grad_branch)
    two_sum = all_sum(line, *cut_up(*two, near), near, far, two_all)
    next(two_sum)
    spread_on()
    grad_pieces, part_small = attn_back(
        line,
        pieces,
        script_rows,
        script_table,
        gain_attn,
        w_qkv,
        grad_mixed,
        grad_middle,
        part_gain_ffn,
    )
    small.append(part_small)
    results = {}

    def make_table():
        tables, total = [], None
        for chunk in range(chunks):
            for _ in spreads[chunk]:
                pass
            own, other = (value.reshape(span // 2, width) for value in halves[chunk])
            table, part = table_and_grad(line, own, other, w_proj, *parts[chunk])
            tables.append(table)
            total = part if total is None else total + part
        results["tables"] = tables
        results["proj"] = total, swap(total, levels[0])

    def look_up(first, last):
        before = results.get("looked_up")
        results["looked_up"] = lookup(line, slot_ids, results["tables"], (first, last), before)

    def add_proj():
        total, other = results["proj"]
        whole = [((), width, features, F32, lambda index: [(0, (), ALL, 0, 0)])]
        results["w_proj"] = stage(line, [(total, [other])], whole)[0]

    def end_ffn():
        results["w_down"] = unpack(line, slot_index, *map(merge, ffn_all[:2]), w_down.shape[0])
        results["w_up"], *results["small"] = unpack_extra(
            line,
            slot_index,
            *map(merge, ffn_all[2:]),
            *w_up.shape,
            (script_table.shape[0], 1, 1),
            math.prod(sizes[3:cut]),
        )

    def end_two():
        for _ in two_sum:
            pass
        results["w_qkv"], results["w_out"] = unpack_two(
            line, slot_index, *map(merge, two_all), *w_qkv.shape
        )

    acts = {
        "f": lambda: next(ffn_sum, 0),
        "t": lambda: next(two_sum, 0),
        "T": make_table,
        "w": add_proj,
        "E": lambda: list(ffn_sum),
        "F": end_ffn,
        "Q": end_two,
    }
    for act in (act for part in PLAN for act in part.split()):
        if act.isdigit():
            look_up(int(act[0]), int(act[1]))
        else:
            acts[act]()
    looked_up, grad_w_proj = results["looked_up"], results["w_proj"]
    grad_w_down, grad_w_up = results["w_down"], results["w_up"]
    grad_w_qkv, grad_w_out = results["w_qkv"], results["w_out"]
    grad_script, grad_gain_attn, grad_gain_ffn = results["small"]
    return (
        looked_up,
        grad_pieces,
        grad_script,
        grad_gain_attn.reshape(width),
        grad_gain_ffn.reshape(width),
        grad_w_qkv,
        grad_w_out,
        grad_w_up,
        grad_w_down,
        grad_w_proj,
    )


def solution(mesh):
    in_specs = (
        P(("ent", "rep"), None, None),
        P(("ent", "rep")),
        P(("ent", "rep")),
        P(),
        P(),
        P(),
        P(),
        P(),
        P(),
        P(),
        P(None, "ent"),
        P("rep", None),
        P("ent", "rep", None),
    )
    out_specs = (
        P("ent", "rep", None),
        P(("ent", "rep"), None, None),
        P(),
        P(),
        P(),
        P(),
        P(),
        P(),
        P(),
        P(None, "ent"),
    )
    return jax.shard_map(
        per_device, mesh=mesh, in_specs=in_specs, out_specs=out_specs, check_vma=False
    )
```
